32 devices in a mesh: gx: 16 (over z, x, core), sec: 2 (over y).
Axes of the slice: x: 2, y: 2, z: 4, core: 2. Of those that a mesh axis runs over, the one named last changes fastest.
Arguments:
- state_init: float32 [16, 128, 16, 128], P(None, 'gx', 'sec'), may hold values from -6 to 6
- rock_type: int32 [128, 1024], P('gx', 'sec'), may hold values from 0 to 15
- perm_table: float32 [3, 16], replicated, may hold values from 0.2 to 1
- well_cells: int32 [256], replicated, may hold values from 0 to 131071
- well_rate: float32 [16, 256], replicated, may hold values from -12 to 12
- basis_in: bfloat16 [128, 16, 128, 256], P(('gx', 'sec')), may hold values from -4 to 4
- singular: float32 [256], replicated, may hold values from 0.5 to 2
Outputs:
- state_out: float32 [16, 128, 16, 128], P(None, 'gx', 'sec')
- basis_out: bfloat16 [128, 16, 128, 256], P(('gx', 'sec'))
- singular_out: float32 [256], replicated
The draws below stay inside these ranges and needn't reach their ends.
All inputs are finite; a program needn't handle non-finite values.
Results may differ from the reference program's by a relative error of at most 0.0059.
Values may be sent and summed in bfloat16 or wider, within the bound.
No kernel may reach another device: no remote copies, remote signals or barrier semaphores. Data moves between devices by JAX's collectives and lax.ppermute only.
A program may use at most 128 MiB of HBM per device.

```python
import math
import jax
import jax.numpy as jnp
from jax import lax

NZ = 64
K = 256
MG = 8
STEPS = 4
GROUPS = 2
ROCKS = 16
WELLS = 256
NX = 128
NY = 16
FZ = 128
SNAPS = 32
MEMB = 16
ROWS = 262144
CELLS = 131072


def basis_table(key):
    values = jax.random.normal(jax.random.fold_in(key, 11), (NX, NY, 2 * NZ, K), jnp.float32)
    partner = jax.random.permutation(jax.random.fold_in(key, 14), K)
    scales = jnp.exp(jax.random.uniform(jax.random.fold_in(key, 15), (K,), jnp.float32, math.log(0.6), math.log(1.4)))
    mixed = (values + 0.4 * jnp.take(values, partner, axis=-1)) * scales
    return jnp.clip(mixed, -4.0, 4.0)


def draw_basis_in(key, part):
    return basis_table(key).astype(jnp.bfloat16)


def draw_state_init(key, part):
    table = basis_table(key)
    mixing = jax.random.normal(jax.random.fold_in(key, 12), (MG * GROUPS, K), jnp.float32) * (1.5 / math.sqrt(K))
    aligned = jnp.einsum('xyfk,mk->mxyf', table, mixing)
    noise_key = jax.random.fold_in(key, 13)
    position = jnp.arange(NX, dtype=jnp.float32) / max(NX - 1, 1)
    ramp = 0.5 * jnp.exp(math.log(3.0) * position)
    rough = jax.random.normal(noise_key, (MG * GROUPS, NX, NY, 2 * NZ), jnp.float32)
    rough = rough * ramp[None, :, None, None]
    return jnp.clip(aligned + rough, -6.0, 6.0)


def with_ends(result, stream_key, least, high):
    extent = result.shape
    index_at = [jax.random.randint(jax.random.fold_in(stream_key, axis), (), 0, extent[axis]) for axis in range(len(extent))]
    result = result.at[tuple(index_at)].set(least)
    longest = extent.index(max(extent))
    index_at[longest] = (index_at[longest] + 1) % extent[longest]
    return result.at[tuple(index_at)].set(high)


def bell_draw(key, dims, width, limit, held_as=jnp.bfloat16):
    array = width * jax.random.normal(key, dims, jnp.float32)
    return jnp.clip(array, min=-limit, max=limit).astype(held_as)


def setup_inputs(seed: int = 0) -> dict:
    splits = jax.random.split(jax.random.key(seed), 8)
    state_init = draw_state_init(jax.random.fold_in(splits[7], 71), 0)
    rock_type = with_ends(jax.random.randint(splits[1], (NX, NY * NZ), 0, ROCKS), jax.random.fold_in(splits[1], 1), 0, ROCKS - 1).astype(jnp.int32)
    perm_table = jnp.clip(jnp.exp(jax.random.uniform(splits[2], (3, ROCKS), jnp.float32, math.log(0.2), math.log(1.0))), 0.2, 1.0)
    well_cells = with_ends(jax.random.randint(splits[3], (WELLS,), 0, NX * NY * NZ), jax.random.fold_in(splits[3], 1), 0, (NX * NY * NZ) - 1).astype(jnp.int32)
    well_rate = bell_draw(splits[4], (MEMB, WELLS), 3.0, 12.0, jnp.float32)
    basis_in = draw_basis_in(jax.random.fold_in(splits[7], 71), 0)
    singular = jnp.clip(jnp.exp(jax.random.uniform(splits[6], (K,), jnp.float32, math.log(0.5), math.log(2.0))), 0.5, 2.0)
    return {"state_init": state_init, "rock_type": rock_type, "perm_table": perm_table, "well_cells": well_cells, "well_rate": well_rate, "basis_in": basis_in, "singular": singular}


DT_PRESSURE = 0.12
DT_SATURATION = 0.06
DT_ADVECT = 0.15

def harmonic(left, right):
    return 2.0 * left * right / (left + right)

def shift_layers(fields):
    blank = jnp.zeros_like(fields[..., :1])
    return (jnp.concatenate([fields[..., 1:], blank], -1), jnp.concatenate([blank, fields[..., :-1]], -1))

def advance(fields, besides, weights, inflow, layers):
    column = lax.broadcasted_iota(jnp.int32, (fields.shape[-1],), 0)
    step_sizes = jnp.where(column < layers, DT_PRESSURE, DT_SATURATION)
    is_sat = (column >= layers).astype(fields.dtype)
    press_both = jnp.concatenate([fields[..., :layers], fields[..., :layers]], -1)
    spread = jnp.zeros_like(fields)
    carried = jnp.zeros_like(fields)
    for beside, weight in zip(besides, weights):
        spread = spread + weight * (beside - fields)
        beside_press = jnp.concatenate([beside[..., :layers], beside[..., :layers]], -1)
        pushed = weight * (beside_press - press_both)
        carried = carried + jnp.maximum(pushed, 0.0) * beside + jnp.minimum(pushed, 0.0) * fields
    return fields + step_sizes * spread + DT_ADVECT * is_sat * carried + DT_PRESSURE * inflow

def small_rotation(coeffs, lower, sigma):
    count = sigma.shape[0]
    extra = lower.shape[0]
    top = jnp.concatenate([jnp.diag(sigma), coeffs.T], 1)
    bottom = jnp.concatenate([jnp.zeros((extra, count), sigma.dtype), lower.T], 1)
    core = jnp.concatenate([top, bottom], 0)
    leading = jnp.dot(core, top.T, precision=lax.Precision.HIGHEST)
    inner = jnp.dot(leading.T, leading, precision=lax.Precision.HIGHEST)
    factor = jnp.linalg.cholesky(inner)
    rotation = lax.linalg.triangular_solve(factor, leading.T, left_side=True, lower=True).T
    energy = jnp.dot(core.T, rotation, precision=lax.Precision.HIGHEST)
    return (rotation, jnp.sqrt(lax.optimization_barrier(jnp.sum(energy * energy, axis=0))))

def compress(snaps, basis_now, sigma):
    flat_basis = basis_now.reshape(ROWS, K)
    coeffs = jnp.dot(snaps.astype(jnp.float32), flat_basis.astype(jnp.float32), preferred_element_type=jnp.float32) / ROWS
    rounded = coeffs.astype(jnp.bfloat16)
    resid = snaps.astype(jnp.float32) - lax.dot_general(rounded.astype(jnp.float32), flat_basis.astype(jnp.float32), (((1,), (1,)), ((), ())), preferred_element_type=jnp.float32)
    gram = jnp.dot(resid, resid.T, precision=lax.Precision.HIGHEST) / ROWS
    lower = jnp.linalg.cholesky(gram)
    ortho = lax.linalg.triangular_solve(lower, resid, left_side=True, lower=True).astype(jnp.bfloat16)
    rotation, sigma_next = small_rotation(coeffs, lower, sigma)
    mixing = rotation.astype(jnp.bfloat16)
    basis_blocks = basis_now.reshape(NX, NY * FZ, K)
    ortho_blocks = jnp.moveaxis(ortho.reshape(SNAPS, NX, NY * FZ), 1, 0)

    def rotate_block(pair):
        basis_block, ortho_block = pair
        value = jnp.dot(basis_block.astype(jnp.float32), mixing[:K].astype(jnp.float32), preferred_element_type=jnp.float32)
        value = value + lax.dot_general(ortho_block.astype(jnp.float32), mixing[K:].astype(jnp.float32), (((0,), (0,)), ((), ())), preferred_element_type=jnp.float32)
        return value.astype(jnp.bfloat16)
    fresh = lax.map(rotate_block, (basis_blocks, ortho_blocks))
    return (fresh.reshape(NX, NY, FZ, K), sigma_next)

def reference(state_init, rock_type, perm_table, well_cells, well_rate, basis_in, singular):
    kinds = lax.broadcasted_iota(jnp.int32, (ROCKS, 1, 1), 0)
    picks = (rock_type[None] == kinds).astype(perm_table.dtype)
    perm = jnp.einsum('dr,rxc->dxc', perm_table, picks, precision=lax.Precision.HIGHEST).reshape(3, NX, NY, NZ)
    padded = jnp.pad(perm, ((0, 0), (1, 1), (1, 1), (1, 1)))
    x_up = harmonic(perm[0], padded[0, 2:, 1:-1, 1:-1])
    x_down = harmonic(padded[0, :-2, 1:-1, 1:-1], perm[0])
    y_up = harmonic(perm[1], padded[1, 1:-1, 2:, 1:-1])
    y_down = harmonic(padded[1, 1:-1, :-2, 1:-1], perm[1])
    z_up = harmonic(perm[2], padded[2, 1:-1, 1:-1, 2:])
    z_down = harmonic(padded[2, 1:-1, 1:-1, :-2], perm[2])
    weights = [jnp.concatenate([face, face], -1) for face in (x_up, x_down, y_up, y_down, z_up, z_down)]
    source = jax.ops.segment_sum(well_rate.T, well_cells, num_segments=CELLS).T.reshape(MEMB, NX, NY, NZ)
    source_full = jnp.concatenate([source, jnp.zeros_like(source)], -1)
    basis_now = basis_in
    sigma = singular
    finals = []
    for group in range(GROUPS):
        fields = state_init[group * MG:(group + 1) * MG]
        inflow = source_full[group * MG:(group + 1) * MG]
        saved = []
        for step_index in range(STEPS):
            bordered = jnp.pad(fields, ((0, 0), (1, 1), (1, 1), (0, 0)))
            up_layer, down_layer = shift_layers(fields)
            besides = [bordered[:, 2:, 1:-1], bordered[:, :-2, 1:-1], bordered[:, 1:-1, 2:], bordered[:, 1:-1, :-2], up_layer, down_layer]
            fields = advance(fields, besides, weights, inflow, NZ)
            saved.append(fields.astype(jnp.bfloat16))
        finals.append(fields)
        snaps = jnp.concatenate(saved, 0).reshape(SNAPS, ROWS)
        basis_now, sigma = compress(snaps, basis_now, sigma)
    return (jnp.concatenate(finals, 0), basis_now, sigma)
```

```python
import jax
import jax.numpy as jnp
from jax import lax
from jax.sharding import PartitionSpec as P

MG = 8
STEPS = 4
GROUPS = 2

DT_PRESSURE = 0.12
DT_SATURATION = 0.06
DT_ADVECT = 0.15
HIGHEST = lax.Precision.HIGHEST
AXES = ("gx", "sec")


def face_weight(left, right):
    total = left + right
    return jnp.where(total > 0.0, 2.0 * left * right / jnp.where(total > 0.0, total, 1.0), 0.0)


def fetch_slab(block, width):
    gx_count = lax.axis_size("gx")
    sec_count = lax.axis_size("sec")
    sec = lax.axis_index("sec")
    across = block.shape[1]
    if sec_count == 2 and across == 2 * width:
        first = sec == 0
        low_rows, high_rows = block[:, :width], block[:, width:]
        outward = jnp.where(first, high_rows, low_rows)
        other = lax.ppermute(block, "sec", [(0, 1), (1, 0)])
        straight = []
        for g in range(gx_count - 1):
            straight += [(2 * g, 2 * g + 2), (2 * g + 3, 2 * g + 1)]
        crossed = []
        for r in range(gx_count):
            if r > 0:
                crossed.append((2 * (r - 1) + 1, 2 * r))
            if r < gx_count - 1:
                crossed.append((2 * (r + 1), 2 * r + 1))
        beside = lax.ppermute(outward, AXES, straight)
        inward = jnp.where(first, low_rows, high_rows)
        cross = lax.ppermute(inward, AXES, crossed)
        left_own = jnp.concatenate([beside, block], 1)
        left_other = jnp.concatenate([cross, other], 1)
        right_own = jnp.concatenate([block, beside], 1)
        right_other = jnp.concatenate([other, cross], 1)
        case0 = jnp.concatenate([left_own, left_other], 2)
        case1 = jnp.concatenate([right_other, right_own], 2)
        return jnp.where(first, case0, case1)
    forward = [(i, i + 1) for i in range(gx_count - 1)]
    backward = [(i + 1, i) for i in range(gx_count - 1)]
    whole = lax.all_gather(block, "sec", axis=2, tiled=True)
    low = lax.ppermute(whole[:, across - width :], "gx", forward)
    high = lax.ppermute(whole[:, :width], "gx", backward)
    padded = jnp.concatenate([low, whole, high], 1)
    rows = across // sec_count
    return lax.dynamic_slice_in_dim(padded, sec * rows, rows + 2 * width, axis=1)


def all_sum(value):
    for axis in AXES:
        count = lax.axis_size(axis)
        if count & (count - 1):
            value = lax.psum(value, axis)
            continue
        stride = 1
        while stride < count:
            value = value + lax.ppermute(value, axis, [(i, i ^ stride) for i in range(count)])
            stride *= 2
    return value


def to_bf16(value):
    return value.astype(jnp.bfloat16)


def hdot(a, b, dims=None):
    if dims is None:
        return jnp.dot(a, b, precision=HIGHEST, preferred_element_type=jnp.float32)
    return lax.dot_general(a, b, (dims, ((), ())), precision=HIGHEST, preferred_element_type=jnp.float32)


def update(coeffs, gram, sigma):
    lead = jnp.diag(sigma * sigma) + hdot(coeffs, coeffs, ((0,), (0,)))
    gc = hdot(gram, coeffs)
    inner = hdot(lead, lead) + hdot(coeffs, gc, ((0,), (0,)))
    factor = jnp.linalg.cholesky(inner)
    right = jnp.concatenate([lead, coeffs.T], 1)
    solved = lax.linalg.triangular_solve(factor, right, left_side=True, lower=True)
    count = sigma.shape[0]
    rot_t, extra_t = solved[:, :count], solved[:, count:]
    energy = jnp.concatenate(
        [rot_t * sigma[None, :], hdot(rot_t, coeffs, ((1,), (1,))) + hdot(extra_t, gram)], 1
    )
    sigma_next = jnp.sqrt(jnp.sum(energy * energy, axis=1))
    return to_bf16(rot_t.T).astype(jnp.float32), extra_t.T, sigma_next


def body(state_init, rock_type, perm_table, well_cells, well_rate, basis_in, singular):
    members, across, along, lanes = state_init.shape
    layers = lanes // 2
    sec_count = lax.axis_size("sec")
    sec = lax.axis_index("sec")
    rows = across // sec_count
    total_y = along * sec_count
    rock = rock_type.reshape(1, across, along, layers)
    sent = jnp.concatenate([to_bf16(state_init), to_bf16(jnp.concatenate([rock, rock], -1))], 0)
    slab = fetch_slab(sent, STEPS)
    fields = slab[:members].astype(jnp.float32)
    rocks = slab[members, :, :, :layers].astype(jnp.float32)
    wide = rows + 2 * STEPS
    x_first = lax.axis_index("gx") * across + sec * rows - STEPS
    x_pos = x_first + lax.broadcasted_iota(jnp.int32, (wide, total_y, layers), 0)
    inside = (x_pos >= 0) & (x_pos < across * lax.axis_size("gx"))
    perm = []
    for d in range(3):
        value = jnp.zeros_like(rocks)
        for r in range(perm_table.shape[1]):
            value = jnp.where(rocks == r, perm_table[d, r], value)
        perm.append(jnp.where(inside, value, 0.0))
    padded = [jnp.pad(p, ((1, 1), (1, 1), (1, 1))) for p in perm]
    x_up = face_weight(perm[0], padded[0][2:, 1:-1, 1:-1])
    x_down = face_weight(perm[0], padded[0][:-2, 1:-1, 1:-1])
    y_up = face_weight(perm[1], padded[1][1:-1, 2:, 1:-1])
    y_down = face_weight(perm[1], padded[1][1:-1, :-2, 1:-1])
    z_up = face_weight(perm[2], padded[2][1:-1, 1:-1, 2:])
    z_down = face_weight(perm[2], padded[2][1:-1, 1:-1, :-2])
    weights = [jnp.concatenate([w, w], -1) for w in (x_up, x_down, y_up, y_down, z_up, z_down)]
    y_pos = lax.broadcasted_iota(jnp.int32, x_pos.shape, 1)
    z_pos = lax.broadcasted_iota(jnp.int32, x_pos.shape, 2)
    cell_ids = (x_pos * total_y + y_pos) * layers + z_pos
    hits = (well_cells[:, None] == cell_ids.reshape(1, -1)).astype(jnp.float32)
    source = hdot(well_rate, hits).reshape(members, wide, total_y, layers)
    inflow = jnp.concatenate([source, jnp.zeros_like(source)], -1)

    column = lax.broadcasted_iota(jnp.int32, (lanes,), 0)
    step_sizes = jnp.where(column < layers, DT_PRESSURE, DT_SATURATION)
    is_sat = (column >= layers).astype(jnp.float32)
    saved = []
    for step in range(STEPS):
        bordered = jnp.pad(fields, ((0, 0), (1, 1), (1, 1), (0, 0)))
        blank = jnp.zeros_like(fields[..., :1])
        besides = [
            bordered[:, 2:, 1:-1],
            bordered[:, :-2, 1:-1],
            bordered[:, 1:-1, 2:],
            bordered[:, 1:-1, :-2],
            jnp.concatenate([fields[..., 1:], blank], -1),
            jnp.concatenate([blank, fields[..., :-1]], -1),
        ]
        press = jnp.concatenate([fields[..., :layers]] * 2, -1)
        spread = jnp.zeros_like(fields)
        carried = jnp.zeros_like(fields)
        for beside, weight in zip(besides, weights):
            spread = spread + weight * (beside - fields)
            pushed = weight * (jnp.concatenate([beside[..., :layers]] * 2, -1) - press)
            carried = carried + jnp.maximum(pushed, 0.0) * beside + jnp.minimum(pushed, 0.0) * fields
        fields = fields + step_sizes * spread + DT_ADVECT * is_sat * carried + DT_PRESSURE * inflow
        saved.append(to_bf16(fields[:, STEPS : STEPS + rows]))
    final = fields[:, STEPS : STEPS + rows]
    state_out = lax.all_to_all(final, "sec", split_axis=2, concat_axis=1, tiled=True)

    stacked = jnp.stack(saved, 0).reshape(STEPS, GROUPS, MG, -1)
    stacked = jnp.moveaxis(stacked, 1, 0).reshape(GROUPS * STEPS * MG, -1)
    snaps = STEPS * MG
    count = basis_in.shape[-1]
    flat = basis_in.reshape(-1, count)
    rows_total = flat.shape[0] * lax.axis_size("gx") * sec_count
    both = jnp.concatenate([flat, stacked.T], 1)
    grams = lax.dot_general(both, both, (((0,), (0,)), ((), ())), preferred_element_type=jnp.float32)
    grams = all_sum(grams) / rows_total

    g_uu = grams[:count, :count]
    g_s = grams[count:]
    coeffs = g_s[:snaps, :count]
    r0 = to_bf16(coeffs).astype(jnp.float32)
    cross = hdot(r0, coeffs, ((1,), (1,)))
    gram = g_s[:snaps, count : count + snaps] - cross - cross.T + hdot(r0, hdot(r0, g_uu), ((1,), (1,)))
    rot, extra, sigma = update(coeffs, gram, singular)
    p0 = rot - hdot(r0, extra, ((0,), (0,)))
    w01 = jnp.concatenate([p0, extra], 0)
    coeffs = hdot(g_s[snaps:, : count + snaps], w01)
    r1 = to_bf16(coeffs).astype(jnp.float32)
    cross = hdot(r1, coeffs, ((1,), (1,)))
    v = hdot(w01, r1, ((1,), (1,)))
    gram = (
        g_s[snaps:, count + snaps :]
        - cross
        - cross.T
        + hdot(v, hdot(grams[: count + snaps, : count + snaps], v), ((0,), (0,)))
    )
    rot, extra, sigma = update(coeffs, gram, sigma)
    p1 = rot - hdot(r1, extra, ((0,), (0,)))
    final_w = jnp.concatenate([hdot(w01, p1), extra], 0)
    high = to_bf16(final_w)
    low = to_bf16(final_w - high.astype(jnp.float32))
    fresh = jnp.dot(both, high, preferred_element_type=jnp.float32) + jnp.dot(
        both, low, preferred_element_type=jnp.float32
    )
    return state_out, to_bf16(fresh).reshape(basis_in.shape), sigma


def solution(mesh):
    return jax.shard_map(
        body,
        mesh=mesh,
        in_specs=(
            P(None, "gx", "sec", None),
            P("gx", "sec"),
            P(),
            P(),
            P(),
            P(("gx", "sec"), None, None, None),
            P(),
        ),
        out_specs=(P(None, "gx", "sec", None), P(("gx", "sec"), None, None, None), P()),
        check_vma=False,
    )
```

```python
import jax
import jax.numpy as jnp
from jax import lax
from jax.experimental import pallas as pl
from jax.experimental.pallas import tpu as pltpu
from jax.sharding import PartitionSpec as P

MG = 8
STEPS = 4
GROUPS = 2

DT_PRESSURE = 0.12
DT_SATURATION = 0.06
DT_ADVECT = 0.15
HIGHEST = lax.Precision.HIGHEST
AXES = ("gx", "sec")


def face_weight(left, right):
    total = left + right
    return jnp.where(total > 0.0, 2.0 * left * right / jnp.where(total > 0.0, total, 1.0), 0.0)


def fetch_slab(block, width):
    gx_count = lax.axis_size("gx")
    sec_count = lax.axis_size("sec")
    sec = lax.axis_index("sec")
    across = block.shape[1]
    if sec_count == 2 and across == 2 * width:
        first = sec == 0
        low_rows, high_rows = block[:, :width], block[:, width:]
        outward = jnp.where(first, high_rows, low_rows)
        other = lax.ppermute(block, "sec", [(0, 1), (1, 0)])
        straight = []
        for g in range(gx_count - 1):
            straight += [(2 * g, 2 * g + 2), (2 * g + 3, 2 * g + 1)]
        crossed = []
        for r in range(gx_count):
            if r > 0:
                crossed.append((2 * (r - 1) + 1, 2 * r))
            if r < gx_count - 1:
                crossed.append((2 * (r + 1), 2 * r + 1))
        beside = lax.ppermute(outward, AXES, straight)
        inward = jnp.where(first, low_rows, high_rows)
        cross = lax.ppermute(inward, AXES, crossed)
        left_own = jnp.concatenate([beside, block], 1)
        left_other = jnp.concatenate([cross, other], 1)
        right_own = jnp.concatenate([block, beside], 1)
        right_other = jnp.concatenate([other, cross], 1)
        case0 = jnp.concatenate([left_own, left_other], 2)
        case1 = jnp.concatenate([right_other, right_own], 2)
        return jnp.where(first, case0, case1)
    forward = [(i, i + 1) for i in range(gx_count - 1)]
    backward = [(i + 1, i) for i in range(gx_count - 1)]
    whole = lax.all_gather(block, "sec", axis=2, tiled=True)
    low = lax.ppermute(whole[:, across - width :], "gx", forward)
    high = lax.ppermute(whole[:, :width], "gx", backward)
    padded = jnp.concatenate([low, whole, high], 1)
    rows = across // sec_count
    return lax.dynamic_slice_in_dim(padded, sec * rows, rows + 2 * width, axis=1)


def all_sum(value):
    for axis in AXES:
        count = lax.axis_size(axis)
        if count & (count - 1):
            value = lax.psum(value, axis)
            continue
        stride = 1
        while stride < count:
            value = value + lax.ppermute(value, axis, [(i, i ^ stride) for i in range(count)])
            stride *= 2
    return value


def to_bf16(value):
    return value.astype(jnp.bfloat16)


def hdot(a, b, left=1, right=0):
    return lax.dot_general(a, b, (((left,), (right,)), ((), ())), precision=HIGHEST, preferred_element_type=jnp.float32)

SUB = 8
PANEL = 32
LANE = 128

def eliminate(panel, column):
    groups = PANEL // SUB
    tiles = panel.shape[1] // LANE
    below = lax.broadcasted_iota(jnp.int32, (SUB, LANE), 0)
    strip = [[panel[h * SUB:(h + 1) * SUB, t * LANE:(t + 1) * LANE] for t in range(tiles)] for h in range(groups)]
    for g in range(groups):
        spread = {}
        for h in range(g, groups):
            for j in range(SUB):
                at = column + g * SUB + j
                tile, lane = at // LANE, at % LANE
                spread[h, j] = jnp.broadcast_to(strip[h][tile][:, lane:lane + 1], (SUB, LANE))
        scale = jnp.zeros((SUB, LANE), jnp.float32)
        for j in range(SUB):
            pivot = jnp.broadcast_to(spread[g, j][j:j + 1], (SUB, LANE))
            inverse = 1.0 / pivot
            scale = jnp.where(below == j, pivot, scale)
            factors = {}
            for h in range(g, groups):
                factors[h] = spread[h, j] * inverse
            factors[g] = jnp.where(below > j, factors[g], 0.0)
            for k in range(j + 1, SUB):
                row = jnp.broadcast_to(spread[g, k][j:j + 1], (SUB, LANE))
                for h in range(g, groups):
                    spread[h, k] = spread[h, k] - factors[h] * row
            for t in range(tiles):
                row = jnp.broadcast_to(strip[g][t][j:j + 1], (SUB, LANE))
                for h in range(g, groups):
                    strip[h][t] = strip[h][t] - factors[h] * row
        root = lax.rsqrt(scale)
        for t in range(tiles):
            strip[g][t] = strip[g][t] * root
    return jnp.concatenate([jnp.concatenate(s, 1) for s in strip], 0)

def solve(aug, count):
    width = aug.shape[1]
    for start in range(0, count, PANEL):
        first = start // LANE * LANE
        done = eliminate(aug[start:start + PANEL, first:], start - first)
        aug[start:start + PANEL, first:] = done
        rest = start + PANEL
        if rest < count:
            base = rest // LANE * LANE
            left = done[:, base - first:count - first]
            change = hdot(left, done[:, base - first:], 0, 0)
            aug[rest:, base:] = aug[rest:, base:] - change[rest - base:]

def small_kernel(gram_ref, sigma_ref, weight_ref, sigma_out, aug):
    count = sigma_ref.shape[1]
    snaps = (gram_ref.shape[0] - count) // 2
    eye = lax.broadcasted_iota(jnp.int32, (count, count), 0) == lax.broadcasted_iota(jnp.int32, (count, count), 1)
    pad = LANE - snaps
    sig2 = sigma_ref[...] * sigma_ref[...]
    prior = None
    for group in range(2):
        rows = gram_ref[count + group * snaps: count + (group + 1) * snaps]
        if group == 0:
            coeffs = rows[:, :count]
            own = rows[:, count:count + snaps]
        else:
            reach = count + snaps
            coeffs = hdot(rows[:, :reach], prior[:, :reach], 1, 1)
            own = rows[:, reach:reach + snaps]
        rounded = coeffs.astype(jnp.bfloat16).astype(jnp.float32)
        if group == 0:
            mapped = rounded
            known = gram_ref[:count, :count]
        else:
            mapped = hdot(rounded, prior[:, :reach])
            known = gram_ref[:reach, :reach]
        spread = hdot(mapped, known)
        gram = own - hdot(rounded, coeffs, 1, 1) - hdot(coeffs, rounded, 1, 1) + hdot(spread, mapped, 1, 1)
        lead = hdot(coeffs, coeffs, 0, 0) + jnp.where(eye, jnp.broadcast_to(sig2, eye.shape), 0.0)
        inner = hdot(lead, lead) + hdot(coeffs, hdot(gram, coeffs), 0, 0)
        aug[:, :count] = inner
        aug[:, count:2 * count] = lead
        aug[:, 2 * count:] = jnp.concatenate([coeffs, jnp.zeros((pad, count), jnp.float32)], 0).T
        solve(aug, count)
        turned = aug[:, count:2 * count]
        extra = aug[:, 2 * count:2 * count + snaps]
        energy = turned * turned * sig2
        ones = jnp.ones((8, count), jnp.float32)
        low = hdot(turned, coeffs, 1, 1) + hdot(extra, gram)
        sig2 = hdot(ones, energy, 1, 1)[:1] + hdot(ones[:, :snaps], low * low, 1, 1)[:1]
        step = turned.astype(jnp.bfloat16).astype(jnp.float32) - hdot(extra, rounded)
        if group == 0:
            prior = jnp.concatenate([step, aug[:, 2 * count:]], 1)
        else:
            weight_ref[:, :count + LANE] = hdot(step, prior)
            weight_ref[:, count + LANE:] = aug[:, 2 * count:]
    sigma_out[...] = jnp.sqrt(sig2)

def small(grams, sigma):
    count = sigma.shape[0]
    w, s = pl.pallas_call(
        small_kernel,
        out_shape=(jax.ShapeDtypeStruct((count, count + 2 * LANE), jnp.float32), jax.ShapeDtypeStruct((1, count), jnp.float32)),
        scratch_shapes=[pltpu.VMEM((count, 2 * count + LANE), jnp.float32)],
        compiler_params=pltpu.CompilerParams(vmem_limit_bytes=48 * 2**20),
    )(grams, sigma.reshape(1, count))
    return w, s.reshape(count)


def body(state_init, rock_type, perm_table, well_cells, well_rate, basis_in, singular):
    members, across, along, lanes = state_init.shape
    layers = lanes // 2
    sec_count = lax.axis_size("sec")
    sec = lax.axis_index("sec")
    rows = across // sec_count
    total_y = along * sec_count
    rock = rock_type.reshape(1, across, along, layers)
    sent = jnp.concatenate([to_bf16(state_init), to_bf16(jnp.concatenate([rock, rock], -1))], 0)
    slab = fetch_slab(sent, STEPS)
    fields = slab[:members].astype(jnp.float32)
    rocks = slab[members, :, :, :layers].astype(jnp.float32)
    wide = rows + 2 * STEPS
    x_first = lax.axis_index("gx") * across + sec * rows - STEPS
    x_pos = x_first + lax.broadcasted_iota(jnp.int32, (wide, total_y, layers), 0)
    inside = (x_pos >= 0) & (x_pos < across * lax.axis_size("gx"))
    perm = []
    for d in range(3):
        value = jnp.zeros_like(rocks)
        for r in range(perm_table.shape[1]):
            value = jnp.where(rocks == r, perm_table[d, r], value)
        perm.append(jnp.where(inside, value, 0.0))
    padded = [jnp.pad(p, ((1, 1), (1, 1), (1, 1))) for p in perm]
    x_up = face_weight(perm[0], padded[0][2:, 1:-1, 1:-1])
    x_down = face_weight(perm[0], padded[0][:-2, 1:-1, 1:-1])
    y_up = face_weight(perm[1], padded[1][1:-1, 2:, 1:-1])
    y_down = face_weight(perm[1], padded[1][1:-1, :-2, 1:-1])
    z_up = face_weight(perm[2], padded[2][1:-1, 1:-1, 2:])
    z_down = face_weight(perm[2], padded[2][1:-1, 1:-1, :-2])
    weights = [jnp.concatenate([w, w], -1) for w in (x_up, x_down, y_up, y_down, z_up, z_down)]
    y_pos = lax.broadcasted_iota(jnp.int32, x_pos.shape, 1)
    z_pos = lax.broadcasted_iota(jnp.int32, x_pos.shape, 2)
    cell_ids = (x_pos * total_y + y_pos) * layers + z_pos
    hits = (well_cells[:, None] == cell_ids.reshape(1, -1)).astype(jnp.float32)
    source = jnp.dot(well_rate, hits, precision=HIGHEST).reshape(members, wide, total_y, layers)
    inflow = jnp.concatenate([source, jnp.zeros_like(source)], -1)

    column = lax.broadcasted_iota(jnp.int32, (lanes,), 0)
    step_sizes = jnp.where(column < layers, DT_PRESSURE, DT_SATURATION)
    is_sat = (column >= layers).astype(jnp.float32)
    saved = []
    for step in range(STEPS):
        bordered = jnp.pad(fields, ((0, 0), (1, 1), (1, 1), (0, 0)))
        blank = jnp.zeros_like(fields[..., :1])
        besides = [
            bordered[:, 2:, 1:-1],
            bordered[:, :-2, 1:-1],
            bordered[:, 1:-1, 2:],
            bordered[:, 1:-1, :-2],
            jnp.concatenate([fields[..., 1:], blank], -1),
            jnp.concatenate([blank, fields[..., :-1]], -1),
        ]
        press = jnp.concatenate([fields[..., :layers]] * 2, -1)
        spread = jnp.zeros_like(fields)
        carried = jnp.zeros_like(fields)
        for beside, weight in zip(besides, weights):
            spread = spread + weight * (beside - fields)
            pushed = weight * (jnp.concatenate([beside[..., :layers]] * 2, -1) - press)
            carried = carried + jnp.maximum(pushed, 0.0) * beside + jnp.minimum(pushed, 0.0) * fields
        fields = fields + step_sizes * spread + DT_ADVECT * is_sat * carried + DT_PRESSURE * inflow
        saved.append(to_bf16(fields[:, STEPS : STEPS + rows]))
    final = fields[:, STEPS : STEPS + rows]
    state_out = lax.all_to_all(final, "sec", split_axis=2, concat_axis=1, tiled=True)

    stacked = jnp.stack(saved, 0).reshape(STEPS, GROUPS, MG, -1)
    stacked = jnp.moveaxis(stacked, 1, 0).reshape(GROUPS * STEPS * MG, -1)
    snaps = STEPS * MG
    count = basis_in.shape[-1]
    flat = basis_in.reshape(-1, count)
    rows_total = flat.shape[0] * lax.axis_size("gx") * sec_count
    both = jnp.concatenate([flat, stacked.T], 1)
    grams = lax.dot_general(both, both, (((0,), (0,)), ((), ())), preferred_element_type=jnp.float32)
    grams = all_sum(grams) / rows_total

    turned, sigma = small(grams, singular)
    final_w = jnp.concatenate(
        [turned[:, :count], turned[:, count : count + snaps], turned[:, count + LANE : count + LANE + snaps]], 1
    ).T
    high = to_bf16(final_w)
    low = to_bf16(final_w - high.astype(jnp.float32))
    fresh = jnp.dot(both, high, preferred_element_type=jnp.float32) + jnp.dot(
        both, low, preferred_element_type=jnp.float32
    )
    return state_out, to_bf16(fresh).reshape(basis_in.shape), sigma


def solution(mesh):
    return jax.shard_map(
        body,
        mesh=mesh,
        in_specs=(
            P(None, "gx", "sec", None),
            P("gx", "sec"),
            P(),
            P(),
            P(),
            P(("gx", "sec"), None, None, None),
            P(),
        ),
        out_specs=(P(None, "gx", "sec", None), P(("gx", "sec"), None, None, None), P()),
        check_vma=False,
    )
```

```python
import jax
import jax.numpy as jnp
from jax import lax
from jax.experimental import pallas as pl
from jax.experimental.pallas import tpu as pltpu
from jax.sharding import PartitionSpec as P

MG = 8
STEPS = 4
GROUPS = 2

DT_PRESSURE = 0.12
DT_SATURATION = 0.06
DT_ADVECT = 0.15
HIGHEST = lax.Precision.HIGHEST
AXES = ("gx", "sec")
VMEM_LIMIT = 48 * 2**20


def place(wide_rows):
    sec_count = lax.axis_size("sec")
    rows = wide_rows - 2 * STEPS
    first = (lax.axis_index("gx") * sec_count + lax.axis_index("sec")) * rows - STEPS
    return first, rows * sec_count * lax.axis_size("gx")


def pack_kernel(state_ref, rock_ref, packed, outward, inward, rock_rows):
    across, entries, members, lanes = packed.shape
    along = entries - 1
    layers = lanes // 2
    rock_rows[...] = jnp.zeros_like(rock_rows)
    for y in range(along):
        chunk = rock_ref[:, y * layers : (y + 1) * layers].astype(jnp.float32)
        rock_rows[pl.ds(y, across, stride=members), :] = jnp.concatenate([chunk, chunk], 1)
    for x in range(across):
        for y in range(along):
            column = state_ref[pl.ds(x * along + y, members, stride=across * along), :]
            packed[x, y] = column.astype(jnp.bfloat16)
        packed[x, along] = rock_rows[x * members : (x + 1) * members].astype(jnp.bfloat16)
    if outward is not None:
        half = across // 2
        sec = lax.axis_index("sec")
        outward[...] = packed[pl.ds((1 - sec) * half, half)]
        inward[...] = packed[pl.ds(sec * half, half)]


def pack(state_init, rock_type, halves):
    members, across, along, lanes = state_init.shape
    shape = (along + 1, members, lanes)
    outs = [jax.ShapeDtypeStruct((across,) + shape, jnp.bfloat16)]
    if halves:
        outs += [jax.ShapeDtypeStruct((across // 2,) + shape, jnp.bfloat16)] * 2

    def kernel(state_ref, rock_ref, *refs):
        packed, outward, inward = refs[:3] if halves else (refs[0], None, None)
        pack_kernel(state_ref, rock_ref, packed, outward, inward, refs[-1])

    return pl.pallas_call(
        kernel,
        out_shape=outs,
        scratch_shapes=[pltpu.VMEM((across * members, lanes), jnp.float32)],
        compiler_params=pltpu.CompilerParams(vmem_limit_bytes=VMEM_LIMIT),
    )(state_init.reshape(-1, lanes), rock_type)


def inflow_kernel(cells_ref, rate_ref, out_ref):
    wide, total_y, group, lanes = out_ref.shape
    layers = lanes // 2
    wells = rate_ref.shape[1]
    first, _ = place(wide)
    out_ref[...] = jnp.zeros_like(out_ref)
    lane = lax.broadcasted_iota(jnp.int32, (group, lanes), 1)
    well = lax.broadcasted_iota(jnp.int32, rate_ref.shape, 1)

    def one(w, carry):
        cell = cells_ref[w]
        column = cell // layers
        z = cell - column * layers
        row = column // total_y
        y = column - row * total_y
        x = row - first

        @pl.when((x >= 0) & (x < wide))
        def _():
            rate = jnp.sum(jnp.where(well == w, rate_ref[...], 0.0), axis=1, keepdims=True) * DT_PRESSURE
            low = jnp.where(lane == z, rate[:group], 0.0)
            high = jnp.where(lane == z + layers, rate[group:], 0.0)
            out_ref[x, y] = out_ref[x, y] + low + high

        return carry

    lax.fori_loop(0, wells, one, 0)


def well_inflow(well_cells, well_rate, wide, total_y, lanes):
    return pl.pallas_call(
        inflow_kernel,
        out_shape=jax.ShapeDtypeStruct((wide, total_y, well_rate.shape[0] // 2, lanes), jnp.float32),
        in_specs=[pl.BlockSpec(memory_space=pltpu.SMEM), pl.BlockSpec(memory_space=pltpu.VMEM)],
        compiler_params=pltpu.CompilerParams(vmem_limit_bytes=VMEM_LIMIT),
    )(well_cells, well_rate)


def roll(value, shift):
    return pltpu.roll(value, shift, 1)


def halves_swap(low, high, left_lanes, layers):
    return (
        jnp.where(left_lanes, low, roll(high, layers)),
        jnp.where(left_lanes, roll(low, layers), high),
    )


def harmonic(left, right):
    total = left + right
    return jnp.where(total > 0.0, 2.0 * left * right / jnp.where(total > 0.0, total, 1.0), 0.0)


def face(w12, w06, p, s, p_next, s_next):
    push = w12 * (p_next - p)
    carried = push * jnp.where(push > 0.0, s_next, s)
    return push, w06 * (s_next - s) + (DT_ADVECT / DT_PRESSURE) * carried


def flux_kernel(fast, *refs):
    if fast:
        state_ref, packed, other, beside, cross = refs[:5]
        refs = refs[5:]
    else:
        slab = refs[0]
        refs = refs[1:]
    table, inflow, basis_hbm, snaps, inner_su, inner_ss, fin, send = refs[:8]
    press_a, sat_a, press_b, sat_b, rock, perm, w12, w06, carry, history, basis, sem = refs[8:]
    wide, total_y = inflow.shape[:2]
    group, lanes = inflow.shape[2:]
    layers = lanes // 2
    blocks, along = rock.shape[1:3]
    rows = wide - 2 * STEPS
    copy = pltpu.make_async_copy(basis_hbm, basis, sem)
    copy.start()
    lane = lax.broadcasted_iota(jnp.int32, (group, lanes), 1)
    left_lanes = lane < layers
    lane_y = lax.broadcasted_iota(jnp.int32, (along, lanes), 1)
    sec = lax.axis_index("sec")

    def put(x, y, low, high):
        p, s = halves_swap(low, high, left_lanes, layers)
        press_a[x, y] = p
        sat_a[x, y] = s

    def put_packed(ref, count, x_at, block):
        def row(x, c):
            for y in range(along):
                value = ref[x, y].astype(jnp.float32)
                put(x_at + x, block * along + y, value[:group], value[group:])
            rock[x_at + x, block] = ref[x, along].astype(jnp.float32)[:along]
            return c

        lax.fori_loop(0, count, row, 0)

    if fast:
        across = packed.shape[0]
        here, there = (1 - sec) * STEPS, sec * across

        def own(x, c):
            for y in range(along):
                at = x * along + y
                stride = across * along
                low = state_ref[pl.ds(at, group, stride=stride), :]
                high = state_ref[pl.ds(at + group * stride, group, stride=stride), :]
                put(here + x, sec * along + y, low, high)
            rock[here + x, sec] = packed[x, along].astype(jnp.float32)[:along]
            return c

        lax.fori_loop(0, across, own, 0)
        put_packed(other, across, here, 1 - sec)
        put_packed(beside, STEPS, there, sec)
        put_packed(cross, STEPS, there, 1 - sec)
    else:
        for block in range(blocks):
            put_packed(slab.at[:, block], wide, 0, block)
    zero = jnp.zeros((group, lanes), jnp.float32)
    for x in range(wide):
        for ref in (press_a, sat_a, press_b, sat_b):
            ref[x, total_y] = zero

    first, total_x = place(wide)

    def look_up(x, c):
        inside = ((first + x >= 0) & (first + x < total_x)).astype(jnp.float32)
        for block in range(blocks):
            kind = rock[x, block]
            for d in range(3):
                value = jnp.zeros((along, lanes), jnp.float32)
                for r in range(table.shape[1]):
                    value = jnp.where(kind == float(r), table[d, r], value)
                perm[d, x, pl.ds(block * along, along), :] = value * inside
        return c

    lax.fori_loop(0, wide, look_up, 0)
    for d in range(3):
        perm[d, wide] = jnp.zeros(perm.shape[2:], jnp.float32)
    perm[1, :, total_y:, :] = jnp.zeros((wide + 1, perm.shape[2] - total_y, lanes), jnp.float32)

    def weigh(x, c):
        for block in range(blocks):
            at = block * along
            here = [perm[d, x, pl.ds(at, along), :] for d in range(3)]
            z_next = jnp.where((lane_y == layers - 1) | (lane_y == lanes - 1), 0.0, roll(here[2], lanes - 1))
            beyond = (perm[0, x + 1, pl.ds(at, along), :], perm[1, x, pl.ds(at + 1, along), :], z_next)
            for d in range(3):
                weight = harmonic(here[d], beyond[d])
                w12[d, x, block] = DT_PRESSURE * weight
                w06[d, x, block] = DT_SATURATION * weight
        return c

    lax.fori_loop(0, wide, weigh, 0)

    def spread(ref, d, x, block, j):
        return jnp.broadcast_to(ref[d, x, block, j : j + 1, :], (group, lanes))

    def x_face(p_ref, s_ref, x, block, j):
        y = block * along + j
        return face(
            spread(w12, 0, x, block, j), spread(w06, 0, x, block, j),
            p_ref[x, y], s_ref[x, y], p_ref[x + 1, y], s_ref[x + 1, y],
        )

    buffers = [(press_a, sat_a), (press_b, sat_b)]
    for step in range(STEPS):
        (p_ref, s_ref), (p_new, s_new) = buffers[step % 2], buffers[(step + 1) % 2]

        def begin(block, c):
            for j in range(along):
                carry[0, block * along + j], carry[1, block * along + j] = x_face(p_ref, s_ref, step, block, j)
            return c

        lax.fori_loop(0, blocks, begin, 0)

        def one_row(x, c):
            def one_block(block, back):
                back_p, back_s = back
                for j in range(along):
                    y = block * along + j
                    p, s = p_ref[x, y], s_ref[x, y]
                    xp, xs = x_face(p_ref, s_ref, x, block, j)
                    yp, ys = face(
                        spread(w12, 1, x, block, j), spread(w06, 1, x, block, j),
                        p, s, p_ref[x, y + 1], s_ref[x, y + 1],
                    )
                    zp, zs = face(
                        spread(w12, 2, x, block, j), spread(w06, 2, x, block, j),
                        p, s, roll(p, lanes - 1), roll(s, lanes - 1),
                    )
                    p_new[x, y] = p + (xp - carry[0, y]) + (yp - back_p) + (zp - roll(zp, 1)) + inflow[x, y]
                    s_new[x, y] = s + (xs - carry[1, y]) + (ys - back_s) + (zs - roll(zs, 1))
                    carry[0, y] = xp
                    carry[1, y] = xs
                    back_p, back_s = yp, ys
                return back_p, back_s

            lax.fori_loop(0, blocks, one_block, (zero, zero))
            return c

        lax.fori_loop(step + 1, wide - 1 - step, one_row, 0)

        def save(at, c):
            x, block = at // blocks, at % blocks
            for j in range(along):
                y = block * along + j
                low, high = halves_swap(p_new[STEPS + x, y], s_new[STEPS + x, y], left_lanes, layers)
                history[x * total_y + y, step * group : (step + 1) * group] = low
                history[x * total_y + y, (STEPS + step) * group : (STEPS + step + 1) * group] = high
                if step == STEPS - 1 and not fast:
                    fin[x, block, j] = jnp.concatenate([low, high], 0)
            return c

        lax.fori_loop(0, rows * blocks, save, 0)

    if fast:
        last = slice((STEPS - 1) * group, STEPS * group)
        past = slice((2 * STEPS - 1) * group, 2 * STEPS * group)
        for ref, block in ((fin, sec), (send, 1 - sec)):
            for x in range(rows):
                for j in range(along):
                    at = x * total_y + block * along + j
                    ref[x, j, :group] = history[at, last]
                    ref[x, j, group:] = history[at, past]

    copy.wait()
    inner_su[...] = jnp.zeros_like(inner_su)
    inner_ss[...] = jnp.zeros_like(inner_ss)
    count = basis.shape[2]

    def add_pair(q, c):
        pair = [history[2 * q].astype(jnp.bfloat16), history[2 * q + 1].astype(jnp.bfloat16)]
        snaps[2 * q] = pair[0]
        snaps[2 * q + 1] = pair[1]
        both = jnp.concatenate(pair, 1)
        inner_su[...] += jnp.dot(both, basis[pl.ds(2 * q, 2)].reshape(2 * lanes, count), preferred_element_type=jnp.float32)
        inner_ss[...] += lax.dot_general(both, both, (((1,), (1,)), ((), ())), preferred_element_type=jnp.float32)
        return c

    lax.fori_loop(0, rows * total_y // 2, add_pair, 0)


def flux(fields, perm_table, inflow, basis_blocks, along):
    fast = len(fields) > 1
    wide, total_y, group, lanes = inflow.shape
    blocks = total_y // along
    rows = wide - 2 * STEPS
    count = basis_blocks.shape[-1]
    snaps = 2 * STEPS * group
    f32 = jnp.float32
    fin = (rows, along, 2 * group, lanes) if fast else (rows, blocks, along, 2 * group, lanes)
    outs = [
        jax.ShapeDtypeStruct((rows * total_y, snaps, lanes), jnp.bfloat16),
        jax.ShapeDtypeStruct((snaps, count), f32),
        jax.ShapeDtypeStruct((snaps, snaps), f32),
        jax.ShapeDtypeStruct(fin, f32),
        jax.ShapeDtypeStruct(fin if fast else (8, lanes), f32),
    ]
    state = pltpu.VMEM((wide, total_y + 1, group, lanes), f32)
    whole = pl.BlockSpec(memory_space=pltpu.VMEM)
    return pl.pallas_call(
        lambda *refs: flux_kernel(fast, *refs),
        out_shape=outs,
        in_specs=[whole] * len(fields)
        + [pl.BlockSpec(memory_space=pltpu.SMEM), whole, pl.BlockSpec(memory_space=pl.ANY)],
        scratch_shapes=[
            state, state, state, state,
            pltpu.VMEM((wide, blocks, along, lanes), f32),
            pltpu.VMEM((3, wide + 1, total_y + 8, lanes), f32),
            pltpu.VMEM((3, wide, blocks, along, lanes), f32),
            pltpu.VMEM((3, wide, blocks, along, lanes), f32),
            pltpu.VMEM((2, total_y, group, lanes), f32),
            pltpu.VMEM((rows * total_y, snaps, lanes), f32),
            pltpu.VMEM(basis_blocks.shape, jnp.bfloat16),
            pltpu.SemaphoreType.DMA,
        ],
        compiler_params=pltpu.CompilerParams(vmem_limit_bytes=VMEM_LIMIT),
    )(*fields, perm_table, inflow, basis_blocks)


def unpack_kernel(parts, *refs):
    out_ref = refs[-1]
    along = refs[0].shape[1]
    members = refs[0].shape[2]
    stride = out_ref.shape[0] // members
    sec = lax.axis_index("sec")
    for part in range(parts):
        rows = refs[part].shape[0]
        start = 0 if parts == 1 else (sec if part == 0 else 1 - sec) * rows
        for x in range(rows):
            for y in range(along):
                out_ref[pl.ds((start + x) * along + y, members, stride=stride), :] = refs[part][x, y]


def unpack(parts):
    rows, along, members, lanes = parts[0].shape
    across = rows * len(parts)
    out = pl.pallas_call(
        lambda *refs: unpack_kernel(len(parts), *refs),
        out_shape=jax.ShapeDtypeStruct((members * across * along, lanes), jnp.float32),
        compiler_params=pltpu.CompilerParams(vmem_limit_bytes=VMEM_LIMIT),
    )(*parts)
    return out.reshape(members, across, along, lanes)


def all_sum(value):
    for axis in AXES:
        count = lax.axis_size(axis)
        if count & (count - 1):
            value = lax.psum(value, axis)
            continue
        stride = 1
        while stride < count:
            value = value + lax.ppermute(value, axis, [(i, i ^ stride) for i in range(count)])
            stride *= 2
    return value


def to_bf16(value):
    return value.astype(jnp.bfloat16)


def hdot(a, b, left=1, right=0):
    return lax.dot_general(a, b, (((left,), (right,)), ((), ())), precision=HIGHEST, preferred_element_type=jnp.float32)

SUB = 8
PANEL = 32
LANE = 128

def eliminate(panel, column):
    groups = PANEL // SUB
    tiles = panel.shape[1] // LANE
    below = lax.broadcasted_iota(jnp.int32, (SUB, LANE), 0)
    strip = [[panel[h * SUB:(h + 1) * SUB, t * LANE:(t + 1) * LANE] for t in range(tiles)] for h in range(groups)]
    for g in range(groups):
        spread = {}
        for h in range(g, groups):
            for j in range(SUB):
                at = column + g * SUB + j
                tile, lane = at // LANE, at % LANE
                spread[h, j] = jnp.broadcast_to(strip[h][tile][:, lane:lane + 1], (SUB, LANE))
        scale = jnp.zeros((SUB, LANE), jnp.float32)
        for j in range(SUB):
            pivot = jnp.broadcast_to(spread[g, j][j:j + 1], (SUB, LANE))
            inverse = 1.0 / pivot
            scale = jnp.where(below == j, pivot, scale)
            factors = {}
            for h in range(g, groups):
                factors[h] = spread[h, j] * inverse
            factors[g] = jnp.where(below > j, factors[g], 0.0)
            for k in range(j + 1, SUB):
                row = jnp.broadcast_to(spread[g, k][j:j + 1], (SUB, LANE))
                for h in range(g, groups):
                    spread[h, k] = spread[h, k] - factors[h] * row
            for t in range(tiles):
                row = jnp.broadcast_to(strip[g][t][j:j + 1], (SUB, LANE))
                for h in range(g, groups):
                    strip[h][t] = strip[h][t] - factors[h] * row
        root = lax.rsqrt(scale)
        for t in range(tiles):
            strip[g][t] = strip[g][t] * root
    return jnp.concatenate([jnp.concatenate(s, 1) for s in strip], 0)

def solve(aug, count):
    width = aug.shape[1]
    for start in range(0, count, PANEL):
        first = start // LANE * LANE
        done = eliminate(aug[start:start + PANEL, first:], start - first)
        aug[start:start + PANEL, first:] = done
        rest = start + PANEL
        if rest < count:
            base = rest // LANE * LANE
            left = done[:, base - first:count - first]
            change = hdot(left, done[:, base - first:], 0, 0)
            aug[rest:, base:] = aug[rest:, base:] - change[rest - base:]

def small_kernel(gram_ref, sigma_ref, weight_ref, sigma_out, aug):
    count = sigma_ref.shape[1]
    snaps = (gram_ref.shape[0] - count) // 2
    eye = lax.broadcasted_iota(jnp.int32, (count, count), 0) == lax.broadcasted_iota(jnp.int32, (count, count), 1)
    pad = LANE - snaps
    sig2 = sigma_ref[...] * sigma_ref[...]
    prior = None
    for group in range(2):
        rows = gram_ref[count + group * snaps: count + (group + 1) * snaps]
        if group == 0:
            coeffs = rows[:, :count]
            own = rows[:, count:count + snaps]
        else:
            reach = count + snaps
            coeffs = hdot(rows[:, :reach], prior[:, :reach], 1, 1)
            own = rows[:, reach:reach + snaps]
        rounded = coeffs.astype(jnp.bfloat16).astype(jnp.float32)
        if group == 0:
            mapped = rounded
            known = gram_ref[:count, :count]
        else:
            mapped = hdot(rounded, prior[:, :reach])
            known = gram_ref[:reach, :reach]
        spread = hdot(mapped, known)
        gram = own - hdot(rounded, coeffs, 1, 1) - hdot(coeffs, rounded, 1, 1) + hdot(spread, mapped, 1, 1)
        lead = hdot(coeffs, coeffs, 0, 0) + jnp.where(eye, jnp.broadcast_to(sig2, eye.shape), 0.0)
        inner = hdot(lead, lead) + hdot(coeffs, hdot(gram, coeffs), 0, 0)
        aug[:, :count] = inner
        aug[:, count:2 * count] = lead
        aug[:, 2 * count:] = jnp.concatenate([coeffs, jnp.zeros((pad, count), jnp.float32)], 0).T
        solve(aug, count)
        turned = aug[:, count:2 * count]
        extra = aug[:, 2 * count:2 * count + snaps]
        energy = turned * turned * sig2
        ones = jnp.ones((8, count), jnp.float32)
        low = hdot(turned, coeffs, 1, 1) + hdot(extra, gram)
        sig2 = hdot(ones, energy, 1, 1)[:1] + hdot(ones[:, :snaps], low * low, 1, 1)[:1]
        step = turned.astype(jnp.bfloat16).astype(jnp.float32) - hdot(extra, rounded)
        if group == 0:
            prior = jnp.concatenate([step, aug[:, 2 * count:]], 1)
        else:
            weight_ref[:, :count + LANE] = hdot(step, prior)
            weight_ref[:, count + LANE:] = aug[:, 2 * count:]
    sigma_out[...] = jnp.sqrt(sig2)

def small(grams, sigma):
    count = sigma.shape[0]
    w, s = pl.pallas_call(
        small_kernel,
        out_shape=(jax.ShapeDtypeStruct((count, count + 2 * LANE), jnp.float32), jax.ShapeDtypeStruct((1, count), jnp.float32)),
        scratch_shapes=[pltpu.VMEM((count, 2 * count + LANE), jnp.float32)],
        compiler_params=pltpu.CompilerParams(vmem_limit_bytes=VMEM_LIMIT),
    )(grams, sigma.reshape(1, count))
    return w, s.reshape(count)


def body(state_init, rock_type, perm_table, well_cells, well_rate, basis_in, singular):
    members, across, along, lanes = state_init.shape
    gx_count = lax.axis_size("gx")
    sec_count = lax.axis_size("sec")
    rows = across // sec_count
    wide = rows + 2 * STEPS
    total_y = along * sec_count
    count = basis_in.shape[-1]
    fast = sec_count == 2 and across == 2 * STEPS
    inflow = well_inflow(well_cells, well_rate, wide, total_y, lanes)
    if fast:
        packed, outward, inward = pack(state_init, rock_type, True)
        straight, crossed = [], []
        for r in range(gx_count):
            if r > 0:
                straight.append((2 * (r - 1), 2 * r))
                crossed.append((2 * (r - 1) + 1, 2 * r))
            if r < gx_count - 1:
                straight.append((2 * (r + 1) + 1, 2 * r + 1))
                crossed.append((2 * (r + 1), 2 * r + 1))
        other = lax.ppermute(packed, "sec", [(0, 1), (1, 0)])
        cross = lax.ppermute(inward, AXES, crossed)
        beside = lax.ppermute(outward, AXES, straight)
        fields = (state_init.reshape(-1, lanes), packed, other, beside, cross)
    else:
        (packed,) = pack(state_init, rock_type, False)
        slab = lax.all_gather(packed, "sec", axis=1)
        low = lax.ppermute(slab[across - STEPS :], "gx", [(i, i + 1) for i in range(gx_count - 1)])
        high = lax.ppermute(slab[:STEPS], "gx", [(i + 1, i) for i in range(gx_count - 1)])
        padded = jnp.concatenate([low, slab, high], 0)
        fields = (lax.dynamic_slice_in_dim(padded, lax.axis_index("sec") * rows, wide, axis=0),)
    flat = basis_in.reshape(-1, count)
    rows_total = flat.shape[0] * gx_count * sec_count
    inner_uu = lax.dot_general(flat, flat, (((0,), (0,)), ((), ())), preferred_element_type=jnp.float32)
    snaps, inner_su, inner_ss, fin, send = flux(fields, perm_table, inflow, flat.reshape(-1, lanes, count), along)
    if fast:
        received = lax.ppermute(send, "sec", [(0, 1), (1, 0)])
        state_out = unpack((fin, received))
    else:
        moved = lax.all_to_all(fin, "sec", split_axis=1, concat_axis=0, tiled=True)
        state_out = unpack((moved.reshape(across, along, members, lanes),))

    snap_count = snaps.shape[1]
    grams = jnp.concatenate(
        [jnp.concatenate([inner_uu, inner_su.T], 1), jnp.concatenate([inner_su, inner_ss], 1)], 0
    )
    grams = all_sum(grams) / rows_total
    turned, sigma = small(grams, singular)
    half = snap_count // 2
    final_w = jnp.concatenate(
        [turned[:, :count], turned[:, count : count + half], turned[:, count + LANE : count + LANE + half]], 1
    ).T
    high = to_bf16(final_w)
    low = to_bf16(final_w - high.astype(jnp.float32))
    columns = jnp.moveaxis(snaps, 1, 2).reshape(-1, snap_count)
    both = jnp.concatenate([flat, columns], 1)
    fresh = jnp.dot(both, high, preferred_element_type=jnp.float32) + jnp.dot(
        both, low, preferred_element_type=jnp.float32
    )
    return state_out, to_bf16(fresh).reshape(basis_in.shape), sigma


def solution(mesh):
    return jax.shard_map(
        body,
        mesh=mesh,
        in_specs=(
            P(None, "gx", "sec", None),
            P("gx", "sec"),
            P(),
            P(),
            P(),
            P(("gx", "sec"), None, None, None),
            P(),
        ),
        out_specs=(P(None, "gx", "sec", None), P(("gx", "sec"), None, None, None), P()),
        check_vma=False,
    )
```

```python
import functools

import jax
import jax.numpy as jnp
from jax import lax
from jax.experimental import pallas as pl
from jax.experimental.pallas import tpu as pltpu
from jax.sharding import PartitionSpec as P

MG = 8
STEPS = 4
GROUPS = 2

DT_PRESSURE = 0.12
DT_SATURATION = 0.06
DT_ADVECT = 0.15
HIGHEST = lax.Precision.HIGHEST
AXES = ("gx", "sec")
VMEM_LIMIT = 48 * 2**20


def place(wide_rows):
    sec_count = lax.axis_size("sec")
    rows = wide_rows - 2 * STEPS
    first = (lax.axis_index("gx") * sec_count + lax.axis_index("sec")) * rows - STEPS
    return first, rows * sec_count * lax.axis_size("gx")


def pack_kernel(state_ref, rock_ref, own, packed, outward, inward, rock_rows):
    across, entries, members, lanes = packed.shape
    along = entries - 1
    layers = lanes // 2
    group = members // 2
    stride = across * along
    left_lanes = lax.broadcasted_iota(jnp.int32, (group, lanes), 1) < layers
    rock_rows[...] = jnp.zeros_like(rock_rows)
    for y in range(along):
        chunk = rock_ref[:, y * layers : (y + 1) * layers].astype(jnp.float32)
        rock_rows[pl.ds(y, across, stride=members), :] = jnp.concatenate([chunk, chunk], 1)
    for x in range(across):
        for y in range(along):
            at = x * along + y
            low = state_ref[pl.ds(at, group, stride=stride), :]
            high = state_ref[pl.ds(at + group * stride, group, stride=stride), :]
            column = jnp.concatenate(halves_swap(low, high, left_lanes, layers), 0)
            own[x, y] = column
            packed[x, y] = column.astype(jnp.bfloat16)
        packed[x, along] = rock_rows[x * members : (x + 1) * members].astype(jnp.bfloat16)
    if outward is not None:
        half = across // 2
        sec = lax.axis_index("sec")
        outward[...] = packed[pl.ds((1 - sec) * half, half)]
        inward[...] = packed[pl.ds(sec * half, half)]


def pack(state_init, rock_type, halves):
    members, across, along, lanes = state_init.shape
    shape = (along + 1, members, lanes)
    outs = [
        jax.ShapeDtypeStruct((across, along, members, lanes), jnp.float32),
        jax.ShapeDtypeStruct((across,) + shape, jnp.bfloat16),
    ]
    if halves:
        outs += [jax.ShapeDtypeStruct((across // 2,) + shape, jnp.bfloat16)] * 2

    def kernel(state_ref, rock_ref, *refs):
        own, packed = refs[:2]
        outward, inward = refs[2:4] if halves else (None, None)
        pack_kernel(state_ref, rock_ref, own, packed, outward, inward, refs[-1])

    return pl.pallas_call(
        kernel,
        out_shape=outs,
        scratch_shapes=[pltpu.VMEM((across * members, lanes), jnp.float32)],
        compiler_params=pltpu.CompilerParams(vmem_limit_bytes=VMEM_LIMIT),
    )(state_init.reshape(-1, lanes), rock_type)


WELL_CHUNK = 8


def inflow_kernel(cells_ref, rate_ref, out_ref):
    wide, total_y, group, lanes = out_ref.shape
    layers = lanes // 2
    wells = cells_ref.shape[0]
    first, _ = place(wide)
    start = first * total_y * layers
    size = wide * total_y * layers
    out_ref[...] = jnp.zeros_like(out_ref)
    lane = lax.broadcasted_iota(jnp.int32, (group, lanes), 1)

    def one(w):
        near = cells_ref[w] - start

        @pl.when((near >= 0) & (near < size))
        def _():
            column = lax.div(near, layers)
            z = near - column * layers
            x = lax.div(column, total_y)
            y = column - x * total_y
            rate = rate_ref[w] * DT_PRESSURE
            out_ref[x, y] = out_ref[x, y] + jnp.where((lane == z) | (lane == z + layers), rate, 0.0)

    def some(c, carry):
        for i in range(WELL_CHUNK):
            one(c * WELL_CHUNK + i)
        return carry

    lax.fori_loop(0, wells // WELL_CHUNK, some, 0)
    for w in range(wells // WELL_CHUNK * WELL_CHUNK, wells):
        one(w)


def well_inflow(well_cells, well_rate, wide, total_y, lanes):
    members, wells = well_rate.shape
    group = members // 2
    layers = lanes // 2
    rate = jnp.moveaxis(well_rate.reshape(2, group, wells), 2, 0)[..., None]
    rate = jnp.broadcast_to(rate, (wells, 2, group, layers))
    rate = jnp.concatenate([rate[:, 0], rate[:, 1]], -1)
    return pl.pallas_call(
        inflow_kernel,
        out_shape=jax.ShapeDtypeStruct((wide, total_y, group, lanes), jnp.float32),
        in_specs=[pl.BlockSpec(memory_space=pltpu.SMEM), pl.BlockSpec(memory_space=pltpu.VMEM)],
        compiler_params=pltpu.CompilerParams(vmem_limit_bytes=VMEM_LIMIT),
        cost_estimate=pl.CostEstimate(flops=2 * 10**9, bytes_accessed=2**20, transcendentals=0),
    )(well_cells, rate)


def roll(value, shift):
    return pltpu.roll(value, shift, 1)


def halves_swap(low, high, left_lanes, layers):
    return (
        jnp.where(left_lanes, low, roll(high, layers)),
        jnp.where(left_lanes, roll(low, layers), high),
    )


def harmonic(left, right):
    total = left + right
    return jnp.where(total > 0.0, 2.0 * left * right / jnp.where(total > 0.0, total, 1.0), 0.0)


def face(w12, w06, p, s, p_next, s_next):
    push = w12 * (p_next - p)
    carried = push * jnp.where(push > 0.0, s_next, s)
    return push, w06 * (s_next - s) + (DT_ADVECT / DT_PRESSURE) * carried


def flux_kernel(fast, *refs):
    if fast:
        own_ref, packed, other, beside, cross = refs[:5]
        refs = refs[5:]
    else:
        slab = refs[0]
        refs = refs[1:]
    table, inflow, inner_uu, basis_hbm, snaps, keep, give, fin, send = refs[:9]
    press_a, sat_a, press_b, sat_b, rock, perm, w12, w06, carry, history, sums, basis, sem = refs[9:]
    wide, total_y = inflow.shape[:2]
    group, lanes = inflow.shape[2:]
    layers = lanes // 2
    blocks, along = rock.shape[1:3]
    rows = wide - 2 * STEPS
    copy = pltpu.make_async_copy(basis_hbm, basis, sem)
    copy.start()
    lane = lax.broadcasted_iota(jnp.int32, (group, lanes), 1)
    left_lanes = lane < layers
    lane_y = lax.broadcasted_iota(jnp.int32, (along, lanes), 1)
    sec = lax.axis_index("sec")

    def put_packed(ref, count, x_at, block):
        def row(x, c):
            for y in range(along):
                value = ref[x, y].astype(jnp.float32)
                press_a[x_at + x, block * along + y] = value[:group]
                sat_a[x_at + x, block * along + y] = value[group:]
            rock[x_at + x, block] = ref[x, along].astype(jnp.float32)[:along]
            return c

        lax.fori_loop(0, count, row, 0)

    if fast:
        across = packed.shape[0]
        here, there = (1 - sec) * STEPS, sec * across

        def own(x, c):
            for y in range(along):
                press_a[here + x, sec * along + y] = own_ref[x, y, :group]
                sat_a[here + x, sec * along + y] = own_ref[x, y, group:]
            rock[here + x, sec] = packed[x, along].astype(jnp.float32)[:along]
            return c

        lax.fori_loop(0, across, own, 0)
        put_packed(other, across, here, 1 - sec)
        put_packed(beside, STEPS, there, sec)
        put_packed(cross, STEPS, there, 1 - sec)
    else:
        for block in range(blocks):
            put_packed(slab.at[:, block], wide, 0, block)
    zero = jnp.zeros((group, lanes), jnp.float32)
    for x in range(wide):
        for ref in (press_a, sat_a, press_b, sat_b):
            ref[x, total_y] = zero

    first, total_x = place(wide)

    def look_up(x, c):
        inside = ((first + x >= 0) & (first + x < total_x)).astype(jnp.float32)
        for block in range(blocks):
            kind = rock[x, block]
            values = [jnp.zeros((along, lanes), jnp.float32)] * 3
            for r in range(table.shape[1]):
                here = kind == float(r)
                values = [jnp.where(here, table[d, r], values[d]) for d in range(3)]
            for d in range(3):
                perm[d, x, pl.ds(block * along, along), :] = values[d] * inside
        return c

    several(wide, look_up, 4)
    for d in range(3):
        perm[d, wide] = jnp.zeros(perm.shape[2:], jnp.float32)
    perm[1, :, total_y:, :] = jnp.zeros((wide + 1, perm.shape[2] - total_y, lanes), jnp.float32)

    def weigh(x, c):
        for block in range(blocks):
            at = block * along
            here = [perm[d, x, pl.ds(at, along), :] for d in range(3)]
            z_next = jnp.where((lane_y == layers - 1) | (lane_y == lanes - 1), 0.0, roll(here[2], lanes - 1))
            beyond = (perm[0, x + 1, pl.ds(at, along), :], perm[1, x, pl.ds(at + 1, along), :], z_next)
            for d in range(3):
                weight = harmonic(here[d], beyond[d])
                w12[d, x, block] = DT_PRESSURE * weight
                w06[d, x, block] = DT_SATURATION * weight
        return c

    several(wide, weigh, 4)

    def spread(ref, d, x, block, j):
        return jnp.broadcast_to(ref[d, x, block, j : j + 1, :], (group, lanes))

    def x_face(p_ref, s_ref, x, block, j):
        y = block * along + j
        return face(
            spread(w12, 0, x, block, j), spread(w06, 0, x, block, j),
            p_ref[x, y], s_ref[x, y], p_ref[x + 1, y], s_ref[x + 1, y],
        )

    buffers = [(press_a, sat_a), (press_b, sat_b)]
    chunk = along * next(n for n in (2, 1) if blocks % n == 0)
    chunks = total_y // chunk

    def columns(c):
        return [(c * chunk + i, c * (chunk // along) + i // along, i % along) for i in range(chunk)]

    for step in range(STEPS):
        (p_ref, s_ref), (p_new, s_new) = buffers[step % 2], buffers[(step + 1) % 2]

        def begin(c, none):
            for y, block, j in columns(c):
                carry[0, y], carry[1, y] = x_face(p_ref, s_ref, step, block, j)
            return none

        lax.fori_loop(0, chunks, begin, 0)
        span = wide - 2 - 2 * step
        deep = 2 if span % 2 == 0 else 1

        def some_rows(r, none):
            x0 = step + 1 + r * deep

            def one_chunk(c, back):
                back = list(back)
                for y, block, j in columns(c):
                    before = carry[0, y], carry[1, y]
                    for i in range(deep):
                        x = x0 + i
                        p, s = p_ref[x, y], s_ref[x, y]
                        xp, xs = x_face(p_ref, s_ref, x, block, j)
                        yp, ys = face(
                            spread(w12, 1, x, block, j), spread(w06, 1, x, block, j),
                            p, s, p_ref[x, y + 1], s_ref[x, y + 1],
                        )
                        zp, zs = face(
                            spread(w12, 2, x, block, j), spread(w06, 2, x, block, j),
                            p, s, roll(p, lanes - 1), roll(s, lanes - 1),
                        )
                        back_p, back_s = back[2 * i : 2 * i + 2]
                        p_new[x, y] = p + (xp - before[0]) + (yp - back_p) + (zp - roll(zp, 1)) + inflow[x, y]
                        s_new[x, y] = s + (xs - before[1]) + (ys - back_s) + (zs - roll(zs, 1))
                        before = xp, xs
                        back[2 * i : 2 * i + 2] = [yp, ys]
                    carry[0, y], carry[1, y] = before
                return tuple(back)

            lax.fori_loop(0, chunks, one_chunk, (zero,) * (2 * deep))
            return none

        lax.fori_loop(0, span // deep, some_rows, 0)

        def save(x, none):
            def save_chunk(c, none):
                for y, block, j in columns(c):
                    low, high = halves_swap(p_new[STEPS + x, y], s_new[STEPS + x, y], left_lanes, layers)
                    history[x * total_y + y, step * group : (step + 1) * group] = low
                    history[x * total_y + y, (STEPS + step) * group : (STEPS + step + 1) * group] = high
                    if step == STEPS - 1 and not fast:
                        fin[x, block, j] = jnp.concatenate([low, high], 0)
                return none

            return lax.fori_loop(0, chunks, save_chunk, none)

        several(rows, save, 2)

    if fast:
        last = slice((STEPS - 1) * group, STEPS * group)
        past = slice((2 * STEPS - 1) * group, 2 * STEPS * group)
        for ref, block in ((fin, sec), (send, 1 - sec)):
            for x in range(rows):
                for j in range(along):
                    at = x * total_y + block * along + j
                    ref[x, j, :group] = history[at, last]
                    ref[x, j, group:] = history[at, past]

    copy.wait()
    count = basis.shape[2]
    cells = rows * total_y
    snap_count = 2 * STEPS * group
    run = next(n for n in (16, 8, 4, 2, 1) if cells % n == 0)
    inner_su = jnp.zeros((snap_count, count), jnp.float32)
    inner_ss = jnp.zeros((snap_count, snap_count), jnp.float32)
    for q in range(0, cells, run):
        part = [history[q + i].astype(jnp.bfloat16) for i in range(run)]
        for i in range(run):
            snaps[q + i] = part[i]
        both = jnp.concatenate(part, 1)
        inner_su += jnp.dot(both, basis[q : q + run].reshape(run * lanes, count), preferred_element_type=jnp.float32)
        inner_ss += lax.dot_general(both, both, (((1,), (1,)), ((), ())), preferred_element_type=jnp.float32)
    fold(sums, inner_uu, inner_su, inner_ss)
    half = sums.shape[0] // 2
    core = lax.rem(lax.axis_index("gx"), 2)
    keep[...] = sums[pl.ds(pl.multiple_of(core * half, 8), half), :]
    give[...] = sums[pl.ds(pl.multiple_of((1 - core) * half, 8), half), :]


def several(total, one, most):
    deep = next(n for n in range(most, 0, -1) if total % n == 0)

    def some(r, none):
        for i in range(deep):
            one(r * deep + i, 0)
        return none

    lax.fori_loop(0, total // deep, some, 0)


def folded_rows(count, snap_count):
    used = count + snap_count * (count // LANE) + snap_count // 2 + 1
    return -(-used // 16) * 16


def lower_mask(side):
    row = lax.broadcasted_iota(jnp.int32, (side, side), 0)
    column = lax.broadcasted_iota(jnp.int32, (side, side), 1)
    return row > column, row == column


def fold(sums, inner_uu, inner_su, inner_ss):
    below, on = lower_mask(LANE)
    first = inner_uu[:LANE, :LANE]
    sums[:LANE] = jnp.where(below, first, inner_uu[LANE:, LANE:])
    sums[LANE : 2 * LANE] = inner_uu[LANE:, :LANE]
    snap_count = inner_su.shape[0]
    at = 2 * LANE
    for tile in range(2):
        sums[at : at + snap_count] = inner_su[:, tile * LANE : (tile + 1) * LANE]
        at += snap_count
    half = snap_count // 2
    sums[at : at + half] = jnp.concatenate([inner_ss[:half], inner_ss[half:]], 1)
    at += half
    diagonal = jnp.sum(jnp.where(on, first, 0.0), axis=0, keepdims=True)
    left = sums.shape[0] - at
    sums[at:] = jnp.broadcast_to(diagonal, (left, LANE))


def unfold(sums, grams, snap_count, scale):
    count = 2 * LANE
    below, on = lower_mask(LANE)
    mixed = sums[:LANE] * scale
    cross = sums[LANE : 2 * LANE] * scale
    at = count + 2 * snap_count
    half = snap_count // 2
    diagonal = sums[at + half : at + half + 1] * scale
    low = jnp.where(below, mixed, 0.0)
    high = jnp.where(below, 0.0, mixed)
    grams[:LANE, :LANE] = low + low.T + jnp.where(on, jnp.broadcast_to(diagonal, on.shape), 0.0)
    grams[LANE:count, LANE:count] = high + jnp.where(on, 0.0, high).T
    grams[LANE:count, :LANE] = cross
    grams[:LANE, LANE:count] = cross.T
    for tile in range(2):
        part = sums[count + tile * snap_count : count + (tile + 1) * snap_count] * scale
        grams[count : count + snap_count, tile * LANE : (tile + 1) * LANE] = part
        wide = jnp.concatenate([part, jnp.zeros((LANE - snap_count, LANE), jnp.float32)], 0)
        grams[tile * LANE : (tile + 1) * LANE, count:] = wide.T
    folded = sums[at : at + half] * scale
    grams[count : count + half, count : count + snap_count] = folded[:, :snap_count]
    grams[count + half : count + snap_count, count : count + snap_count] = folded[:, snap_count:]


def flux(fields, perm_table, inflow, inner_uu, basis_blocks, along):
    fast = len(fields) > 1
    wide, total_y, group, lanes = inflow.shape
    blocks = total_y // along
    rows = wide - 2 * STEPS
    count = basis_blocks.shape[-1]
    snaps = 2 * STEPS * group
    folded = folded_rows(count, snaps)
    f32 = jnp.float32
    fin = (rows, along, 2 * group, lanes) if fast else (rows, blocks, along, 2 * group, lanes)
    outs = [
        jax.ShapeDtypeStruct((rows * total_y, snaps, lanes), jnp.bfloat16),
        jax.ShapeDtypeStruct((folded // 2, LANE), f32),
        jax.ShapeDtypeStruct((folded // 2, LANE), f32),
        jax.ShapeDtypeStruct(fin, f32),
        jax.ShapeDtypeStruct(fin if fast else (8, lanes), f32),
    ]
    state = pltpu.VMEM((wide, total_y + 1, group, lanes), f32)
    whole = pl.BlockSpec(memory_space=pltpu.VMEM)
    return pl.pallas_call(
        lambda *refs: flux_kernel(fast, *refs),
        out_shape=outs,
        in_specs=[whole] * len(fields)
        + [pl.BlockSpec(memory_space=pltpu.SMEM), whole, whole, pl.BlockSpec(memory_space=pl.ANY)],
        scratch_shapes=[
            state, state, state, state,
            pltpu.VMEM((wide, blocks, along, lanes), f32),
            pltpu.VMEM((3, wide + 1, total_y + 8, lanes), f32),
            pltpu.VMEM((3, wide, blocks, along, lanes), f32),
            pltpu.VMEM((3, wide, blocks, along, lanes), f32),
            pltpu.VMEM((2, total_y, group, lanes), f32),
            pltpu.VMEM((rows * total_y, snaps, lanes), f32),
            pltpu.VMEM((folded, LANE), f32),
            pltpu.VMEM(basis_blocks.shape, jnp.bfloat16),
            pltpu.SemaphoreType.DMA,
        ],
        compiler_params=pltpu.CompilerParams(vmem_limit_bytes=VMEM_LIMIT),
    )(*fields, perm_table, inflow, inner_uu, basis_blocks)


def unpack_kernel(parts, *refs):
    out_ref = refs[-1]
    along = refs[0].shape[1]
    members = refs[0].shape[2]
    stride = out_ref.shape[0] // members
    sec = lax.axis_index("sec")
    for part in range(parts):
        rows = refs[part].shape[0]
        start = 0 if parts == 1 else (sec if part == 0 else 1 - sec) * rows
        for x in range(rows):
            for y in range(along):
                out_ref[pl.ds((start + x) * along + y, members, stride=stride), :] = refs[part][x, y]


def unpack(parts):
    rows, along, members, lanes = parts[0].shape
    across = rows * len(parts)
    out = pl.pallas_call(
        lambda *refs: unpack_kernel(len(parts), *refs),
        out_shape=jax.ShapeDtypeStruct((members * across * along, lanes), jnp.float32),
        compiler_params=pltpu.CompilerParams(vmem_limit_bytes=VMEM_LIMIT),
    )(*parts)
    return out.reshape(members, across, along, lanes)


def all_sum(keep, give):
    counts = [lax.axis_size(axis) for axis in AXES]
    total = counts[0] * counts[1]
    pair = counts[1]
    swap = [(i, i ^ pair) for i in range(total)]
    value = keep + lax.ppermute(give, AXES, swap)
    masks = [1 << b for b in range(total.bit_length() - 1) if 1 << b != pair]
    turned = list(masks)
    for i in range(0, len(masks) - 1, 2):
        turned[i], turned[i + 1] = masks[i + 1], masks[i]
    for even, odd in zip(masks, turned):
        value = value + lax.ppermute(value, AXES, [(i, i ^ (odd if i & pair else even)) for i in range(total)])
    return value, lax.ppermute(value, AXES, swap)


def to_bf16(value):
    return value.astype(jnp.bfloat16)


def hdot(a, b, left=1, right=0):
    return lax.dot_general(a, b, (((left,), (right,)), ((), ())), precision=HIGHEST, preferred_element_type=jnp.float32)

SUB = 8
PANEL = 32
LANE = 128

def eliminate(panel, column):
    groups = PANEL // SUB
    tiles = panel.shape[1] // LANE
    below = lax.broadcasted_iota(jnp.int32, (SUB, LANE), 0)
    strip = [[panel[h * SUB:(h + 1) * SUB, t * LANE:(t + 1) * LANE] for t in range(tiles)] for h in range(groups)]
    for g in range(groups):
        spread = {}
        for h in range(g, groups):
            for j in range(SUB):
                at = column + g * SUB + j
                tile, lane = at // LANE, at % LANE
                spread[h, j] = jnp.broadcast_to(strip[h][tile][:, lane:lane + 1], (SUB, LANE))
        scale = jnp.zeros((SUB, LANE), jnp.float32)
        for j in range(SUB):
            pivot = jnp.broadcast_to(spread[g, j][j:j + 1], (SUB, LANE))
            inverse = 1.0 / pivot
            scale = jnp.where(below == j, pivot, scale)
            factors = {}
            for h in range(g, groups):
                factors[h] = spread[h, j] * inverse
            factors[g] = jnp.where(below > j, factors[g], 0.0)
            for k in range(j + 1, SUB):
                row = jnp.broadcast_to(spread[g, k][j:j + 1], (SUB, LANE))
                for h in range(g, groups):
                    spread[h, k] = spread[h, k] - factors[h] * row
            for t in range(tiles):
                row = jnp.broadcast_to(strip[g][t][j:j + 1], (SUB, LANE))
                for h in range(g, groups):
                    strip[h][t] = strip[h][t] - factors[h] * row
        root = lax.rsqrt(scale)
        for t in range(tiles):
            strip[g][t] = strip[g][t] * root
    return jnp.concatenate([jnp.concatenate(s, 1) for s in strip], 0)

def solve(aug, count):
    width = aug.shape[1]
    for start in range(0, count, PANEL):
        first = start // LANE * LANE
        done = eliminate(aug[start:start + PANEL, first:], start - first)
        aug[start:start + PANEL, first:] = done
        rest = start + PANEL
        if rest < count:
            base = rest // LANE * LANE
            left = done[:, base - first:count - first]
            change = hdot(left, done[:, base - first:], 0, 0)
            aug[rest:, base:] = aug[rest:, base:] - change[rest - base:]

def small_kernel(scale, mine_ref, other_ref, sigma_ref, high_ref, low_ref, snap_ref, sigma_out, aug, sums, gram_ref):
    count = sigma_ref.shape[1]
    snaps = (gram_ref.shape[0] - count) // 2
    half = sums.shape[0] // 2
    core = lax.rem(lax.axis_index("gx"), 2)
    sums[pl.ds(pl.multiple_of(core * half, 8), half), :] = mine_ref[...]
    sums[pl.ds(pl.multiple_of((1 - core) * half, 8), half), :] = other_ref[...]
    unfold(sums, gram_ref, 2 * snaps, scale)
    eye = lax.broadcasted_iota(jnp.int32, (count, count), 0) == lax.broadcasted_iota(jnp.int32, (count, count), 1)
    pad = LANE - snaps
    sig2 = sigma_ref[...] * sigma_ref[...]
    prior = None
    for group in range(2):
        rows = gram_ref[count + group * snaps: count + (group + 1) * snaps]
        if group == 0:
            coeffs = rows[:, :count]
            own = rows[:, count:count + snaps]
        else:
            reach = count + snaps
            coeffs = hdot(rows[:, :reach], prior[:, :reach], 1, 1)
            own = rows[:, reach:reach + snaps]
        rounded = coeffs.astype(jnp.bfloat16).astype(jnp.float32)
        if group == 0:
            mapped = rounded
            known = gram_ref[:count, :count]
        else:
            mapped = hdot(rounded, prior[:, :reach])
            known = gram_ref[:reach, :reach]
        spread = hdot(mapped, known)
        gram = own - hdot(rounded, coeffs, 1, 1) - hdot(coeffs, rounded, 1, 1) + hdot(spread, mapped, 1, 1)
        lead = hdot(coeffs, coeffs, 0, 0) + jnp.where(eye, jnp.broadcast_to(sig2, eye.shape), 0.0)
        inner = hdot(lead, lead) + hdot(coeffs, hdot(gram, coeffs), 0, 0)
        aug[:, :count] = inner
        aug[:, count:2 * count] = lead
        aug[:, 2 * count:] = jnp.concatenate([coeffs, jnp.zeros((pad, count), jnp.float32)], 0).T
        solve(aug, count)
        turned = aug[:, count:2 * count]
        extra = aug[:, 2 * count:2 * count + snaps]
        energy = turned * turned * sig2
        ones = jnp.ones((8, count), jnp.float32)
        low = hdot(turned, coeffs, 1, 1) + hdot(extra, gram)
        sig2 = hdot(ones, energy, 1, 1)[:1] + hdot(ones[:, :snaps], low * low, 1, 1)[:1]
        step = turned.astype(jnp.bfloat16).astype(jnp.float32) - hdot(extra, rounded)
        if group == 0:
            prior = jnp.concatenate([step, aug[:, 2 * count:]], 1)
        else:
            final = hdot(step, prior)
            high = final[:, :count].astype(jnp.bfloat16)
            high_ref[...] = high
            low_ref[...] = (final[:, :count] - high.astype(jnp.float32)).astype(jnp.bfloat16)
            both = jnp.concatenate([final[:, count:].T[:snaps], aug[:, 2 * count:].T[:snaps]], 0)
            high = both.astype(jnp.bfloat16)
            snap_ref[:2 * snaps] = high
            snap_ref[2 * snaps:] = (both - high.astype(jnp.float32)).astype(jnp.bfloat16)
    sigma_out[...] = jnp.sqrt(sig2)

def small(mine, other, sigma, snap_count, rows_total):
    count = sigma.shape[0]
    rows = count + snap_count
    high, low, snap_weights, sigma_out = pl.pallas_call(
        functools.partial(small_kernel, 1.0 / rows_total),
        out_shape=(
            jax.ShapeDtypeStruct((count, count), jnp.bfloat16),
            jax.ShapeDtypeStruct((count, count), jnp.bfloat16),
            jax.ShapeDtypeStruct((2 * snap_count, count), jnp.bfloat16),
            jax.ShapeDtypeStruct((1, count), jnp.float32),
        ),
        scratch_shapes=[
            pltpu.VMEM((count, 2 * count + LANE), jnp.float32),
            pltpu.VMEM((2 * mine.shape[0], LANE), jnp.float32),
            pltpu.VMEM((rows, count + LANE), jnp.float32),
        ],
        compiler_params=pltpu.CompilerParams(vmem_limit_bytes=VMEM_LIMIT),
        cost_estimate=pl.CostEstimate(flops=2 * 10**10, bytes_accessed=2**20, transcendentals=0),
    )(mine, other, sigma.reshape(1, count))
    return high, low, snap_weights, sigma_out.reshape(count)


def renew_kernel(basis_ref, snaps_ref, high_ref, low_ref, snap_ref, out_ref):
    lanes = snaps_ref.shape[2]
    flat = basis_ref[...]
    turned = (((1,), (1,)), ((), ()))
    value = lax.dot_general(flat, high_ref[...], turned, preferred_element_type=jnp.float32)
    value += lax.dot_general(flat, low_ref[...], turned, preferred_element_type=jnp.float32)
    for q in range(snaps_ref.shape[0]):
        part = snaps_ref[q]
        part = lax.dot_general(
            jnp.concatenate([part, part], 0), snap_ref[...], (((0,), (0,)), ((), ())),
            preferred_element_type=jnp.float32,
        )
        out_ref[q * lanes : (q + 1) * lanes] = (value[q * lanes : (q + 1) * lanes] + part).astype(jnp.bfloat16)


def renew(flat, snaps, high, low, snap_weights):
    cells, snap_count, lanes = snaps.shape
    count = flat.shape[1]
    run = next(n for n in (8, 4, 2, 1) if cells % n == 0)
    same = lambda i: (0, 0)
    return pl.pallas_call(
        renew_kernel,
        out_shape=jax.ShapeDtypeStruct(flat.shape, jnp.bfloat16),
        grid=(cells // run,),
        in_specs=[
            pl.BlockSpec((run * lanes, count), lambda i: (i, 0)),
            pl.BlockSpec((run, snap_count, lanes), lambda i: (i, 0, 0)),
            pl.BlockSpec((count, count), same),
            pl.BlockSpec((count, count), same),
            pl.BlockSpec((2 * snap_count, count), same),
        ],
        out_specs=pl.BlockSpec((run * lanes, count), lambda i: (i, 0)),
        compiler_params=pltpu.CompilerParams(vmem_limit_bytes=VMEM_LIMIT),
    )(flat, snaps, high, low, snap_weights)


def body(state_init, rock_type, perm_table, well_cells, well_rate, basis_in, singular):
    members, across, along, lanes = state_init.shape
    gx_count = lax.axis_size("gx")
    sec_count = lax.axis_size("sec")
    rows = across // sec_count
    wide = rows + 2 * STEPS
    total_y = along * sec_count
    count = basis_in.shape[-1]
    fast = sec_count == 2 and across == 2 * STEPS
    inflow = well_inflow(well_cells, well_rate, wide, total_y, lanes)
    if fast:
        own, packed, outward, inward = pack(state_init, rock_type, True)
        straight, crossed = [], []
        for r in range(gx_count):
            if r > 0:
                straight.append((2 * (r - 1), 2 * r))
                crossed.append((2 * (r - 1) + 1, 2 * r))
            if r < gx_count - 1:
                straight.append((2 * (r + 1) + 1, 2 * r + 1))
                crossed.append((2 * (r + 1), 2 * r + 1))
        other = lax.ppermute(packed, "sec", [(0, 1), (1, 0)])
        cross = lax.ppermute(inward, AXES, crossed)
        beside = lax.ppermute(outward, AXES, straight)
        fields = (own, packed, other, beside, cross)
    else:
        _, packed = pack(state_init, rock_type, False)
        slab = lax.all_gather(packed, "sec", axis=1)
        low = lax.ppermute(slab[across - STEPS :], "gx", [(i, i + 1) for i in range(gx_count - 1)])
        high = lax.ppermute(slab[:STEPS], "gx", [(i + 1, i) for i in range(gx_count - 1)])
        padded = jnp.concatenate([low, slab, high], 0)
        fields = (lax.dynamic_slice_in_dim(padded, lax.axis_index("sec") * rows, wide, axis=0),)
    flat = basis_in.reshape(-1, count)
    rows_total = flat.shape[0] * gx_count * sec_count
    inner_uu = lax.dot_general(flat, flat, (((0,), (0,)), ((), ())), preferred_element_type=jnp.float32)
    snaps, keep, give, fin, send = flux(
        fields, perm_table, inflow, inner_uu, flat.reshape(-1, lanes, count), along
    )
    mine, others = all_sum(keep, give)
    if fast:
        send, mine = lax.optimization_barrier((send, mine))
        received = lax.ppermute(send, "sec", [(0, 1), (1, 0)])
    high, low, snap_weights, sigma = small(mine, others, singular, snaps.shape[1], rows_total)
    if fast:
        state_out = unpack((fin, received))
    else:
        moved = lax.all_to_all(fin, "sec", split_axis=1, concat_axis=0, tiled=True)
        state_out = unpack((moved.reshape(across, along, members, lanes),))
    fresh = renew(flat, snaps, high, low, snap_weights)
    return state_out, fresh.reshape(basis_in.shape), sigma


def solution(mesh):
    return jax.shard_map(
        body,
        mesh=mesh,
        in_specs=(
            P(None, "gx", "sec", None),
            P("gx", "sec"),
            P(),
            P(),
            P(),
            P(("gx", "sec"), None, None, None),
            P(),
        ),
        out_specs=(P(None, "gx", "sec", None), P(("gx", "sec"), None, None, None), P()),
        check_vma=False,
    )
```

```python
import functools

import jax
import jax.numpy as jnp
from jax import lax
from jax.experimental import pallas as pl
from jax.experimental.pallas import tpu as pltpu
from jax.sharding import PartitionSpec as P

MG = 8
STEPS = 4
GROUPS = 2

DT_PRESSURE = 0.12
DT_SATURATION = 0.06
DT_ADVECT = 0.15
HIGHEST = lax.Precision.HIGHEST
AXES = ("gx", "sec")
VMEM_LIMIT = 48 * 2**20


def place(wide_rows):
    sec_count = lax.axis_size("sec")
    rows = wide_rows - 2 * STEPS
    first = (lax.axis_index("gx") * sec_count + lax.axis_index("sec")) * rows - STEPS
    return first, rows * sec_count * lax.axis_size("gx")


def pack_kernel(state_ref, rock_ref, own, packed, rock_rows):
    across, entries, members, lanes = packed.shape
    along = entries - 1
    layers = lanes // 2
    group = members // 2
    stride = across * along
    left_lanes = lax.broadcasted_iota(jnp.int32, (group, lanes), 1) < layers
    rock_rows[...] = jnp.zeros_like(rock_rows)
    for y in range(along):
        chunk = rock_ref[:, y * layers : (y + 1) * layers].astype(jnp.float32)
        rock_rows[pl.ds(y, across, stride=members), :] = jnp.concatenate([chunk, chunk], 1)
    for x in range(across):
        for y in range(along):
            at = x * along + y
            low = state_ref[pl.ds(at, group, stride=stride), :]
            high = state_ref[pl.ds(at + group * stride, group, stride=stride), :]
            column = jnp.concatenate(halves_swap(low, high, left_lanes, layers), 0)
            own[x, y] = column
            packed[x, y] = column.astype(jnp.bfloat16)
        packed[x, along] = rock_rows[x * members : (x + 1) * members].astype(jnp.bfloat16)


def pack(state_init, rock_type):
    members, across, along, lanes = state_init.shape
    shape = (along + 1, members, lanes)
    outs = [
        jax.ShapeDtypeStruct((across, along, members, lanes), jnp.float32),
        jax.ShapeDtypeStruct((across,) + shape, jnp.bfloat16),
    ]

    def kernel(state_hbm, rock_hbm, *refs):
        own, packed = refs[:2]
        rock_rows, state_ref, rock_ref, state_sem, rock_sem = refs[-5:]
        state_copy = pltpu.make_async_copy(state_hbm, state_ref, state_sem)
        rock_copy = pltpu.make_async_copy(rock_hbm, rock_ref, rock_sem)
        state_copy.start()
        rock_copy.start()
        rock_copy.wait()
        state_copy.wait()
        pack_kernel(state_ref, rock_ref, own, packed, rock_rows)

    return pl.pallas_call(
        kernel,
        out_shape=outs,
        in_specs=[pl.BlockSpec(memory_space=pl.ANY)] * 2,
        scratch_shapes=[
            pltpu.VMEM((across * members, lanes), jnp.float32),
            pltpu.VMEM((members * across * along, lanes), jnp.float32),
            pltpu.VMEM(rock_type.shape, jnp.int32),
            pltpu.SemaphoreType.DMA,
            pltpu.SemaphoreType.DMA,
        ],
        compiler_params=pltpu.CompilerParams(vmem_limit_bytes=VMEM_LIMIT),
    )(state_init.reshape(-1, lanes), rock_type)


def split_kernel(packed, outward, inward):
    half = packed.shape[0] // 2
    sec = lax.axis_index("sec")
    outward[...] = packed[pl.ds((1 - sec) * half, half)]
    inward[...] = packed[pl.ds(sec * half, half)]


def split(packed):
    half = jax.ShapeDtypeStruct((packed.shape[0] // 2,) + packed.shape[1:], packed.dtype)
    return pl.pallas_call(
        split_kernel, out_shape=(half, half), compiler_params=pltpu.CompilerParams(vmem_limit_bytes=VMEM_LIMIT)
    )(packed)


def inflow_rows(cell_row, rate_ref, out_ref, wide, total_y):
    columns = wide * total_y
    members, wells = rate_ref.shape
    group = members // 2
    lanes = out_ref.shape[1]
    layers = lanes // 2
    first, _ = place(wide)
    start = first * total_y
    row = lax.broadcasted_iota(jnp.int32, (columns, wells), 0)
    near = lax.div(cell_row[...], layers) - start
    picks = jnp.where(row == near, 1.0, 0.0).astype(jnp.bfloat16)
    layer = lax.rem(jnp.broadcast_to(cell_row[...], (lanes, wells)).T, layers)
    lane = lax.broadcasted_iota(jnp.int32, (wells, lanes), 1)
    left_lanes = lane < layers
    at = jnp.where(left_lanes, lane, lane - layers) == layer
    short = jnp.zeros((lanes - members, wells), jnp.float32)
    rate = (jnp.concatenate([rate_ref[...], short], 0) * DT_PRESSURE).T
    for m in range(group):
        value = jnp.where(left_lanes, rate[:, m : m + 1], rate[:, m + group : m + group + 1])
        value = jnp.where(at, value, 0.0)
        sums = [jnp.dot(picks, t, preferred_element_type=jnp.float32) for t in terms(value)]
        out_ref[pl.ds(m, columns, stride=group), :] = (sums[2] + sums[1]) + sums[0]


def prepare_kernel(wide, total_y, parts, cell_row, rate_ref, basis_hbm, inflow, inner_uu, basis, sems):
    run = basis.shape[0] // parts
    copies = [
        pltpu.make_async_copy(basis_hbm.at[pl.ds(i * run, run)], basis.at[pl.ds(i * run, run)], sems.at[i])
        for i in range(parts)
    ]
    for copy in copies:
        copy.start()
    inflow_rows(cell_row, rate_ref, inflow, wide, total_y)
    total = jnp.zeros(inner_uu.shape, jnp.float32)
    for i, copy in enumerate(copies):
        copy.wait()
        rows = basis[i * run : (i + 1) * run]
        total += lax.dot_general(rows, rows, (((0,), (0,)), ((), ())), preferred_element_type=jnp.float32)
    inner_uu[...] = total


def prepare(well_cells, well_rate, flat, wide, total_y, lanes):
    members, wells = well_rate.shape
    count = flat.shape[1]
    parts = next(n for n in (4, 2, 1) if flat.shape[0] % (16 * n) == 0)
    whole = pl.BlockSpec(memory_space=pltpu.VMEM)
    inflow, inner_uu = pl.pallas_call(
        functools.partial(prepare_kernel, wide, total_y, parts),
        out_shape=(
            jax.ShapeDtypeStruct((wide * total_y * members // 2, lanes), jnp.float32),
            jax.ShapeDtypeStruct((count, count), jnp.float32),
        ),
        in_specs=[whole, whole, pl.BlockSpec(memory_space=pl.ANY)],
        scratch_shapes=[pltpu.VMEM(flat.shape, jnp.bfloat16), pltpu.SemaphoreType.DMA((parts,))],
        compiler_params=pltpu.CompilerParams(vmem_limit_bytes=VMEM_LIMIT),
        cost_estimate=pl.CostEstimate(flops=4 * 10**9, bytes_accessed=2**20, transcendentals=0),
    )(well_cells.reshape(1, wells), well_rate, flat)
    return inflow.reshape(wide, total_y, members // 2, lanes), inner_uu


def roll(value, shift):
    return pltpu.roll(value, shift, 1)


def halves_swap(low, high, left_lanes, layers):
    return (
        jnp.where(left_lanes, low, roll(high, layers)),
        jnp.where(left_lanes, roll(low, layers), high),
    )


def harmonic(left, right):
    total = left + right
    return jnp.where(total > 0.0, 2.0 * left * right / jnp.where(total > 0.0, total, 1.0), 0.0)


def face(w12, w06, p, s, p_next, s_next):
    push = w12 * (p_next - p)
    carried = push * jnp.where(push > 0.0, s_next, s)
    return push, w06 * (s_next - s) + (DT_ADVECT / DT_PRESSURE) * carried


def flux_kernel(fast, *refs):
    if fast:
        own_ref, packed, other, beside, cross = refs[:5]
        refs = refs[5:]
    else:
        slab = refs[0]
        refs = refs[1:]
    table, inflow, inner_uu, basis_hbm, snaps, keep, give, fin, send = refs[:9]
    press_a, sat_a, press_b, sat_b, rock, perm, w12, w06, carry, history, sums, basis, sem = refs[9:]
    wide, total_y = inflow.shape[:2]
    group, lanes = inflow.shape[2:]
    layers = lanes // 2
    blocks, along = rock.shape[1:3]
    rows = wide - 2 * STEPS
    copy = pltpu.make_async_copy(basis_hbm, basis, sem)
    copy.start()
    lane = lax.broadcasted_iota(jnp.int32, (group, lanes), 1)
    left_lanes = lane < layers
    lane_y = lax.broadcasted_iota(jnp.int32, (along, lanes), 1)
    sec = lax.axis_index("sec")

    def put_packed(ref, count, x_at, block):
        def row(x, c):
            for y in range(along):
                value = ref[x, y].astype(jnp.float32)
                press_a[x_at + x, block * along + y] = value[:group]
                sat_a[x_at + x, block * along + y] = value[group:]
            rock[x_at + x, block] = ref[x, along].astype(jnp.float32)[:along]
            return c

        lax.fori_loop(0, count, row, 0)

    if fast:
        across = packed.shape[0]
        here, there = (1 - sec) * STEPS, sec * across

        def own(x, c):
            for y in range(along):
                press_a[here + x, sec * along + y] = own_ref[x, y, :group]
                sat_a[here + x, sec * along + y] = own_ref[x, y, group:]
            rock[here + x, sec] = packed[x, along].astype(jnp.float32)[:along]
            return c

        lax.fori_loop(0, across, own, 0)
        put_packed(other, across, here, 1 - sec)
        put_packed(beside, STEPS, there, sec)
        put_packed(cross, STEPS, there, 1 - sec)
    else:
        for block in range(blocks):
            put_packed(slab.at[:, block], wide, 0, block)
    zero = jnp.zeros((group, lanes), jnp.float32)
    for x in range(wide):
        for ref in (press_a, sat_a, press_b, sat_b):
            ref[x, total_y] = zero

    first, total_x = place(wide)

    def look_up(x, c):
        inside = ((first + x >= 0) & (first + x < total_x)).astype(jnp.float32)
        for block in range(blocks):
            kind = rock[x, block]
            values = [jnp.zeros((along, lanes), jnp.float32)] * 3
            for r in range(table.shape[1]):
                here = kind == float(r)
                values = [jnp.where(here, table[d, r], values[d]) for d in range(3)]
            for d in range(3):
                perm[d, x, pl.ds(block * along, along), :] = values[d] * inside
        return c

    several(wide, look_up, 4)
    for d in range(3):
        perm[d, wide] = jnp.zeros(perm.shape[2:], jnp.float32)
    perm[1, :, total_y:, :] = jnp.zeros((wide + 1, perm.shape[2] - total_y, lanes), jnp.float32)

    def weigh(x, c):
        for block in range(blocks):
            at = block * along
            here = [perm[d, x, pl.ds(at, along), :] for d in range(3)]
            z_next = jnp.where((lane_y == layers - 1) | (lane_y == lanes - 1), 0.0, roll(here[2], lanes - 1))
            beyond = (perm[0, x + 1, pl.ds(at, along), :], perm[1, x, pl.ds(at + 1, along), :], z_next)
            for d in range(3):
                weight = harmonic(here[d], beyond[d])
                w12[d, x, block] = DT_PRESSURE * weight
                w06[d, x, block] = DT_SATURATION * weight
        return c

    several(wide, weigh, 4)

    def spread(ref, d, x, block, j):
        return jnp.broadcast_to(ref[d, x, block, j : j + 1, :], (group, lanes))

    def x_face(p_ref, s_ref, x, block, j):
        y = block * along + j
        return face(
            spread(w12, 0, x, block, j), spread(w06, 0, x, block, j),
            p_ref[x, y], s_ref[x, y], p_ref[x + 1, y], s_ref[x + 1, y],
        )

    buffers = [(press_a, sat_a), (press_b, sat_b)]
    chunk = along * next(n for n in (2, 1) if blocks % n == 0)
    chunks = total_y // chunk

    def columns(c):
        return [(c * chunk + i, c * (chunk // along) + i // along, i % along) for i in range(chunk)]

    for step in range(STEPS):
        (p_ref, s_ref), (p_new, s_new) = buffers[step % 2], buffers[(step + 1) % 2]

        def begin(c, none):
            for y, block, j in columns(c):
                carry[0, y], carry[1, y] = x_face(p_ref, s_ref, step, block, j)
            return none

        lax.fori_loop(0, chunks, begin, 0)
        span = wide - 2 - 2 * step
        deep = 2 if span % 2 == 0 else 1

        def some_rows(r, none):
            x0 = step + 1 + r * deep

            def one_chunk(c, back):
                back = list(back)
                for y, block, j in columns(c):
                    before = carry[0, y], carry[1, y]
                    for i in range(deep):
                        x = x0 + i
                        p, s = p_ref[x, y], s_ref[x, y]
                        xp, xs = x_face(p_ref, s_ref, x, block, j)
                        yp, ys = face(
                            spread(w12, 1, x, block, j), spread(w06, 1, x, block, j),
                            p, s, p_ref[x, y + 1], s_ref[x, y + 1],
                        )
                        zp, zs = face(
                            spread(w12, 2, x, block, j), spread(w06, 2, x, block, j),
                            p, s, roll(p, lanes - 1), roll(s, lanes - 1),
                        )
                        back_p, back_s = back[2 * i : 2 * i + 2]
                        p_new[x, y] = p + (xp - before[0]) + (yp - back_p) + (zp - roll(zp, 1)) + inflow[x, y]
                        s_new[x, y] = s + (xs - before[1]) + (ys - back_s) + (zs - roll(zs, 1))
                        before = xp, xs
                        back[2 * i : 2 * i + 2] = [yp, ys]
                    carry[0, y], carry[1, y] = before
                return tuple(back)

            lax.fori_loop(0, chunks, one_chunk, (zero,) * (2 * deep))
            return none

        lax.fori_loop(0, span // deep, some_rows, 0)

        def save(x, none):
            def save_chunk(c, none):
                for y, block, j in columns(c):
                    low, high = halves_swap(p_new[STEPS + x, y], s_new[STEPS + x, y], left_lanes, layers)
                    history[x * total_y + y, step * group : (step + 1) * group] = low
                    history[x * total_y + y, (STEPS + step) * group : (STEPS + step + 1) * group] = high
                    if step == STEPS - 1 and not fast:
                        fin[x, block, j] = jnp.concatenate([low, high], 0)
                return none

            return lax.fori_loop(0, chunks, save_chunk, none)

        several(rows, save, 2)

    if fast:
        last = slice((STEPS - 1) * group, STEPS * group)
        past = slice((2 * STEPS - 1) * group, 2 * STEPS * group)
        for ref, block in ((fin, sec), (send, 1 - sec)):
            for x in range(rows):
                for j in range(along):
                    at = x * total_y + block * along + j
                    ref[x, j, :group] = history[at, last]
                    ref[x, j, group:] = history[at, past]

    copy.wait()
    count = basis.shape[2]
    cells = rows * total_y
    snap_count = 2 * STEPS * group
    run = next(n for n in (16, 8, 4, 2, 1) if cells % n == 0)
    inner_su = jnp.zeros((snap_count, count), jnp.float32)
    inner_ss = jnp.zeros((snap_count, snap_count), jnp.float32)
    for q in range(0, cells, run):
        part = [history[q + i].astype(jnp.bfloat16) for i in range(run)]
        for i in range(run):
            snaps[q + i] = part[i]
        both = jnp.concatenate(part, 1)
        inner_su += jnp.dot(both, basis[q : q + run].reshape(run * lanes, count), preferred_element_type=jnp.float32)
        inner_ss += lax.dot_general(both, both, (((1,), (1,)), ((), ())), preferred_element_type=jnp.float32)
    fold(sums, inner_uu, inner_su, inner_ss)
    half = sums.shape[0] // 2
    core = lax.rem(lax.axis_index("gx"), 2)
    keep[...] = sums[pl.ds(pl.multiple_of(core * half, 8), half), :]
    give[...] = sums[pl.ds(pl.multiple_of((1 - core) * half, 8), half), :]


def several(total, one, most):
    deep = next(n for n in range(most, 0, -1) if total % n == 0)

    def some(r, none):
        for i in range(deep):
            one(r * deep + i, 0)
        return none

    lax.fori_loop(0, total // deep, some, 0)


def folded_rows(count, snap_count):
    used = count + snap_count * (count // LANE) + snap_count // 2 + 1
    return -(-used // 16) * 16


def lower_mask(side):
    row = lax.broadcasted_iota(jnp.int32, (side, side), 0)
    column = lax.broadcasted_iota(jnp.int32, (side, side), 1)
    return row > column, row == column


def fold(sums, inner_uu, inner_su, inner_ss):
    below, on = lower_mask(LANE)
    first = inner_uu[:LANE, :LANE]
    sums[:LANE] = jnp.where(below, first, inner_uu[LANE:, LANE:])
    sums[LANE : 2 * LANE] = inner_uu[LANE:, :LANE]
    snap_count = inner_su.shape[0]
    at = 2 * LANE
    for tile in range(2):
        sums[at : at + snap_count] = inner_su[:, tile * LANE : (tile + 1) * LANE]
        at += snap_count
    half = snap_count // 2
    sums[at : at + half] = jnp.concatenate([inner_ss[:half], inner_ss[half:]], 1)
    at += half
    diagonal = jnp.sum(jnp.where(on, first, 0.0), axis=0, keepdims=True)
    left = sums.shape[0] - at
    sums[at:] = jnp.broadcast_to(diagonal, (left, LANE))


def unfold(sums, grams, snap_count, scale):
    count = 2 * LANE
    below, on = lower_mask(LANE)
    mixed = sums[:LANE] * scale
    cross = sums[LANE : 2 * LANE] * scale
    at = count + 2 * snap_count
    half = snap_count // 2
    diagonal = sums[at + half : at + half + 1] * scale
    low = jnp.where(below, mixed, 0.0)
    high = jnp.where(below, 0.0, mixed)
    grams[:LANE, :LANE] = low + low.T + jnp.where(on, jnp.broadcast_to(diagonal, on.shape), 0.0)
    grams[LANE:count, LANE:count] = high + jnp.where(on, 0.0, high).T
    grams[LANE:count, :LANE] = cross
    grams[:LANE, LANE:count] = cross.T
    for tile in range(2):
        part = sums[count + tile * snap_count : count + (tile + 1) * snap_count] * scale
        grams[count : count + snap_count, tile * LANE : (tile + 1) * LANE] = part
        wide = jnp.concatenate([part, jnp.zeros((LANE - snap_count, LANE), jnp.float32)], 0)
        grams[tile * LANE : (tile + 1) * LANE, count:] = wide.T
    folded = sums[at : at + half] * scale
    grams[count : count + half, count : count + snap_count] = folded[:, :snap_count]
    grams[count + half : count + snap_count, count : count + snap_count] = folded[:, snap_count:]


def flux(fields, perm_table, inflow, inner_uu, basis_blocks, along):
    fast = len(fields) > 1
    wide, total_y, group, lanes = inflow.shape
    blocks = total_y // along
    rows = wide - 2 * STEPS
    count = basis_blocks.shape[-1]
    snaps = 2 * STEPS * group
    folded = folded_rows(count, snaps)
    f32 = jnp.float32
    fin = (rows, along, 2 * group, lanes) if fast else (rows, blocks, along, 2 * group, lanes)
    outs = [
        jax.ShapeDtypeStruct((rows * total_y, snaps, lanes), jnp.bfloat16),
        jax.ShapeDtypeStruct((folded // 2, LANE), f32),
        jax.ShapeDtypeStruct((folded // 2, LANE), f32),
        jax.ShapeDtypeStruct(fin, f32),
        jax.ShapeDtypeStruct(fin if fast else (8, lanes), f32),
    ]
    state = pltpu.VMEM((wide, total_y + 1, group, lanes), f32)
    whole = pl.BlockSpec(memory_space=pltpu.VMEM)
    return pl.pallas_call(
        lambda *refs: flux_kernel(fast, *refs),
        out_shape=outs,
        in_specs=[whole] * len(fields)
        + [pl.BlockSpec(memory_space=pltpu.SMEM), whole, whole, pl.BlockSpec(memory_space=pl.ANY)],
        scratch_shapes=[
            state, state, state, state,
            pltpu.VMEM((wide, blocks, along, lanes), f32),
            pltpu.VMEM((3, wide + 1, total_y + 8, lanes), f32),
            pltpu.VMEM((3, wide, blocks, along, lanes), f32),
            pltpu.VMEM((3, wide, blocks, along, lanes), f32),
            pltpu.VMEM((2, total_y, group, lanes), f32),
            pltpu.VMEM((rows * total_y, snaps, lanes), f32),
            pltpu.VMEM((folded, LANE), f32),
            pltpu.VMEM(basis_blocks.shape, jnp.bfloat16),
            pltpu.SemaphoreType.DMA,
        ],
        compiler_params=pltpu.CompilerParams(vmem_limit_bytes=VMEM_LIMIT),
    )(*fields, perm_table, inflow, inner_uu, basis_blocks)


def unpack_kernel(parts, *refs):
    out_ref = refs[-1]
    along = refs[0].shape[1]
    members = refs[0].shape[2]
    stride = out_ref.shape[0] // members
    sec = lax.axis_index("sec")
    for part in range(parts):
        rows = refs[part].shape[0]
        start = 0 if parts == 1 else (sec if part == 0 else 1 - sec) * rows
        for x in range(rows):
            for y in range(along):
                out_ref[pl.ds((start + x) * along + y, members, stride=stride), :] = refs[part][x, y]


def unpack(parts):
    rows, along, members, lanes = parts[0].shape
    across = rows * len(parts)
    out = pl.pallas_call(
        lambda *refs: unpack_kernel(len(parts), *refs),
        out_shape=jax.ShapeDtypeStruct((members * across * along, lanes), jnp.float32),
        compiler_params=pltpu.CompilerParams(vmem_limit_bytes=VMEM_LIMIT),
    )(*parts)
    return out.reshape(members, across, along, lanes)


def all_sum(keep, give, beside=None):
    swapped = None
    counts = [lax.axis_size(axis) for axis in AXES]
    total = counts[0] * counts[1]
    pair = counts[1]
    swap = [(i, i ^ pair) for i in range(total)]
    value = keep + lax.ppermute(give, AXES, swap)
    masks = [1 << b for b in range(total.bit_length() - 1) if 1 << b != pair]
    turned = list(masks)
    for i in range(0, len(masks) - 1, 2):
        turned[i], turned[i + 1] = masks[i + 1], masks[i]
    for hop, (even, odd) in enumerate(zip(masks, turned)):
        value = value + lax.ppermute(value, AXES, [(i, i ^ (odd if i & pair else even)) for i in range(total)])
        if hop == 1 and beside is not None:
            beside, value = lax.optimization_barrier((beside, value))
            swapped = lax.ppermute(beside, "sec", [(0, 1), (1, 0)])
    return value, lax.ppermute(value, AXES, swap), swapped


def to_bf16(value):
    return value.astype(jnp.bfloat16)


def hdot(a, b, left=1, right=0):
    return lax.dot_general(a, b, (((left,), (right,)), ((), ())), precision=HIGHEST, preferred_element_type=jnp.float32)

SUB = 8
PANEL = 32
LANE = 128

def row_of(value, j):
    return jnp.broadcast_to(value[j:j + 1], (SUB, LANE))

def eliminate(panel, column):
    groups = PANEL // SUB
    tiles = panel.shape[1] // LANE
    row = lax.broadcasted_iota(jnp.int32, (SUB, LANE), 0)
    strip = [[panel[h * SUB:(h + 1) * SUB, t * LANE:(t + 1) * LANE] for t in range(tiles)] for h in range(groups)]
    spread = {}

    def expand(g, first_group):
        for h in range(first_group, groups):
            for j in range(g * SUB, (g + 1) * SUB):
                tile, lane = (column + j) // LANE, (column + j) % LANE
                spread[h, j] = jnp.broadcast_to(strip[h][tile][:, lane:lane + 1], (SUB, LANE))

    expand(0, 0)
    for g in range(groups):
        if g + 1 < groups:
            expand(g + 1, g)
        scale = jnp.zeros((SUB, LANE), jnp.float32)
        for j in range(0, SUB, 2):
            left, right = spread[g, g * SUB + j], spread[g, g * SUB + j + 1]
            a, b, c = row_of(left, j), row_of(right, j), row_of(right, j + 1)
            det = a * c - b * b
            inv_a, inv_det = 1.0 / a, 1.0 / det
            slope = b * inv_a
            second = a * inv_det
            scale = jnp.where(row == j, a, jnp.where(row == j + 1, det * inv_a, scale))
            one, two = {}, {}
            for h in range(g, groups):
                one[h] = spread[h, g * SUB + j] * inv_a
                two[h] = (spread[h, g * SUB + j + 1] - one[h] * b) * second
            one[g] = jnp.where(row > j, one[g], 0.0)
            two[g] = jnp.where(row > j + 1, two[g], 0.0)
            for k in range(g * SUB + j + 2, min(g + 2, groups) * SUB):
                first = row_of(spread[g, k], j)
                next_ = row_of(spread[g, k], j + 1) - slope * first
                for h in range(g, groups):
                    spread[h, k] = spread[h, k] - one[h] * first - two[h] * next_
            for t in range(tiles):
                first = row_of(strip[g][t], j)
                next_ = row_of(strip[g][t], j + 1) - slope * first
                for h in range(g, groups):
                    strip[h][t] = strip[h][t] - one[h] * first - two[h] * next_
        root = lax.rsqrt(scale)
        for t in range(tiles):
            strip[g][t] = strip[g][t] * root
    return jnp.concatenate([jnp.concatenate(s, 1) for s in strip], 0)

def terms(value):
    high = value.astype(jnp.bfloat16)
    rest = value - high.astype(jnp.float32)
    middle = rest.astype(jnp.bfloat16)
    return high, middle, (rest - middle.astype(jnp.float32)).astype(jnp.bfloat16)

def left_stack(t):
    return jnp.concatenate([t[0], t[0], t[1], t[1], t[0], t[2]], 0)

def right_stack(t):
    return jnp.concatenate([t[0], t[1], t[0], t[1], t[2], t[0]], 0)

def stacked_dot(left, right):
    return lax.dot_general(left, right, (((0,), (0,)), ((), ())), preferred_element_type=jnp.float32)

def tdot(a, b):
    return stacked_dot(left_stack(terms(a)), right_stack(terms(b)))

def solve(aug, count):
    for start in range(0, count, PANEL):
        first = start // LANE * LANE
        done = eliminate(aug[start:start + PANEL, first:], start - first)
        aug[start:start + PANEL, first:] = done
        rest = start + PANEL
        if rest < count:
            base = rest // LANE * LANE
            parts = terms(done[:, base - first:])
            left, right = left_stack(parts), right_stack(parts)
            change = stacked_dot(left[:, :count - base], right)
            aug[rest:, base:] = aug[rest:, base:] - change[rest - base:]

def small_kernel(
    scale, mine_ref, other_ref, sigma_ref, snaps_hbm, basis_hbm, fresh_hbm, sigma_out,
    aug, sums, gram_ref, weights, snaps_ref, basis, fresh, in_sems, out_sems,
):
    copies = [
        pltpu.make_async_copy(basis_hbm, basis, in_sems.at[0]),
        pltpu.make_async_copy(snaps_hbm, snaps_ref, in_sems.at[1]),
    ]
    for copy in copies:
        copy.start()
    count = sigma_ref.shape[1]
    snaps = (gram_ref.shape[0] - count) // 2
    half = sums.shape[0] // 2
    core = lax.rem(lax.axis_index("gx"), 2)
    sums[pl.ds(pl.multiple_of(core * half, 8), half), :] = mine_ref[...]
    sums[pl.ds(pl.multiple_of((1 - core) * half, 8), half), :] = other_ref[...]
    unfold(sums, gram_ref, 2 * snaps, scale)
    eye = lax.broadcasted_iota(jnp.int32, (count, count), 0) == lax.broadcasted_iota(jnp.int32, (count, count), 1)
    pad = LANE - snaps
    sig2 = sigma_ref[...] * sigma_ref[...]
    prior = None
    for group in range(2):
        rows = gram_ref[count + group * snaps: count + (group + 1) * snaps]
        if group == 0:
            coeffs = rows[:, :count]
            own = rows[:, count:count + snaps]
        else:
            reach = count + snaps
            coeffs = hdot(rows[:, :reach], prior[:, :reach], 1, 1)
            own = rows[:, reach:reach + snaps]
        rounded = coeffs.astype(jnp.bfloat16).astype(jnp.float32)
        if group == 0:
            mapped = rounded
            known = gram_ref[:count, :count]
        else:
            mapped = hdot(rounded, prior[:, :reach])
            known = gram_ref[:reach, :reach]
        spread = hdot(mapped, known)
        gram = own - hdot(rounded, coeffs, 1, 1) - hdot(coeffs, rounded, 1, 1) + hdot(spread, mapped, 1, 1)
        lead = tdot(coeffs, coeffs) + jnp.where(eye, jnp.broadcast_to(sig2, eye.shape), 0.0)
        inner = hdot(lead, lead) + tdot(coeffs, hdot(gram, coeffs))
        aug[:, :count] = inner
        aug[:, count:2 * count] = lead
        aug[:, 2 * count:] = jnp.concatenate([coeffs, jnp.zeros((pad, count), jnp.float32)], 0).T
        solve(aug, count)
        turned = aug[:, count:2 * count]
        extra = aug[:, 2 * count:2 * count + snaps]
        energy = turned * turned * sig2
        ones = jnp.ones((8, count), jnp.float32)
        low = hdot(turned, coeffs, 1, 1) + hdot(extra, gram)
        sig2 = hdot(ones, energy, 1, 1)[:1] + hdot(ones[:, :snaps], low * low, 1, 1)[:1]
        step = turned.astype(jnp.bfloat16).astype(jnp.float32) - hdot(extra, rounded)
        if group == 0:
            prior = jnp.concatenate([step, aug[:, 2 * count:]], 1)
        else:
            final = hdot(step, prior)
            high = final[:, :count].astype(jnp.bfloat16)
            low = (final[:, :count] - high.astype(jnp.float32)).astype(jnp.bfloat16)
            weights[:count] = high.T
            weights[count:2 * count] = low.T
            both = jnp.concatenate([final[:, count:].T[:snaps], aug[:, 2 * count:].T[:snaps]], 0)
            high = both.astype(jnp.bfloat16)
            weights[2 * count:2 * count + 2 * snaps] = high
            weights[2 * count + 2 * snaps:] = (both - high.astype(jnp.float32)).astype(jnp.bfloat16)
    sigma_out[...] = jnp.sqrt(sig2)
    for copy in copies:
        copy.wait()
    renew(weights, snaps_ref, basis, fresh, fresh_hbm, out_sems)


def renew(weights, snaps_ref, basis, fresh, fresh_hbm, out_sems):
    parts = out_sems.shape[0]
    cells, _, lanes = snaps_ref.shape
    run = cells // parts

    def out(i):
        rows = pl.ds(pl.multiple_of(i * run * lanes, run * lanes), run * lanes)
        return pltpu.make_async_copy(fresh.at[rows], fresh_hbm.at[rows], out_sems.at[i])

    def part(i, none):
        at = pl.multiple_of(i * run * lanes, run * lanes)
        flat = basis[pl.ds(at, run * lanes), :]
        turned = []
        for q in range(run):
            one = snaps_ref[i * run + q]
            turned.append(jnp.concatenate([one, one], 0).T)
        value = jnp.dot(
            jnp.concatenate([flat, flat, jnp.concatenate(turned, 0)], 1), weights[...],
            preferred_element_type=jnp.float32,
        )
        fresh[pl.ds(at, run * lanes), :] = value.astype(jnp.bfloat16)
        out(i).start()
        return none

    lax.fori_loop(0, parts, part, 0)

    def finish(i, none):
        out(i).wait()
        return none

    lax.fori_loop(0, parts, finish, 0)


def small(mine, other, sigma, snaps, flat, rows_total):
    count = sigma.shape[0]
    cells, snap_count, lanes = snaps.shape
    rows = count + snap_count
    parts = next(n for n in (8, 4, 2, 1) if cells % n == 0)
    whole = pl.BlockSpec(memory_space=pltpu.VMEM)
    outside = pl.BlockSpec(memory_space=pl.ANY)
    fresh, sigma_out = pl.pallas_call(
        functools.partial(small_kernel, 1.0 / rows_total),
        out_shape=(
            jax.ShapeDtypeStruct(flat.shape, jnp.bfloat16),
            jax.ShapeDtypeStruct((1, count), jnp.float32),
        ),
        in_specs=[whole, whole, whole, outside, outside],
        out_specs=(outside, whole),
        scratch_shapes=[
            pltpu.VMEM((count, 2 * count + LANE), jnp.float32),
            pltpu.VMEM((2 * mine.shape[0], LANE), jnp.float32),
            pltpu.VMEM((rows, count + LANE), jnp.float32),
            pltpu.VMEM((2 * count + 2 * snap_count, count), jnp.bfloat16),
            pltpu.VMEM(snaps.shape, jnp.bfloat16),
            pltpu.VMEM(flat.shape, jnp.bfloat16),
            pltpu.VMEM(flat.shape, jnp.bfloat16),
            pltpu.SemaphoreType.DMA((2,)),
            pltpu.SemaphoreType.DMA((parts,)),
        ],
        compiler_params=pltpu.CompilerParams(vmem_limit_bytes=VMEM_LIMIT),
        cost_estimate=pl.CostEstimate(flops=2 * 10**10, bytes_accessed=2**20, transcendentals=0),
    )(mine, other, sigma.reshape(1, count), snaps, flat)
    return fresh, sigma_out.reshape(count)


def body(state_init, rock_type, perm_table, well_cells, well_rate, basis_in, singular):
    members, across, along, lanes = state_init.shape
    gx_count = lax.axis_size("gx")
    sec_count = lax.axis_size("sec")
    rows = across // sec_count
    wide = rows + 2 * STEPS
    total_y = along * sec_count
    count = basis_in.shape[-1]
    fast = sec_count == 2 and across == 2 * STEPS
    if fast:
        own, packed = pack(state_init, rock_type)
        outward, inward = split(packed)
        straight, crossed = [], []
        for r in range(gx_count):
            if r > 0:
                straight.append((2 * (r - 1), 2 * r))
                crossed.append((2 * (r - 1) + 1, 2 * r))
            if r < gx_count - 1:
                straight.append((2 * (r + 1) + 1, 2 * r + 1))
                crossed.append((2 * (r + 1), 2 * r + 1))
        other = lax.ppermute(packed, "sec", [(0, 1), (1, 0)])
        cross = lax.ppermute(inward, AXES, crossed)
        beside = lax.ppermute(outward, AXES, straight)
        fields = (own, packed, other, beside, cross)
    else:
        _, packed = pack(state_init, rock_type)
        slab = lax.all_gather(packed, "sec", axis=1)
        low = lax.ppermute(slab[across - STEPS :], "gx", [(i, i + 1) for i in range(gx_count - 1)])
        high = lax.ppermute(slab[:STEPS], "gx", [(i + 1, i) for i in range(gx_count - 1)])
        padded = jnp.concatenate([low, slab, high], 0)
        fields = (lax.dynamic_slice_in_dim(padded, lax.axis_index("sec") * rows, wide, axis=0),)
    flat = basis_in.reshape(-1, count)
    rows_total = flat.shape[0] * gx_count * sec_count
    inflow, inner_uu = prepare(well_cells, well_rate, flat, wide, total_y, lanes)
    snaps, keep, give, fin, send = flux(
        fields, perm_table, inflow, inner_uu, flat.reshape(-1, lanes, count), along
    )
    mine, others, received = all_sum(keep, give, send if fast else None)
    if fast:
        state_out = unpack((fin, received))
        state_out, mine = lax.optimization_barrier((state_out, mine))
    else:
        moved = lax.all_to_all(fin, "sec", split_axis=1, concat_axis=0, tiled=True)
        state_out = unpack((moved.reshape(across, along, members, lanes),))
    fresh, sigma = small(mine, others, singular, snaps, flat, rows_total)
    return state_out, fresh.reshape(basis_in.shape), sigma


def solution(mesh):
    return jax.shard_map(
        body,
        mesh=mesh,
        in_specs=(
            P(None, "gx", "sec", None),
            P("gx", "sec"),
            P(),
            P(),
            P(),
            P(("gx", "sec"), None, None, None),
            P(),
        ),
        out_specs=(P(None, "gx", "sec", None), P(("gx", "sec"), None, None, None), P()),
        check_vma=False,
    )
```

```python
import functools

import jax
import jax.numpy as jnp
from jax import lax
from jax.experimental import pallas as pl
from jax.experimental.pallas import tpu as pltpu
from jax.sharding import PartitionSpec as P

MG = 8
STEPS = 4
GROUPS = 2

DT_PRESSURE = 0.12
DT_SATURATION = 0.06
DT_ADVECT = 0.15
HIGHEST = lax.Precision.HIGHEST
AXES = ("gx", "sec")
VMEM_LIMIT = 48 * 2**20


def place(wide_rows):
    sec_count = lax.axis_size("sec")
    rows = wide_rows - 2 * STEPS
    first = (lax.axis_index("gx") * sec_count + lax.axis_index("sec")) * rows - STEPS
    return first, rows * sec_count * lax.axis_size("gx")


def pack_kernel(state_ref, rock_ref, own, packed, rock_rows):
    across, entries, members, lanes = packed.shape
    along = entries - 1
    layers = lanes // 2
    group = members // 2
    stride = across * along
    left_lanes = lax.broadcasted_iota(jnp.int32, (group, lanes), 1) < layers
    rock_rows[...] = jnp.zeros_like(rock_rows)
    for y in range(along):
        chunk = rock_ref[:, y * layers : (y + 1) * layers].astype(jnp.float32)
        rock_rows[pl.ds(y, across, stride=members), :] = jnp.concatenate([chunk, chunk], 1)
    for x in range(across):
        for y in range(along):
            at = x * along + y
            low = state_ref[pl.ds(at, group, stride=stride), :]
            high = state_ref[pl.ds(at + group * stride, group, stride=stride), :]
            column = jnp.concatenate(halves_swap(low, high, left_lanes, layers), 0)
            own[x, y] = column
            packed[x, y] = column.astype(jnp.bfloat16)
        packed[x, along] = rock_rows[x * members : (x + 1) * members].astype(jnp.bfloat16)


def pack(state_init, rock_type):
    members, across, along, lanes = state_init.shape
    shape = (along + 1, members, lanes)
    outs = [
        jax.ShapeDtypeStruct((across, along, members, lanes), jnp.float32),
        jax.ShapeDtypeStruct((across,) + shape, jnp.bfloat16),
    ]

    def kernel(state_hbm, rock_hbm, *refs):
        own, packed = refs[:2]
        rock_rows, state_ref, rock_ref, state_sem, rock_sem = refs[-5:]
        state_copy = pltpu.make_async_copy(state_hbm, state_ref, state_sem)
        rock_copy = pltpu.make_async_copy(rock_hbm, rock_ref, rock_sem)
        state_copy.start()
        rock_copy.start()
        rock_copy.wait()
        state_copy.wait()
        pack_kernel(state_ref, rock_ref, own, packed, rock_rows)

    return pl.pallas_call(
        kernel,
        out_shape=outs,
        in_specs=[pl.BlockSpec(memory_space=pl.ANY)] * 2,
        scratch_shapes=[
            pltpu.VMEM((across * members, lanes), jnp.float32),
            pltpu.VMEM((members * across * along, lanes), jnp.float32),
            pltpu.VMEM(rock_type.shape, jnp.int32),
            pltpu.SemaphoreType.DMA,
            pltpu.SemaphoreType.DMA,
        ],
        compiler_params=pltpu.CompilerParams(vmem_limit_bytes=VMEM_LIMIT),
    )(state_init.reshape(-1, lanes), rock_type)


def split_kernel(packed, outward, inward):
    half = packed.shape[0] // 2
    sec = lax.axis_index("sec")
    outward[...] = packed[pl.ds((1 - sec) * half, half)]
    inward[...] = packed[pl.ds(sec * half, half)]


def split(packed):
    half = jax.ShapeDtypeStruct((packed.shape[0] // 2,) + packed.shape[1:], packed.dtype)
    return pl.pallas_call(
        split_kernel, out_shape=(half, half), compiler_params=pltpu.CompilerParams(vmem_limit_bytes=VMEM_LIMIT)
    )(packed)


def inflow_rows(cell_row, rate_ref, out_ref, wide, total_y):
    columns = wide * total_y
    members, wells = rate_ref.shape
    group = members // 2
    lanes = out_ref.shape[1]
    layers = lanes // 2
    first, _ = place(wide)
    start = first * total_y
    row = lax.broadcasted_iota(jnp.int32, (columns, wells), 0)
    near = lax.div(cell_row[...], layers) - start
    picks = jnp.where(row == near, 1.0, 0.0).astype(jnp.bfloat16)
    layer = lax.rem(jnp.broadcast_to(cell_row[...], (lanes, wells)).T, layers)
    lane = lax.broadcasted_iota(jnp.int32, (wells, lanes), 1)
    left_lanes = lane < layers
    at = jnp.where(left_lanes, lane, lane - layers) == layer
    short = jnp.zeros((lanes - members, wells), jnp.float32)
    rate = (jnp.concatenate([rate_ref[...], short], 0) * DT_PRESSURE).T
    for m in range(group):
        value = jnp.where(left_lanes, rate[:, m : m + 1], rate[:, m + group : m + group + 1])
        value = jnp.where(at, value, 0.0)
        sums = [jnp.dot(picks, t, preferred_element_type=jnp.float32) for t in terms(value)]
        out_ref[pl.ds(m, columns, stride=group), :] = (sums[2] + sums[1]) + sums[0]


def before_flux(well_cells, well_rate, perm_table, wide, total_y, lanes):
    members, wells = well_rate.shape

    def kernel(cell_row, rate_ref, table_ref, out_ref, table_out):
        inflow_rows(cell_row, rate_ref, out_ref, wide, total_y)
        for d in range(table_ref.shape[0]):
            for r in range(table_ref.shape[1]):
                table_out[d, r : r + 1, :] = jnp.full((1, lanes), table_ref[d, r], jnp.float32)

    inflow, table = pl.pallas_call(
        kernel,
        out_shape=(
            jax.ShapeDtypeStruct((wide * total_y * members // 2, lanes), jnp.float32),
            jax.ShapeDtypeStruct(perm_table.shape + (lanes,), jnp.float32),
        ),
        in_specs=[pl.BlockSpec(memory_space=pltpu.VMEM)] * 2 + [pl.BlockSpec(memory_space=pltpu.SMEM)],
        compiler_params=pltpu.CompilerParams(vmem_limit_bytes=VMEM_LIMIT),
    )(well_cells.reshape(1, wells), well_rate, perm_table)
    return inflow.reshape(wide, total_y, members // 2, lanes), table


def roll(value, shift):
    return pltpu.roll(value, shift, 1)


def halves_swap(low, high, left_lanes, layers):
    return (
        jnp.where(left_lanes, low, roll(high, layers)),
        jnp.where(left_lanes, roll(low, layers), high),
    )


def harmonic(left, right):
    total = left + right
    return jnp.where(total > 0.0, 2.0 * left * right / jnp.where(total > 0.0, total, 1.0), 0.0)


def face(w12, w06, p, s, p_next, s_next):
    push = w12 * (p_next - p)
    carried = push * jnp.where(push > 0.0, s_next, s)
    return push, w06 * (s_next - s) + (DT_ADVECT / DT_PRESSURE) * carried


def flux_kernel(fast, *refs):
    if fast:
        own_ref, packed, other, beside, cross = refs[:5]
        refs = refs[5:]
    else:
        slab = refs[0]
        refs = refs[1:]
    table, inflow, basis_hbm, snaps, keep, give, fin, send = refs[:8]
    press_a, sat_a, press_b, sat_b, rock, perm, w12, w06, carry, history, sums, inner_uu, basis, sems = refs[8:]
    wide, total_y = inflow.shape[:2]
    group, lanes = inflow.shape[2:]
    layers = lanes // 2
    blocks, along = rock.shape[1:3]
    rows = wide - 2 * STEPS
    parts = sems.shape[0]
    cells = rows * total_y
    copies = [
        pltpu.make_async_copy(
            basis_hbm.at[pl.ds(i * (cells // parts), cells // parts)],
            basis.at[pl.ds(i * (cells // parts), cells // parts)],
            sems.at[i],
        )
        for i in range(parts)
    ]
    for copy in copies:
        copy.start()
    lane = lax.broadcasted_iota(jnp.int32, (group, lanes), 1)
    left_lanes = lane < layers
    lane_y = lax.broadcasted_iota(jnp.int32, (along, lanes), 1)
    sec = lax.axis_index("sec")

    def put_packed(ref, count, x_at, block):
        def row(x, c):
            for y in range(along):
                value = ref[x, y].astype(jnp.float32)
                press_a[x_at + x, block * along + y] = value[:group]
                sat_a[x_at + x, block * along + y] = value[group:]
            rock[x_at + x, block] = ref[x, along].astype(jnp.float32)[:along]
            return c

        lax.fori_loop(0, count, row, 0)

    if fast:
        across = packed.shape[0]
        here, there = (1 - sec) * STEPS, sec * across

        def own(x, c):
            for y in range(along):
                press_a[here + x, sec * along + y] = own_ref[x, y, :group]
                sat_a[here + x, sec * along + y] = own_ref[x, y, group:]
            rock[here + x, sec] = packed[x, along].astype(jnp.float32)[:along]
            return c

        lax.fori_loop(0, across, own, 0)
        put_packed(other, across, here, 1 - sec)
        put_packed(beside, STEPS, there, sec)
        put_packed(cross, STEPS, there, 1 - sec)
    else:
        for block in range(blocks):
            put_packed(slab.at[:, block], wide, 0, block)
    zero = jnp.zeros((group, lanes), jnp.float32)
    for x in range(wide):
        for ref in (press_a, sat_a, press_b, sat_b):
            ref[x, total_y] = zero

    first, total_x = place(wide)

    def look_up(x, c):
        inside = ((first + x >= 0) & (first + x < total_x)).astype(jnp.float32)
        for block in range(blocks):
            kind = rock[x, block]
            values = [jnp.zeros((along, lanes), jnp.float32)] * 3
            for r in range(table.shape[1]):
                here = kind == float(r)
                values = [jnp.where(here, jnp.broadcast_to(table[d, r : r + 1, :], here.shape), values[d]) for d in range(3)]
            for d in range(3):
                perm[d, x, pl.ds(block * along, along), :] = values[d] * inside
        return c

    several(wide, look_up, 4)
    for d in range(3):
        perm[d, wide] = jnp.zeros(perm.shape[2:], jnp.float32)
    perm[1, :, total_y:, :] = jnp.zeros((wide + 1, perm.shape[2] - total_y, lanes), jnp.float32)

    def weigh(x, c):
        for block in range(blocks):
            at = block * along
            here = [perm[d, x, pl.ds(at, along), :] for d in range(3)]
            z_next = jnp.where((lane_y == layers - 1) | (lane_y == lanes - 1), 0.0, roll(here[2], lanes - 1))
            beyond = (perm[0, x + 1, pl.ds(at, along), :], perm[1, x, pl.ds(at + 1, along), :], z_next)
            for d in range(3):
                weight = harmonic(here[d], beyond[d])
                w12[d, x, block] = DT_PRESSURE * weight
                w06[d, x, block] = DT_SATURATION * weight
        return c

    several(wide, weigh, 4)

    def spread(ref, d, x, block, j):
        return jnp.broadcast_to(ref[d, x, block, j : j + 1, :], (group, lanes))

    def x_face(p_ref, s_ref, x, block, j):
        y = block * along + j
        return face(
            spread(w12, 0, x, block, j), spread(w06, 0, x, block, j),
            p_ref[x, y], s_ref[x, y], p_ref[x + 1, y], s_ref[x + 1, y],
        )

    buffers = [(press_a, sat_a), (press_b, sat_b)]
    chunk = along * next(n for n in (2, 1) if blocks % n == 0)
    chunks = total_y // chunk

    def columns(c):
        return [(c * chunk + i, c * (chunk // along) + i // along, i % along) for i in range(chunk)]

    for step in range(STEPS):
        (p_ref, s_ref), (p_new, s_new) = buffers[step % 2], buffers[(step + 1) % 2]

        def begin(c, none):
            for y, block, j in columns(c):
                carry[0, y], carry[1, y] = x_face(p_ref, s_ref, step, block, j)
            return none

        lax.fori_loop(0, chunks, begin, 0)
        span = wide - 2 - 2 * step
        deep = 2 if span % 2 == 0 else 1

        def some_rows(r, none):
            x0 = step + 1 + r * deep

            def one_chunk(c, back):
                back = list(back)
                for y, block, j in columns(c):
                    before = carry[0, y], carry[1, y]
                    for i in range(deep):
                        x = x0 + i
                        p, s = p_ref[x, y], s_ref[x, y]
                        xp, xs = x_face(p_ref, s_ref, x, block, j)
                        yp, ys = face(
                            spread(w12, 1, x, block, j), spread(w06, 1, x, block, j),
                            p, s, p_ref[x, y + 1], s_ref[x, y + 1],
                        )
                        zp, zs = face(
                            spread(w12, 2, x, block, j), spread(w06, 2, x, block, j),
                            p, s, roll(p, lanes - 1), roll(s, lanes - 1),
                        )
                        back_p, back_s = back[2 * i : 2 * i + 2]
                        p_new[x, y] = p + (xp - before[0]) + (yp - back_p) + (zp - roll(zp, 1)) + inflow[x, y]
                        s_new[x, y] = s + (xs - before[1]) + (ys - back_s) + (zs - roll(zs, 1))
                        before = xp, xs
                        back[2 * i : 2 * i + 2] = [yp, ys]
                    carry[0, y], carry[1, y] = before
                return tuple(back)

            lax.fori_loop(0, chunks, one_chunk, (zero,) * (2 * deep))
            return none

        lax.fori_loop(0, span // deep, some_rows, 0)

        def save(x, none):
            def save_chunk(c, none):
                for y, block, j in columns(c):
                    low, high = halves_swap(p_new[STEPS + x, y], s_new[STEPS + x, y], left_lanes, layers)
                    history[x * total_y + y, step * group : (step + 1) * group] = low
                    history[x * total_y + y, (STEPS + step) * group : (STEPS + step + 1) * group] = high
                    if step == STEPS - 1 and not fast:
                        fin[x, block, j] = jnp.concatenate([low, high], 0)
                return none

            return lax.fori_loop(0, chunks, save_chunk, none)

        several(rows, save, 2)

    if fast:
        last = slice((STEPS - 1) * group, STEPS * group)
        past = slice((2 * STEPS - 1) * group, 2 * STEPS * group)
        for ref, block in ((fin, sec), (send, 1 - sec)):
            for x in range(rows):
                for j in range(along):
                    at = x * total_y + block * along + j
                    ref[x, j, :group] = history[at, last]
                    ref[x, j, group:] = history[at, past]

    for copy in copies:
        copy.wait()
    count = basis.shape[2]
    snap_count = 2 * STEPS * group
    run = next(n for n in (16, 8, 4, 2, 1) if cells % n == 0)
    inner_su = jnp.zeros((snap_count, count), jnp.float32)
    inner_ss = jnp.zeros((snap_count, snap_count), jnp.float32)
    inner_uu[...] = jnp.zeros_like(inner_uu)
    for q in range(0, cells, run):
        rows_q = basis[q : q + run].reshape(run * lanes, count)
        inner_uu[...] += lax.dot_general(rows_q, rows_q, (((0,), (0,)), ((), ())), preferred_element_type=jnp.float32)
        part = [history[q + i].astype(jnp.bfloat16) for i in range(run)]
        for i in range(run):
            snaps[q + i] = part[i]
        both = jnp.concatenate(part, 1)
        inner_su += jnp.dot(both, basis[q : q + run].reshape(run * lanes, count), preferred_element_type=jnp.float32)
        inner_ss += lax.dot_general(both, both, (((1,), (1,)), ((), ())), preferred_element_type=jnp.float32)
    fold(sums, inner_uu, inner_su, inner_ss)
    half = sums.shape[0] // 2
    core = lax.rem(lax.axis_index("gx"), 2)
    keep[...] = sums[pl.ds(pl.multiple_of(core * half, 8), half), :]
    give[...] = sums[pl.ds(pl.multiple_of((1 - core) * half, 8), half), :]


def several(total, one, most):
    deep = next(n for n in range(most, 0, -1) if total % n == 0)

    def some(r, none):
        for i in range(deep):
            one(r * deep + i, 0)
        return none

    lax.fori_loop(0, total // deep, some, 0)


def folded_rows(count, snap_count):
    used = count + snap_count * (count // LANE) + snap_count // 2 + 1
    return -(-used // 16) * 16


def lower_mask(side):
    row = lax.broadcasted_iota(jnp.int32, (side, side), 0)
    column = lax.broadcasted_iota(jnp.int32, (side, side), 1)
    return row > column, row == column


def fold(sums, inner_uu, inner_su, inner_ss):
    below, on = lower_mask(LANE)
    first = inner_uu[:LANE, :LANE]
    sums[:LANE] = jnp.where(below, first, inner_uu[LANE:, LANE:])
    sums[LANE : 2 * LANE] = inner_uu[LANE:, :LANE]
    snap_count = inner_su.shape[0]
    at = 2 * LANE
    for tile in range(2):
        sums[at : at + snap_count] = inner_su[:, tile * LANE : (tile + 1) * LANE]
        at += snap_count
    half = snap_count // 2
    sums[at : at + half] = jnp.concatenate([inner_ss[:half], inner_ss[half:]], 1)
    at += half
    diagonal = jnp.sum(jnp.where(on, first, 0.0), axis=0, keepdims=True)
    left = sums.shape[0] - at
    sums[at:] = jnp.broadcast_to(diagonal, (left, LANE))


def unfold(sums, grams, snap_count, scale):
    count = 2 * LANE
    below, on = lower_mask(LANE)
    mixed = sums[:LANE] * scale
    cross = sums[LANE : 2 * LANE] * scale
    at = count + 2 * snap_count
    half = snap_count // 2
    diagonal = sums[at + half : at + half + 1] * scale
    low = jnp.where(below, mixed, 0.0)
    high = jnp.where(below, 0.0, mixed)
    grams[:LANE, :LANE] = low + low.T + jnp.where(on, jnp.broadcast_to(diagonal, on.shape), 0.0)
    grams[LANE:count, LANE:count] = high + jnp.where(on, 0.0, high).T
    grams[LANE:count, :LANE] = cross
    grams[:LANE, LANE:count] = cross.T
    for tile in range(2):
        part = sums[count + tile * snap_count : count + (tile + 1) * snap_count] * scale
        grams[count : count + snap_count, tile * LANE : (tile + 1) * LANE] = part
        wide = jnp.concatenate([part, jnp.zeros((LANE - snap_count, LANE), jnp.float32)], 0)
        grams[tile * LANE : (tile + 1) * LANE, count:] = wide.T
    folded = sums[at : at + half] * scale
    grams[count : count + half, count : count + snap_count] = folded[:, :snap_count]
    grams[count + half : count + snap_count, count : count + snap_count] = folded[:, snap_count:]


def flux(fields, table, inflow, basis_blocks, along):
    fast = len(fields) > 1
    wide, total_y, group, lanes = inflow.shape
    blocks = total_y // along
    rows = wide - 2 * STEPS
    count = basis_blocks.shape[-1]
    snaps = 2 * STEPS * group
    folded = folded_rows(count, snaps)
    f32 = jnp.float32
    fin = (rows, along, 2 * group, lanes) if fast else (rows, blocks, along, 2 * group, lanes)
    outs = [
        jax.ShapeDtypeStruct((rows * total_y, snaps, lanes), jnp.bfloat16),
        jax.ShapeDtypeStruct((folded // 2, LANE), f32),
        jax.ShapeDtypeStruct((folded // 2, LANE), f32),
        jax.ShapeDtypeStruct(fin, f32),
        jax.ShapeDtypeStruct(fin if fast else (8, lanes), f32),
    ]
    state = pltpu.VMEM((wide, total_y + 1, group, lanes), f32)
    whole = pl.BlockSpec(memory_space=pltpu.VMEM)
    return pl.pallas_call(
        lambda *refs: flux_kernel(fast, *refs),
        out_shape=outs,
        in_specs=[whole] * len(fields)
        + [whole, whole, pl.BlockSpec(memory_space=pl.ANY)],
        scratch_shapes=[
            state, state, state, state,
            pltpu.VMEM((wide, blocks, along, lanes), f32),
            pltpu.VMEM((3, wide + 1, total_y + 8, lanes), f32),
            pltpu.VMEM((3, wide, blocks, along, lanes), f32),
            pltpu.VMEM((3, wide, blocks, along, lanes), f32),
            pltpu.VMEM((2, total_y, group, lanes), f32),
            pltpu.VMEM((rows * total_y, snaps, lanes), f32),
            pltpu.VMEM((folded, LANE), f32),
            pltpu.VMEM((count, count), f32),
            pltpu.VMEM(basis_blocks.shape, jnp.bfloat16),
            pltpu.SemaphoreType.DMA((next(n for n in (4, 2, 1) if rows * total_y % n == 0),)),
        ],
        compiler_params=pltpu.CompilerParams(vmem_limit_bytes=VMEM_LIMIT),
    )(*fields, table, inflow, basis_blocks)


def unpack_kernel(parts, *refs):
    out_ref = refs[-1]
    along = refs[0].shape[1]
    members = refs[0].shape[2]
    stride = out_ref.shape[0] // members
    sec = lax.axis_index("sec")
    for part in range(parts):
        rows = refs[part].shape[0]
        start = 0 if parts == 1 else (sec if part == 0 else 1 - sec) * rows
        for x in range(rows):
            for y in range(along):
                out_ref[pl.ds((start + x) * along + y, members, stride=stride), :] = refs[part][x, y]


def unpack(parts):
    rows, along, members, lanes = parts[0].shape
    across = rows * len(parts)
    out = pl.pallas_call(
        lambda *refs: unpack_kernel(len(parts), *refs),
        out_shape=jax.ShapeDtypeStruct((members * across * along, lanes), jnp.float32),
        compiler_params=pltpu.CompilerParams(vmem_limit_bytes=VMEM_LIMIT),
    )(*parts)
    return out.reshape(members, across, along, lanes)


def all_sum(keep, give, beside=None):
    swapped = None
    counts = [lax.axis_size(axis) for axis in AXES]
    total = counts[0] * counts[1]
    pair = counts[1]
    swap = [(i, i ^ pair) for i in range(total)]
    value = keep + lax.ppermute(give, AXES, swap)
    masks = [1 << b for b in range(total.bit_length() - 1) if 1 << b != pair]
    turned = list(masks)
    for i in range(0, len(masks) - 1, 2):
        turned[i], turned[i + 1] = masks[i + 1], masks[i]
    for hop, (even, odd) in enumerate(zip(masks, turned)):
        value = value + lax.ppermute(value, AXES, [(i, i ^ (odd if i & pair else even)) for i in range(total)])
        if hop == 1 and beside is not None:
            beside, value = lax.optimization_barrier((beside, value))
            swapped = lax.ppermute(beside, "sec", [(0, 1), (1, 0)])
    return value, lax.ppermute(value, AXES, swap), swapped


def to_bf16(value):
    return value.astype(jnp.bfloat16)


def hdot(a, b, left=1, right=0):
    return lax.dot_general(a, b, (((left,), (right,)), ((), ())), precision=HIGHEST, preferred_element_type=jnp.float32)

SUB = 8
PANEL = 32
LANE = 128

def row_of(value, j):
    return jnp.broadcast_to(value[j:j + 1], (SUB, LANE))

def eliminate(panel, column):
    groups = PANEL // SUB
    tiles = panel.shape[1] // LANE
    row = lax.broadcasted_iota(jnp.int32, (SUB, LANE), 0)
    strip = [[panel[h * SUB:(h + 1) * SUB, t * LANE:(t + 1) * LANE] for t in range(tiles)] for h in range(groups)]
    spread = {}

    def expand(g, first_group):
        for h in range(first_group, groups):
            for j in range(g * SUB, (g + 1) * SUB):
                tile, lane = (column + j) // LANE, (column + j) % LANE
                spread[h, j] = jnp.broadcast_to(strip[h][tile][:, lane:lane + 1], (SUB, LANE))

    expand(0, 0)
    for g in range(groups):
        if g + 1 < groups:
            expand(g + 1, g)
        scale = jnp.zeros((SUB, LANE), jnp.float32)
        for j in range(0, SUB, 2):
            left, right = spread[g, g * SUB + j], spread[g, g * SUB + j + 1]
            a, b, c = row_of(left, j), row_of(right, j), row_of(right, j + 1)
            det = a * c - b * b
            inv_a, inv_det = 1.0 / a, 1.0 / det
            slope = b * inv_a
            second = a * inv_det
            scale = jnp.where(row == j, a, jnp.where(row == j + 1, det * inv_a, scale))
            one, two = {}, {}
            for h in range(g, groups):
                one[h] = spread[h, g * SUB + j] * inv_a
                two[h] = (spread[h, g * SUB + j + 1] - one[h] * b) * second
            one[g] = jnp.where(row > j, one[g], 0.0)
            two[g] = jnp.where(row > j + 1, two[g], 0.0)
            for k in range(g * SUB + j + 2, min(g + 2, groups) * SUB):
                first = row_of(spread[g, k], j)
                next_ = row_of(spread[g, k], j + 1) - slope * first
                for h in range(g, groups):
                    spread[h, k] = spread[h, k] - one[h] * first - two[h] * next_
            for t in range(tiles):
                first = row_of(strip[g][t], j)
                next_ = row_of(strip[g][t], j + 1) - slope * first
                for h in range(g, groups):
                    strip[h][t] = strip[h][t] - one[h] * first - two[h] * next_
        root = lax.rsqrt(scale)
        for t in range(tiles):
            strip[g][t] = strip[g][t] * root
    return jnp.concatenate([jnp.concatenate(s, 1) for s in strip], 0)

def terms(value):
    high = value.astype(jnp.bfloat16)
    rest = value - high.astype(jnp.float32)
    middle = rest.astype(jnp.bfloat16)
    return high, middle, (rest - middle.astype(jnp.float32)).astype(jnp.bfloat16)

def left_stack(t):
    return jnp.concatenate([t[0], t[0], t[1], t[1], t[0], t[2]], 0)

def right_stack(t):
    return jnp.concatenate([t[0], t[1], t[0], t[1], t[2], t[0]], 0)

def stacked_dot(left, right):
    return lax.dot_general(left, right, (((0,), (0,)), ((), ())), preferred_element_type=jnp.float32)

def tdot(a, b):
    return stacked_dot(left_stack(terms(a)), right_stack(terms(b)))

def solve(aug, count):
    for start in range(0, count, PANEL):
        first = start // LANE * LANE
        done = eliminate(aug[start:start + PANEL, first:], start - first)
        aug[start:start + PANEL, first:] = done
        rest = start + PANEL
        if rest < count:
            base = rest // LANE * LANE
            parts = terms(done[:, base - first:])
            left, right = left_stack(parts), right_stack(parts)
            change = stacked_dot(left[:, :count - base], right)
            aug[rest:, base:] = aug[rest:, base:] - change[rest - base:]

def small_kernel(
    scale, mine_ref, other_ref, sigma_ref, snaps_hbm, basis_hbm, fresh_hbm, sigma_out,
    aug, sums, gram_ref, weights, snaps_ref, basis, fresh, in_sems, out_sems,
):
    copies = [
        pltpu.make_async_copy(basis_hbm, basis, in_sems.at[0]),
        pltpu.make_async_copy(snaps_hbm, snaps_ref, in_sems.at[1]),
    ]
    for copy in copies:
        copy.start()
    count = sigma_ref.shape[1]
    snaps = (gram_ref.shape[0] - count) // 2
    half = sums.shape[0] // 2
    core = lax.rem(lax.axis_index("gx"), 2)
    sums[pl.ds(pl.multiple_of(core * half, 8), half), :] = mine_ref[...]
    sums[pl.ds(pl.multiple_of((1 - core) * half, 8), half), :] = other_ref[...]
    unfold(sums, gram_ref, 2 * snaps, scale)
    eye = lax.broadcasted_iota(jnp.int32, (count, count), 0) == lax.broadcasted_iota(jnp.int32, (count, count), 1)
    pad = LANE - snaps
    sig2 = sigma_ref[...] * sigma_ref[...]
    prior = None
    for group in range(2):
        rows = gram_ref[count + group * snaps: count + (group + 1) * snaps]
        if group == 0:
            coeffs = rows[:, :count]
            own = rows[:, count:count + snaps]
        else:
            reach = count + snaps
            coeffs = hdot(rows[:, :reach], prior[:, :reach], 1, 1)
            own = rows[:, reach:reach + snaps]
        rounded = coeffs.astype(jnp.bfloat16).astype(jnp.float32)
        if group == 0:
            mapped = rounded
            known = gram_ref[:count, :count]
        else:
            mapped = hdot(rounded, prior[:, :reach])
            known = gram_ref[:reach, :reach]
        spread = hdot(mapped, known)
        gram = own - hdot(rounded, coeffs, 1, 1) - hdot(coeffs, rounded, 1, 1) + hdot(spread, mapped, 1, 1)
        lead = tdot(coeffs, coeffs) + jnp.where(eye, jnp.broadcast_to(sig2, eye.shape), 0.0)
        inner = hdot(lead, lead) + tdot(coeffs, hdot(gram, coeffs))
        aug[:, :count] = inner
        aug[:, count:2 * count] = lead
        aug[:, 2 * count:] = jnp.concatenate([coeffs, jnp.zeros((pad, count), jnp.float32)], 0).T
        solve(aug, count)
        turned = aug[:, count:2 * count]
        extra = aug[:, 2 * count:2 * count + snaps]
        energy = turned * turned * sig2
        ones = jnp.ones((8, count), jnp.float32)
        low = hdot(turned, coeffs, 1, 1) + hdot(extra, gram)
        sig2 = hdot(ones, energy, 1, 1)[:1] + hdot(ones[:, :snaps], low * low, 1, 1)[:1]
        step = turned.astype(jnp.bfloat16).astype(jnp.float32) - hdot(extra, rounded)
        if group == 0:
            prior = jnp.concatenate([step, aug[:, 2 * count:]], 1)
        else:
            final = hdot(step, prior)
            high = final[:, :count].astype(jnp.bfloat16)
            weights[:count] = high.T
            both = jnp.concatenate([final[:, count:].T[:snaps], aug[:, 2 * count:].T[:snaps]], 0)
            high = both.astype(jnp.bfloat16)
            weights[count:count + 2 * snaps] = high
            weights[count + 2 * snaps:] = (both - high.astype(jnp.float32)).astype(jnp.bfloat16)
    sigma_out[...] = jnp.sqrt(sig2)
    for copy in copies:
        copy.wait()
    renew(weights, snaps_ref, basis, fresh, fresh_hbm, out_sems)


def renew(weights, snaps_ref, basis, fresh, fresh_hbm, out_sems):
    parts = out_sems.shape[0]
    cells, _, lanes = snaps_ref.shape
    run = cells // parts

    def out(i):
        rows = pl.ds(i * run * lanes, run * lanes)
        return pltpu.make_async_copy(fresh.at[rows], fresh_hbm.at[rows], out_sems.at[i])

    def part(i):
        at = i * run * lanes
        flat = basis[pl.ds(at, run * lanes), :]
        turned = []
        for q in range(run):
            one = snaps_ref[i * run + q]
            turned.append(jnp.concatenate([one, one], 0).T)
        value = jnp.dot(
            jnp.concatenate([flat, jnp.concatenate(turned, 0)], 1), weights[...],
            preferred_element_type=jnp.float32,
        )
        fresh[pl.ds(at, run * lanes), :] = value.astype(jnp.bfloat16)
        out(i).start()

    for i in range(parts):
        part(i)
    for i in range(parts):
        out(i).wait()


def small(mine, other, sigma, snaps, flat, rows_total):
    count = sigma.shape[0]
    cells, snap_count, lanes = snaps.shape
    rows = count + snap_count
    parts = next(n for n in (8, 4, 2, 1) if cells % n == 0)
    whole = pl.BlockSpec(memory_space=pltpu.VMEM)
    outside = pl.BlockSpec(memory_space=pl.ANY)
    fresh, sigma_out = pl.pallas_call(
        functools.partial(small_kernel, 1.0 / rows_total),
        out_shape=(
            jax.ShapeDtypeStruct(flat.shape, jnp.bfloat16),
            jax.ShapeDtypeStruct((1, count), jnp.float32),
        ),
        in_specs=[whole, whole, whole, outside, outside],
        out_specs=(outside, whole),
        scratch_shapes=[
            pltpu.VMEM((count, 2 * count + LANE), jnp.float32),
            pltpu.VMEM((2 * mine.shape[0], LANE), jnp.float32),
            pltpu.VMEM((rows, count + LANE), jnp.float32),
            pltpu.VMEM((count + 2 * snap_count, count), jnp.bfloat16),
            pltpu.VMEM(snaps.shape, jnp.bfloat16),
            pltpu.VMEM(flat.shape, jnp.bfloat16),
            pltpu.VMEM(flat.shape, jnp.bfloat16),
            pltpu.SemaphoreType.DMA((2,)),
            pltpu.SemaphoreType.DMA((parts,)),
        ],
        compiler_params=pltpu.CompilerParams(vmem_limit_bytes=VMEM_LIMIT),
        cost_estimate=pl.CostEstimate(flops=2 * 10**10, bytes_accessed=2**20, transcendentals=0),
    )(mine, other, sigma.reshape(1, count), snaps, flat)
    return fresh, sigma_out.reshape(count)


def body(state_init, rock_type, perm_table, well_cells, well_rate, basis_in, singular):
    members, across, along, lanes = state_init.shape
    gx_count = lax.axis_size("gx")
    sec_count = lax.axis_size("sec")
    rows = across // sec_count
    wide = rows + 2 * STEPS
    total_y = along * sec_count
    count = basis_in.shape[-1]
    fast = sec_count == 2 and across == 2 * STEPS
    if fast:
        own, packed = pack(state_init, rock_type)
        outward, inward = split(packed)
        straight, crossed = [], []
        for r in range(gx_count):
            if r > 0:
                straight.append((2 * (r - 1), 2 * r))
                crossed.append((2 * (r - 1) + 1, 2 * r))
            if r < gx_count - 1:
                straight.append((2 * (r + 1) + 1, 2 * r + 1))
                crossed.append((2 * (r + 1), 2 * r + 1))
        other = lax.ppermute(packed, "sec", [(0, 1), (1, 0)])
        cross = lax.ppermute(inward, AXES, crossed)
        beside = lax.ppermute(outward, AXES, straight)
        fields = (own, packed, other, beside, cross)
    else:
        _, packed = pack(state_init, rock_type)
        slab = lax.all_gather(packed, "sec", axis=1)
        low = lax.ppermute(slab[across - STEPS :], "gx", [(i, i + 1) for i in range(gx_count - 1)])
        high = lax.ppermute(slab[:STEPS], "gx", [(i + 1, i) for i in range(gx_count - 1)])
        padded = jnp.concatenate([low, slab, high], 0)
        fields = (lax.dynamic_slice_in_dim(padded, lax.axis_index("sec") * rows, wide, axis=0),)
    flat = basis_in.reshape(-1, count)
    rows_total = flat.shape[0] * gx_count * sec_count
    inflow, table = before_flux(well_cells, well_rate, perm_table, wide, total_y, lanes)
    snaps, keep, give, fin, send = flux(
        fields, table, inflow, flat.reshape(-1, lanes, count), along
    )
    mine, others, received = all_sum(keep, give, send if fast else None)
    if fast:
        state_out = unpack((fin, received))
        state_out, mine = lax.optimization_barrier((state_out, mine))
    else:
        moved = lax.all_to_all(fin, "sec", split_axis=1, concat_axis=0, tiled=True)
        state_out = unpack((moved.reshape(across, along, members, lanes),))
    fresh, sigma = small(mine, others, singular, snaps, flat, rows_total)
    return state_out, fresh.reshape(basis_in.shape), sigma


def solution(mesh):
    return jax.shard_map(
        body,
        mesh=mesh,
        in_specs=(
            P(None, "gx", "sec", None),
            P("gx", "sec"),
            P(),
            P(),
            P(),
            P(("gx", "sec"), None, None, None),
            P(),
        ),
        out_specs=(P(None, "gx", "sec", None), P(("gx", "sec"), None, None, None), P()),
        check_vma=False,
    )
```

```python
import functools

import jax
import jax.numpy as jnp
from jax import lax
from jax.experimental import pallas as pl
from jax.experimental.pallas import tpu as pltpu
from jax.sharding import PartitionSpec as P

MG = 8
STEPS = 4
GROUPS = 2

DT_PRESSURE = 0.12
DT_SATURATION = 0.06
DT_ADVECT = 0.15
HIGHEST = lax.Precision.HIGHEST
AXES = ("gx", "sec")
VMEM_LIMIT = 48 * 2**20


def place(wide_rows):
    sec_count = lax.axis_size("sec")
    rows = wide_rows - 2 * STEPS
    first = (lax.axis_index("gx") * sec_count + lax.axis_index("sec")) * rows - STEPS
    return first, rows * sec_count * lax.axis_size("gx")


def pack_kernel(state_ref, rock_ref, own, packed, rock_rows):
    across, entries, members, lanes = packed.shape
    along = entries - 1
    layers = lanes // 2
    group = members // 2
    stride = across * along
    left_lanes = lax.broadcasted_iota(jnp.int32, (group, lanes), 1) < layers
    rock_rows[...] = jnp.zeros_like(rock_rows)
    for y in range(along):
        chunk = rock_ref[:, y * layers : (y + 1) * layers].astype(jnp.float32)
        rock_rows[pl.ds(y, across, stride=members), :] = jnp.concatenate([chunk, chunk], 1)
    for x in range(across):
        for y in range(along):
            at = x * along + y
            low = state_ref[pl.ds(at, group, stride=stride), :]
            high = state_ref[pl.ds(at + group * stride, group, stride=stride), :]
            column = jnp.concatenate(halves_swap(low, high, left_lanes, layers), 0)
            own[x, y] = column
            packed[x, y] = column.astype(jnp.bfloat16)
        packed[x, along] = rock_rows[x * members : (x + 1) * members].astype(jnp.bfloat16)


def pack(state_init, rock_type):
    members, across, along, lanes = state_init.shape
    shape = (along + 1, members, lanes)
    outs = [
        jax.ShapeDtypeStruct((across, along, members, lanes), jnp.float32),
        jax.ShapeDtypeStruct((across,) + shape, jnp.bfloat16),
    ]

    def kernel(state_hbm, rock_hbm, *refs):
        own, packed = refs[:2]
        rock_rows, state_ref, rock_ref, state_sem, rock_sem = refs[-5:]
        state_copy = pltpu.make_async_copy(state_hbm, state_ref, state_sem)
        rock_copy = pltpu.make_async_copy(rock_hbm, rock_ref, rock_sem)
        state_copy.start()
        rock_copy.start()
        rock_copy.wait()
        state_copy.wait()
        pack_kernel(state_ref, rock_ref, own, packed, rock_rows)

    return pl.pallas_call(
        kernel,
        out_shape=outs,
        in_specs=[pl.BlockSpec(memory_space=pl.ANY)] * 2,
        scratch_shapes=[
            pltpu.VMEM((across * members, lanes), jnp.float32),
            pltpu.VMEM((members * across * along, lanes), jnp.float32),
            pltpu.VMEM(rock_type.shape, jnp.int32),
            pltpu.SemaphoreType.DMA,
            pltpu.SemaphoreType.DMA,
        ],
        compiler_params=pltpu.CompilerParams(vmem_limit_bytes=VMEM_LIMIT),
    )(state_init.reshape(-1, lanes), rock_type)


def split_kernel(packed, outward, inward):
    half = packed.shape[0] // 2
    sec = lax.axis_index("sec")
    outward[...] = packed[pl.ds((1 - sec) * half, half)]
    inward[...] = packed[pl.ds(sec * half, half)]


def split(packed):
    half = jax.ShapeDtypeStruct((packed.shape[0] // 2,) + packed.shape[1:], packed.dtype)
    return pl.pallas_call(
        split_kernel, out_shape=(half, half), compiler_params=pltpu.CompilerParams(vmem_limit_bytes=VMEM_LIMIT)
    )(packed)


def inflow_rows(cell_row, rate_ref, out_ref, wide, total_y):
    columns = wide * total_y
    members, wells = rate_ref.shape
    group = members // 2
    lanes = out_ref.shape[1]
    layers = lanes // 2
    first, _ = place(wide)
    start = first * total_y
    row = lax.broadcasted_iota(jnp.int32, (columns, wells), 0)
    near = lax.div(cell_row[...], layers) - start
    picks = jnp.where(row == near, 1.0, 0.0).astype(jnp.bfloat16)
    layer = lax.rem(jnp.broadcast_to(cell_row[...], (lanes, wells)).T, layers)
    lane = lax.broadcasted_iota(jnp.int32, (wells, lanes), 1)
    left_lanes = lane < layers
    at = jnp.where(left_lanes, lane, lane - layers) == layer
    short = jnp.zeros((lanes - members, wells), jnp.float32)
    rate = (jnp.concatenate([rate_ref[...], short], 0) * DT_PRESSURE).T
    for m in range(group):
        value = jnp.where(left_lanes, rate[:, m : m + 1], rate[:, m + group : m + group + 1])
        value = jnp.where(at, value, 0.0)
        sums = [jnp.dot(picks, t, preferred_element_type=jnp.float32) for t in terms(value)]
        out_ref[pl.ds(m, columns, stride=group), :] = (sums[2] + sums[1]) + sums[0]


def before_flux(well_cells, well_rate, perm_table, wide, total_y, lanes):
    members, wells = well_rate.shape

    def kernel(cell_row, rate_ref, table_ref, out_ref, table_out):
        inflow_rows(cell_row, rate_ref, out_ref, wide, total_y)
        for d in range(table_ref.shape[0]):
            for r in range(table_ref.shape[1]):
                table_out[d, r : r + 1, :] = jnp.full((1, lanes), table_ref[d, r], jnp.float32)

    inflow, table = pl.pallas_call(
        kernel,
        out_shape=(
            jax.ShapeDtypeStruct((wide * total_y * members // 2, lanes), jnp.float32),
            jax.ShapeDtypeStruct(perm_table.shape + (lanes,), jnp.float32),
        ),
        in_specs=[pl.BlockSpec(memory_space=pltpu.VMEM)] * 2 + [pl.BlockSpec(memory_space=pltpu.SMEM)],
        compiler_params=pltpu.CompilerParams(vmem_limit_bytes=VMEM_LIMIT),
    )(well_cells.reshape(1, wells), well_rate, perm_table)
    return inflow.reshape(wide, total_y, members // 2, lanes), table


def roll(value, shift):
    return pltpu.roll(value, shift, 1)


def halves_swap(low, high, left_lanes, layers):
    return (
        jnp.where(left_lanes, low, roll(high, layers)),
        jnp.where(left_lanes, roll(low, layers), high),
    )


def harmonic(left, right):
    total = left + right
    return jnp.where(total > 0.0, 2.0 * left * right / jnp.where(total > 0.0, total, 1.0), 0.0)


def face(w12, w06, p, s, p_next, s_next):
    push = w12 * (p_next - p)
    carried = push * jnp.where(push > 0.0, s_next, s)
    return push, w06 * (s_next - s) + (DT_ADVECT / DT_PRESSURE) * carried


def flux_kernel(fast, *refs):
    if fast:
        own_ref, packed, other, beside, cross = refs[:5]
        refs = refs[5:]
    else:
        slab = refs[0]
        refs = refs[1:]
    table, inflow, basis_hbm, snaps, keep, give, fin, send = refs[:8]
    press_a, sat_a, press_b, sat_b, rock, perm, w12, w06, carry, history, sums, inner_uu, basis, sems = refs[8:]
    wide, total_y = inflow.shape[:2]
    group, lanes = inflow.shape[2:]
    layers = lanes // 2
    blocks, along = rock.shape[1:3]
    rows = wide - 2 * STEPS
    parts = sems.shape[0]
    cells = rows * total_y
    copies = [
        pltpu.make_async_copy(
            basis_hbm.at[pl.ds(i * (cells // parts), cells // parts)],
            basis.at[pl.ds(i * (cells // parts), cells // parts)],
            sems.at[i],
        )
        for i in range(parts)
    ]
    for copy in copies:
        copy.start()
    lane = lax.broadcasted_iota(jnp.int32, (group, lanes), 1)
    left_lanes = lane < layers
    lane_y = lax.broadcasted_iota(jnp.int32, (along, lanes), 1)
    sec = lax.axis_index("sec")

    def put_packed(ref, count, x_at, block):
        def row(x, c):
            for y in range(along):
                value = ref[x, y].astype(jnp.float32)
                press_a[x_at + x, block * along + y] = value[:group]
                sat_a[x_at + x, block * along + y] = value[group:]
            rock[x_at + x, block] = ref[x, along].astype(jnp.float32)[:along]
            return c

        lax.fori_loop(0, count, row, 0)

    if fast:
        across = packed.shape[0]
        here, there = (1 - sec) * STEPS, sec * across

        def own(x, c):
            for y in range(along):
                press_a[here + x, sec * along + y] = own_ref[x, y, :group]
                sat_a[here + x, sec * along + y] = own_ref[x, y, group:]
            rock[here + x, sec] = packed[x, along].astype(jnp.float32)[:along]
            return c

        lax.fori_loop(0, across, own, 0)
        put_packed(other, across, here, 1 - sec)
        put_packed(beside, STEPS, there, sec)
        put_packed(cross, STEPS, there, 1 - sec)
    else:
        for block in range(blocks):
            put_packed(slab.at[:, block], wide, 0, block)
    zero = jnp.zeros((group, lanes), jnp.float32)
    for x in range(wide):
        for ref in (press_a, sat_a, press_b, sat_b):
            ref[x, total_y] = zero

    first, total_x = place(wide)

    def look_up(x, c):
        inside = ((first + x >= 0) & (first + x < total_x)).astype(jnp.float32)
        for block in range(blocks):
            kind = rock[x, block]
            values = [jnp.zeros((along, lanes), jnp.float32)] * 3
            for r in range(table.shape[1]):
                here = kind == float(r)
                values = [jnp.where(here, jnp.broadcast_to(table[d, r : r + 1, :], here.shape), values[d]) for d in range(3)]
            for d in range(3):
                perm[d, x, pl.ds(block * along, along), :] = values[d] * inside
        return c

    several(wide, look_up, 4)
    for d in range(3):
        perm[d, wide] = jnp.zeros(perm.shape[2:], jnp.float32)
    perm[1, :, total_y:, :] = jnp.zeros((wide + 1, perm.shape[2] - total_y, lanes), jnp.float32)

    def weigh(x, c):
        for block in range(blocks):
            at = block * along
            here = [perm[d, x, pl.ds(at, along), :] for d in range(3)]
            z_next = jnp.where((lane_y == layers - 1) | (lane_y == lanes - 1), 0.0, roll(here[2], lanes - 1))
            beyond = (perm[0, x + 1, pl.ds(at, along), :], perm[1, x, pl.ds(at + 1, along), :], z_next)
            for d in range(3):
                weight = harmonic(here[d], beyond[d])
                w12[d, x, block] = DT_PRESSURE * weight
                w06[d, x, block] = DT_SATURATION * weight
        return c

    several(wide, weigh, 4)

    def spread(ref, d, x, block, j):
        return jnp.broadcast_to(ref[d, x, block, j : j + 1, :], (group, lanes))

    def x_face(p_ref, s_ref, x, block, j):
        y = block * along + j
        return face(
            spread(w12, 0, x, block, j), spread(w06, 0, x, block, j),
            p_ref[x, y], s_ref[x, y], p_ref[x + 1, y], s_ref[x + 1, y],
        )

    buffers = [(press_a, sat_a), (press_b, sat_b)]
    chunk = along * next(n for n in (2, 1) if blocks % n == 0)
    chunks = total_y // chunk

    def columns(c):
        return [(c * chunk + i, c * (chunk // along) + i // along, i % along) for i in range(chunk)]

    for step in range(STEPS):
        (p_ref, s_ref), (p_new, s_new) = buffers[step % 2], buffers[(step + 1) % 2]

        def begin(c, none):
            for y, block, j in columns(c):
                carry[0, y], carry[1, y] = x_face(p_ref, s_ref, step, block, j)
            return none

        lax.fori_loop(0, chunks, begin, 0)
        span = wide - 2 - 2 * step
        deep = 2 if span % 2 == 0 else 1

        def some_rows(r, none):
            x0 = step + 1 + r * deep

            def one_chunk(c, back):
                back = list(back)
                for y, block, j in columns(c):
                    before = carry[0, y], carry[1, y]
                    for i in range(deep):
                        x = x0 + i
                        p, s = p_ref[x, y], s_ref[x, y]
                        xp, xs = x_face(p_ref, s_ref, x, block, j)
                        yp, ys = face(
                            spread(w12, 1, x, block, j), spread(w06, 1, x, block, j),
                            p, s, p_ref[x, y + 1], s_ref[x, y + 1],
                        )
                        zp, zs = face(
                            spread(w12, 2, x, block, j), spread(w06, 2, x, block, j),
                            p, s, roll(p, lanes - 1), roll(s, lanes - 1),
                        )
                        back_p, back_s = back[2 * i : 2 * i + 2]
                        p_new[x, y] = p + (xp - before[0]) + (yp - back_p) + (zp - roll(zp, 1)) + inflow[x, y]
                        s_new[x, y] = s + (xs - before[1]) + (ys - back_s) + (zs - roll(zs, 1))
                        before = xp, xs
                        back[2 * i : 2 * i + 2] = [yp, ys]
                    carry[0, y], carry[1, y] = before
                return tuple(back)

            lax.fori_loop(0, chunks, one_chunk, (zero,) * (2 * deep))
            return none

        lax.fori_loop(0, span // deep, some_rows, 0)

        def save(x, none):
            def save_chunk(c, none):
                for y, block, j in columns(c):
                    low, high = halves_swap(p_new[STEPS + x, y], s_new[STEPS + x, y], left_lanes, layers)
                    history[x * total_y + y, step * group : (step + 1) * group] = low
                    history[x * total_y + y, (STEPS + step) * group : (STEPS + step + 1) * group] = high
                    if step == STEPS - 1 and not fast:
                        fin[x, block, j] = jnp.concatenate([low, high], 0)
                return none

            return lax.fori_loop(0, chunks, save_chunk, none)

        several(rows, save, 2)

    if fast:
        last = slice((STEPS - 1) * group, STEPS * group)
        past = slice((2 * STEPS - 1) * group, 2 * STEPS * group)
        for ref, block in ((fin, sec), (send, 1 - sec)):
            for x in range(rows):
                for j in range(along):
                    at = x * total_y + block * along + j
                    ref[x, j, :group] = history[at, last]
                    ref[x, j, group:] = history[at, past]

    for copy in copies:
        copy.wait()
    count = basis.shape[2]
    snap_count = 2 * STEPS * group
    run = next(n for n in (16, 8, 4, 2, 1) if cells % n == 0)
    inner_su = jnp.zeros((snap_count, count), jnp.float32)
    inner_ss = jnp.zeros((snap_count, snap_count), jnp.float32)
    inner_uu[...] = jnp.zeros_like(inner_uu)
    for q in range(0, cells, run):
        rows_q = basis[q : q + run].reshape(run * lanes, count)
        inner_uu[...] += lax.dot_general(rows_q, rows_q, (((0,), (0,)), ((), ())), preferred_element_type=jnp.float32)
        part = [history[q + i].astype(jnp.bfloat16) for i in range(run)]
        for i in range(run):
            snaps[q + i] = part[i]
        both = jnp.concatenate(part, 1)
        inner_su += jnp.dot(both, basis[q : q + run].reshape(run * lanes, count), preferred_element_type=jnp.float32)
        inner_ss += lax.dot_general(both, both, (((1,), (1,)), ((), ())), preferred_element_type=jnp.float32)
    fold(sums, inner_uu, inner_su, inner_ss)
    half = sums.shape[0] // 2
    core = lax.rem(lax.axis_index("gx"), 2)
    keep[...] = sums[pl.ds(pl.multiple_of(core * half, 8), half), :]
    give[...] = sums[pl.ds(pl.multiple_of((1 - core) * half, 8), half), :]


def several(total, one, most):
    deep = next(n for n in range(most, 0, -1) if total % n == 0)

    def some(r, none):
        for i in range(deep):
            one(r * deep + i, 0)
        return none

    lax.fori_loop(0, total // deep, some, 0)


def folded_rows(count, snap_count):
    used = count + snap_count * (count // LANE) + snap_count // 2 + 1
    return -(-used // 16) * 16


def lower_mask(side):
    row = lax.broadcasted_iota(jnp.int32, (side, side), 0)
    column = lax.broadcasted_iota(jnp.int32, (side, side), 1)
    return row > column, row == column


def fold(sums, inner_uu, inner_su, inner_ss):
    below, on = lower_mask(LANE)
    first = inner_uu[:LANE, :LANE]
    sums[:LANE] = jnp.where(below, first, inner_uu[LANE:, LANE:])
    sums[LANE : 2 * LANE] = inner_uu[LANE:, :LANE]
    snap_count = inner_su.shape[0]
    at = 2 * LANE
    for tile in range(2):
        sums[at : at + snap_count] = inner_su[:, tile * LANE : (tile + 1) * LANE]
        at += snap_count
    half = snap_count // 2
    sums[at : at + half] = jnp.concatenate([inner_ss[:half], inner_ss[half:]], 1)
    at += half
    diagonal = jnp.sum(jnp.where(on, first, 0.0), axis=0, keepdims=True)
    left = sums.shape[0] - at
    sums[at:] = jnp.broadcast_to(diagonal, (left, LANE))


def unfold(sums, grams, snap_count, scale):
    count = 2 * LANE
    below, on = lower_mask(LANE)
    mixed = sums[:LANE] * scale
    cross = sums[LANE : 2 * LANE] * scale
    at = count + 2 * snap_count
    half = snap_count // 2
    diagonal = sums[at + half : at + half + 1] * scale
    low = jnp.where(below, mixed, 0.0)
    high = jnp.where(below, 0.0, mixed)
    grams[:LANE, :LANE] = low + low.T + jnp.where(on, jnp.broadcast_to(diagonal, on.shape), 0.0)
    grams[LANE:count, LANE:count] = high + jnp.where(on, 0.0, high).T
    grams[LANE:count, :LANE] = cross
    grams[:LANE, LANE:count] = cross.T
    for tile in range(2):
        part = sums[count + tile * snap_count : count + (tile + 1) * snap_count] * scale
        grams[count : count + snap_count, tile * LANE : (tile + 1) * LANE] = part
        wide = jnp.concatenate([part, jnp.zeros((LANE - snap_count, LANE), jnp.float32)], 0)
        grams[tile * LANE : (tile + 1) * LANE, count:] = wide.T
    folded = sums[at : at + half] * scale
    grams[count : count + half, count : count + snap_count] = folded[:, :snap_count]
    grams[count + half : count + snap_count, count : count + snap_count] = folded[:, snap_count:]


def flux(fields, table, inflow, basis_blocks, along):
    fast = len(fields) > 1
    wide, total_y, group, lanes = inflow.shape
    blocks = total_y // along
    rows = wide - 2 * STEPS
    count = basis_blocks.shape[-1]
    snaps = 2 * STEPS * group
    folded = folded_rows(count, snaps)
    f32 = jnp.float32
    fin = (rows, along, 2 * group, lanes) if fast else (rows, blocks, along, 2 * group, lanes)
    outs = [
        jax.ShapeDtypeStruct((rows * total_y, snaps, lanes), jnp.bfloat16),
        jax.ShapeDtypeStruct((folded // 2, LANE), f32),
        jax.ShapeDtypeStruct((folded // 2, LANE), f32),
        jax.ShapeDtypeStruct(fin, f32),
        jax.ShapeDtypeStruct(fin if fast else (8, lanes), f32),
    ]
    state = pltpu.VMEM((wide, total_y + 1, group, lanes), f32)
    whole = pl.BlockSpec(memory_space=pltpu.VMEM)
    return pl.pallas_call(
        lambda *refs: flux_kernel(fast, *refs),
        out_shape=outs,
        in_specs=[whole] * len(fields)
        + [whole, whole, pl.BlockSpec(memory_space=pl.ANY)],
        scratch_shapes=[
            state, state, state, state,
            pltpu.VMEM((wide, blocks, along, lanes), f32),
            pltpu.VMEM((3, wide + 1, total_y + 8, lanes), f32),
            pltpu.VMEM((3, wide, blocks, along, lanes), f32),
            pltpu.VMEM((3, wide, blocks, along, lanes), f32),
            pltpu.VMEM((2, total_y, group, lanes), f32),
            pltpu.VMEM((rows * total_y, snaps, lanes), f32),
            pltpu.VMEM((folded, LANE), f32),
            pltpu.VMEM((count, count), f32),
            pltpu.VMEM(basis_blocks.shape, jnp.bfloat16),
            pltpu.SemaphoreType.DMA((next(n for n in (4, 2, 1) if rows * total_y % n == 0),)),
        ],
        compiler_params=pltpu.CompilerParams(vmem_limit_bytes=VMEM_LIMIT),
    )(*fields, table, inflow, basis_blocks)


def unpack_kernel(parts, *refs):
    out_ref = refs[-1]
    along = refs[0].shape[1]
    members = refs[0].shape[2]
    stride = out_ref.shape[0] // members
    sec = lax.axis_index("sec")
    for part in range(parts):
        rows = refs[part].shape[0]
        start = 0 if parts == 1 else (sec if part == 0 else 1 - sec) * rows
        for x in range(rows):
            for y in range(along):
                out_ref[pl.ds((start + x) * along + y, members, stride=stride), :] = refs[part][x, y]


def unpack(parts):
    rows, along, members, lanes = parts[0].shape
    across = rows * len(parts)
    out = pl.pallas_call(
        lambda *refs: unpack_kernel(len(parts), *refs),
        out_shape=jax.ShapeDtypeStruct((members * across * along, lanes), jnp.float32),
        compiler_params=pltpu.CompilerParams(vmem_limit_bytes=VMEM_LIMIT),
    )(*parts)
    return out.reshape(members, across, along, lanes)


def all_sum(keep, give, beside=None):
    swapped = None
    counts = [lax.axis_size(axis) for axis in AXES]
    total = counts[0] * counts[1]
    pair = counts[1]
    swap = [(i, i ^ pair) for i in range(total)]
    value = keep + lax.ppermute(give, AXES, swap)
    masks = [1 << b for b in range(total.bit_length() - 1) if 1 << b != pair]
    turned = list(masks)
    for i in range(0, len(masks) - 1, 2):
        turned[i], turned[i + 1] = masks[i + 1], masks[i]
    for hop, (even, odd) in enumerate(zip(masks, turned)):
        value = value + lax.ppermute(value, AXES, [(i, i ^ (odd if i & pair else even)) for i in range(total)])
        if hop == 1 and beside is not None:
            beside, value = lax.optimization_barrier((beside, value))
            swapped = lax.ppermute(beside, "sec", [(0, 1), (1, 0)])
    return value, lax.ppermute(value, AXES, swap), swapped


def to_bf16(value):
    return value.astype(jnp.bfloat16)


def hdot(a, b, left=1, right=0):
    return lax.dot_general(a, b, (((left,), (right,)), ((), ())), precision=HIGHEST, preferred_element_type=jnp.float32)

SUB = 8
PANEL = 32
LANE = 128

def row_of(value, j):
    return jnp.broadcast_to(value[j:j + 1], (SUB, LANE))

def eliminate(panel, column):
    groups = PANEL // SUB
    tiles = panel.shape[1] // LANE
    row = lax.broadcasted_iota(jnp.int32, (SUB, LANE), 0)
    strip = [[panel[h * SUB:(h + 1) * SUB, t * LANE:(t + 1) * LANE] for t in range(tiles)] for h in range(groups)]
    spread = {}

    def expand(g, first_group):
        for h in range(first_group, groups):
            for j in range(g * SUB, (g + 1) * SUB):
                tile, lane = (column + j) // LANE, (column + j) % LANE
                spread[h, j] = jnp.broadcast_to(strip[h][tile][:, lane:lane + 1], (SUB, LANE))

    expand(0, 0)
    for g in range(groups):
        if g + 1 < groups:
            expand(g + 1, g)
        scale = jnp.zeros((SUB, LANE), jnp.float32)
        for j in range(0, SUB, 2):
            left, right = spread[g, g * SUB + j], spread[g, g * SUB + j + 1]
            a, b, c = row_of(left, j), row_of(right, j), row_of(right, j + 1)
            det = a * c - b * b
            inv_a, inv_det = 1.0 / a, 1.0 / det
            slope = b * inv_a
            second = a * inv_det
            scale = jnp.where(row == j, a, jnp.where(row == j + 1, det * inv_a, scale))
            one, two = {}, {}
            for h in range(g, groups):
                one[h] = spread[h, g * SUB + j] * inv_a
                two[h] = (spread[h, g * SUB + j + 1] - one[h] * b) * second
            one[g] = jnp.where(row > j, one[g], 0.0)
            two[g] = jnp.where(row > j + 1, two[g], 0.0)
            for k in range(g * SUB + j + 2, min(g + 2, groups) * SUB):
                first = row_of(spread[g, k], j)
                next_ = row_of(spread[g, k], j + 1) - slope * first
                for h in range(g, groups):
                    spread[h, k] = spread[h, k] - one[h] * first - two[h] * next_
            for t in range(tiles):
                first = row_of(strip[g][t], j)
                next_ = row_of(strip[g][t], j + 1) - slope * first
                for h in range(g, groups):
                    strip[h][t] = strip[h][t] - one[h] * first - two[h] * next_
        root = lax.rsqrt(scale)
        for t in range(tiles):
            strip[g][t] = strip[g][t] * root
    return jnp.concatenate([jnp.concatenate(s, 1) for s in strip], 0)

def terms(value):
    high = value.astype(jnp.bfloat16)
    rest = value - high.astype(jnp.float32)
    middle = rest.astype(jnp.bfloat16)
    return high, middle, (rest - middle.astype(jnp.float32)).astype(jnp.bfloat16)

def left_stack(t):
    return jnp.concatenate([t[0], t[0], t[1], t[1], t[0], t[2]], 0)

def right_stack(t):
    return jnp.concatenate([t[0], t[1], t[0], t[1], t[2], t[0]], 0)

def stacked_dot(left, right):
    return lax.dot_general(left, right, (((0,), (0,)), ((), ())), preferred_element_type=jnp.float32)

def tdot(a, b):
    return stacked_dot(left_stack(terms(a)), right_stack(terms(b)))

def solve(aug, count):
    for start in range(0, count, PANEL):
        first = start // LANE * LANE
        done = eliminate(aug[start:start + PANEL, first:], start - first)
        aug[start:start + PANEL, first:] = done
        rest = start + PANEL
        if rest < count:
            base = rest // LANE * LANE
            parts = terms(done[:, base - first:])
            left, right = left_stack(parts), right_stack(parts)
            change = stacked_dot(left[:, :count - base], right)
            aug[rest:, base:] = aug[rest:, base:] - change[rest - base:]

def next_squares(turned, extra, coeffs, gram, sig2):
    energy = turned * turned * sig2
    ones = jnp.ones((8, turned.shape[0]), jnp.float32)
    low = hdot(turned, coeffs, 1, 1) + hdot(extra, gram)
    return hdot(ones, energy, 1, 1)[:1] + hdot(ones[:, : low.shape[1]], low * low, 1, 1)[:1]


def small_kernel(
    scale, mine_ref, other_ref, sigma_ref, snaps_hbm, basis_hbm, fresh_hbm, sigma_out,
    aug, sums, gram_ref, weights, snaps_ref, basis, fresh, in_sems, out_sems,
):
    copies = [
        pltpu.make_async_copy(basis_hbm, basis, in_sems.at[0]),
        pltpu.make_async_copy(snaps_hbm, snaps_ref, in_sems.at[1]),
    ]
    for copy in copies:
        copy.start()
    count = sigma_ref.shape[1]
    snaps = (gram_ref.shape[0] - count) // 2
    half = sums.shape[0] // 2
    core = lax.rem(lax.axis_index("gx"), 2)
    sums[pl.ds(pl.multiple_of(core * half, 8), half), :] = mine_ref[...]
    sums[pl.ds(pl.multiple_of((1 - core) * half, 8), half), :] = other_ref[...]
    unfold(sums, gram_ref, 2 * snaps, scale)
    eye = lax.broadcasted_iota(jnp.int32, (count, count), 0) == lax.broadcasted_iota(jnp.int32, (count, count), 1)
    pad = LANE - snaps
    sig2 = sigma_ref[...] * sigma_ref[...]
    prior = None
    for group in range(2):
        rows = gram_ref[count + group * snaps: count + (group + 1) * snaps]
        if group == 0:
            coeffs = rows[:, :count]
            own = rows[:, count:count + snaps]
        else:
            reach = count + snaps
            coeffs = hdot(rows[:, :reach], prior[:, :reach], 1, 1)
            own = rows[:, reach:reach + snaps]
        rounded = coeffs.astype(jnp.bfloat16).astype(jnp.float32)
        if group == 0:
            mapped = rounded
            known = gram_ref[:count, :count]
        else:
            mapped = hdot(rounded, prior[:, :reach])
            known = gram_ref[:reach, :reach]
        spread = hdot(mapped, known)
        gram = own - hdot(rounded, coeffs, 1, 1) - hdot(coeffs, rounded, 1, 1) + hdot(spread, mapped, 1, 1)
        lead = tdot(coeffs, coeffs) + jnp.where(eye, jnp.broadcast_to(sig2, eye.shape), 0.0)
        inner = hdot(lead, lead) + tdot(coeffs, hdot(gram, coeffs))
        aug[:, :count] = inner
        aug[:, count:2 * count] = lead
        aug[:, 2 * count:] = jnp.concatenate([coeffs, jnp.zeros((pad, count), jnp.float32)], 0).T
        solve(aug, count)
        turned = aug[:, count:2 * count]
        extra = aug[:, 2 * count:2 * count + snaps]
        step = turned.astype(jnp.bfloat16).astype(jnp.float32) - hdot(extra, rounded)
        if group == 0:
            sig2 = next_squares(turned, extra, coeffs, gram, sig2)
            prior = jnp.concatenate([step, aug[:, 2 * count:]], 1)
        else:
            final = hdot(step, prior)
            high = final[:, :count].astype(jnp.bfloat16)
            weights[:count] = high.T
            both = jnp.concatenate([final[:, count:].T[:snaps], aug[:, 2 * count:].T[:snaps]], 0)
            high = both.astype(jnp.bfloat16)
            weights[count:count + 2 * snaps] = high
            weights[count + 2 * snaps:] = (both - high.astype(jnp.float32)).astype(jnp.bfloat16)
    for copy in copies:
        copy.wait()
    wait_all = renew(weights, snaps_ref, basis, fresh, fresh_hbm, out_sems)
    sigma_out[...] = jnp.sqrt(next_squares(turned, extra, coeffs, gram, sig2))
    wait_all()


def renew(weights, snaps_ref, basis, fresh, fresh_hbm, out_sems):
    parts = out_sems.shape[0]
    cells, _, lanes = snaps_ref.shape
    run = cells // parts

    def out(i):
        rows = pl.ds(i * run * lanes, run * lanes)
        return pltpu.make_async_copy(fresh.at[rows], fresh_hbm.at[rows], out_sems.at[i])

    def part(i):
        at = i * run * lanes
        flat = basis[pl.ds(at, run * lanes), :]
        turned = []
        for q in range(run):
            one = snaps_ref[i * run + q]
            turned.append(jnp.concatenate([one, one], 0).T)
        value = jnp.dot(
            jnp.concatenate([flat, jnp.concatenate(turned, 0)], 1), weights[...],
            preferred_element_type=jnp.float32,
        )
        fresh[pl.ds(at, run * lanes), :] = value.astype(jnp.bfloat16)
        out(i).start()

    for i in range(parts):
        part(i)

    def wait_all():
        for i in range(parts):
            out(i).wait()

    return wait_all


def small(mine, other, sigma, snaps, flat, rows_total):
    count = sigma.shape[0]
    cells, snap_count, lanes = snaps.shape
    rows = count + snap_count
    parts = next(n for n in (8, 4, 2, 1) if cells % n == 0)
    whole = pl.BlockSpec(memory_space=pltpu.VMEM)
    outside = pl.BlockSpec(memory_space=pl.ANY)
    fresh, sigma_out = pl.pallas_call(
        functools.partial(small_kernel, 1.0 / rows_total),
        out_shape=(
            jax.ShapeDtypeStruct(flat.shape, jnp.bfloat16),
            jax.ShapeDtypeStruct((1, count), jnp.float32),
        ),
        in_specs=[whole, whole, whole, outside, outside],
        out_specs=(outside, whole),
        scratch_shapes=[
            pltpu.VMEM((count, 2 * count + LANE), jnp.float32),
            pltpu.VMEM((2 * mine.shape[0], LANE), jnp.float32),
            pltpu.VMEM((rows, count + LANE), jnp.float32),
            pltpu.VMEM((count + 2 * snap_count, count), jnp.bfloat16),
            pltpu.VMEM(snaps.shape, jnp.bfloat16),
            pltpu.VMEM(flat.shape, jnp.bfloat16),
            pltpu.VMEM(flat.shape, jnp.bfloat16),
            pltpu.SemaphoreType.DMA((2,)),
            pltpu.SemaphoreType.DMA((parts,)),
        ],
        compiler_params=pltpu.CompilerParams(vmem_limit_bytes=VMEM_LIMIT),
        cost_estimate=pl.CostEstimate(flops=2 * 10**10, bytes_accessed=2**20, transcendentals=0),
    )(mine, other, sigma.reshape(1, count), snaps, flat)
    return fresh, sigma_out.reshape(count)


def body(state_init, rock_type, perm_table, well_cells, well_rate, basis_in, singular):
    members, across, along, lanes = state_init.shape
    gx_count = lax.axis_size("gx")
    sec_count = lax.axis_size("sec")
    rows = across // sec_count
    wide = rows + 2 * STEPS
    total_y = along * sec_count
    count = basis_in.shape[-1]
    fast = sec_count == 2 and across == 2 * STEPS
    if fast:
        own, packed = pack(state_init, rock_type)
        outward, inward = split(packed)
        straight, crossed = [], []
        for r in range(gx_count):
            if r > 0:
                straight.append((2 * (r - 1), 2 * r))
                crossed.append((2 * (r - 1) + 1, 2 * r))
            if r < gx_count - 1:
                straight.append((2 * (r + 1) + 1, 2 * r + 1))
                crossed.append((2 * (r + 1), 2 * r + 1))
        other = lax.ppermute(packed, "sec", [(0, 1), (1, 0)])
        cross = lax.ppermute(inward, AXES, crossed)
        beside = lax.ppermute(outward, AXES, straight)
        fields = (own, packed, other, beside, cross)
    else:
        _, packed = pack(state_init, rock_type)
        slab = lax.all_gather(packed, "sec", axis=1)
        low = lax.ppermute(slab[across - STEPS :], "gx", [(i, i + 1) for i in range(gx_count - 1)])
        high = lax.ppermute(slab[:STEPS], "gx", [(i + 1, i) for i in range(gx_count - 1)])
        padded = jnp.concatenate([low, slab, high], 0)
        fields = (lax.dynamic_slice_in_dim(padded, lax.axis_index("sec") * rows, wide, axis=0),)
    flat = basis_in.reshape(-1, count)
    rows_total = flat.shape[0] * gx_count * sec_count
    inflow, table = before_flux(well_cells, well_rate, perm_table, wide, total_y, lanes)
    snaps, keep, give, fin, send = flux(
        fields, table, inflow, flat.reshape(-1, lanes, count), along
    )
    mine, others, received = all_sum(keep, give, send if fast else None)
    if fast:
        state_out = unpack((fin, received))
        state_out, mine = lax.optimization_barrier((state_out, mine))
    else:
        moved = lax.all_to_all(fin, "sec", split_axis=1, concat_axis=0, tiled=True)
        state_out = unpack((moved.reshape(across, along, members, lanes),))
    fresh, sigma = small(mine, others, singular, snaps, flat, rows_total)
    return state_out, fresh.reshape(basis_in.shape), sigma


def solution(mesh):
    return jax.shard_map(
        body,
        mesh=mesh,
        in_specs=(
            P(None, "gx", "sec", None),
            P("gx", "sec"),
            P(),
            P(),
            P(),
            P(("gx", "sec"), None, None, None),
            P(),
        ),
        out_specs=(P(None, "gx", "sec", None), P(("gx", "sec"), None, None, None), P()),
        check_vma=False,
    )
```

```python
import functools

import jax
import jax.numpy as jnp
from jax import lax
from jax.experimental import pallas as pl
from jax.experimental.pallas import tpu as pltpu
from jax.sharding import PartitionSpec as P

MG = 8
STEPS = 4
GROUPS = 2

DT_PRESSURE = 0.12
DT_SATURATION = 0.06
DT_ADVECT = 0.15
HIGHEST = lax.Precision.HIGHEST
AXES = ("gx", "sec")
VMEM_LIMIT = 48 * 2**20


def place(wide_rows):
    sec_count = lax.axis_size("sec")
    rows = wide_rows - 2 * STEPS
    first = (lax.axis_index("gx") * sec_count + lax.axis_index("sec")) * rows - STEPS
    return first, rows * sec_count * lax.axis_size("gx")


def pack_kernel(state_ref, rock_ref, own, packed, rock_rows):
    across, entries, members, lanes = packed.shape
    along = entries - 1
    layers = lanes // 2
    group = members // 2
    stride = across * along
    left_lanes = lax.broadcasted_iota(jnp.int32, (group, lanes), 1) < layers
    rock_rows[...] = jnp.zeros_like(rock_rows)
    for y in range(along):
        chunk = rock_ref[:, y * layers : (y + 1) * layers].astype(jnp.float32)
        rock_rows[pl.ds(y, across, stride=members), :] = jnp.concatenate([chunk, chunk], 1)
    for x in range(across):
        for y in range(along):
            at = x * along + y
            low = state_ref[pl.ds(at, group, stride=stride), :]
            high = state_ref[pl.ds(at + group * stride, group, stride=stride), :]
            column = jnp.concatenate(halves_swap(low, high, left_lanes, layers), 0)
            own[x, y] = column
            packed[x, y] = column.astype(jnp.bfloat16)
        packed[x, along] = rock_rows[x * members : (x + 1) * members].astype(jnp.bfloat16)


def pack(state_init, rock_type):
    members, across, along, lanes = state_init.shape
    shape = (along + 1, members, lanes)
    outs = [
        jax.ShapeDtypeStruct((across, along, members, lanes), jnp.float32),
        jax.ShapeDtypeStruct((across,) + shape, jnp.bfloat16),
    ]

    def kernel(state_hbm, rock_hbm, *refs):
        own, packed = refs[:2]
        rock_rows, state_ref, rock_ref, state_sem, rock_sem = refs[-5:]
        state_copy = pltpu.make_async_copy(state_hbm, state_ref, state_sem)
        rock_copy = pltpu.make_async_copy(rock_hbm, rock_ref, rock_sem)
        state_copy.start()
        rock_copy.start()
        rock_copy.wait()
        state_copy.wait()
        pack_kernel(state_ref, rock_ref, own, packed, rock_rows)

    return pl.pallas_call(
        kernel,
        out_shape=outs,
        in_specs=[pl.BlockSpec(memory_space=pl.ANY)] * 2,
        scratch_shapes=[
            pltpu.VMEM((across * members, lanes), jnp.float32),
            pltpu.VMEM((members * across * along, lanes), jnp.float32),
            pltpu.VMEM(rock_type.shape, jnp.int32),
            pltpu.SemaphoreType.DMA,
            pltpu.SemaphoreType.DMA,
        ],
        compiler_params=pltpu.CompilerParams(vmem_limit_bytes=VMEM_LIMIT),
    )(state_init.reshape(-1, lanes), rock_type)


def split_kernel(packed, outward, inward):
    half = packed.shape[0] // 2
    sec = lax.axis_index("sec")
    outward[...] = packed[pl.ds((1 - sec) * half, half)]
    inward[...] = packed[pl.ds(sec * half, half)]


def split(packed):
    half = jax.ShapeDtypeStruct((packed.shape[0] // 2,) + packed.shape[1:], packed.dtype)
    return pl.pallas_call(
        split_kernel, out_shape=(half, half), compiler_params=pltpu.CompilerParams(vmem_limit_bytes=VMEM_LIMIT)
    )(packed)


def inflow_rows(cell_row, rate_ref, out_ref, wide, total_y):
    columns = wide * total_y
    members, wells = rate_ref.shape
    group = members // 2
    lanes = out_ref.shape[1]
    layers = lanes // 2
    first, _ = place(wide)
    start = first * total_y
    row = lax.broadcasted_iota(jnp.int32, (columns, wells), 0)
    near = lax.div(cell_row[...], layers) - start
    picks = jnp.where(row == near, 1.0, 0.0).astype(jnp.bfloat16)
    layer = lax.rem(jnp.broadcast_to(cell_row[...], (lanes, wells)).T, layers)
    lane = lax.broadcasted_iota(jnp.int32, (wells, lanes), 1)
    left_lanes = lane < layers
    at = jnp.where(left_lanes, lane, lane - layers) == layer
    short = jnp.zeros((lanes - members, wells), jnp.float32)
    rate = (jnp.concatenate([rate_ref[...], short], 0) * DT_PRESSURE).T
    for m in range(group):
        value = jnp.where(left_lanes, rate[:, m : m + 1], rate[:, m + group : m + group + 1])
        value = jnp.where(at, value, 0.0)
        sums = [jnp.dot(picks, t, preferred_element_type=jnp.float32) for t in terms(value)]
        out_ref[pl.ds(m, columns, stride=group), :] = (sums[2] + sums[1]) + sums[0]


def before_flux(well_cells, well_rate, perm_table, wide, total_y, lanes):
    members, wells = well_rate.shape

    def kernel(cell_row, rate_ref, table_ref, out_ref, table_out):
        inflow_rows(cell_row, rate_ref, out_ref, wide, total_y)
        for d in range(table_ref.shape[0]):
            for r in range(table_ref.shape[1]):
                table_out[d, r : r + 1, :] = jnp.full((1, lanes), table_ref[d, r], jnp.float32)

    inflow, table = pl.pallas_call(
        kernel,
        out_shape=(
            jax.ShapeDtypeStruct((wide * total_y * members // 2, lanes), jnp.float32),
            jax.ShapeDtypeStruct(perm_table.shape + (lanes,), jnp.float32),
        ),
        in_specs=[pl.BlockSpec(memory_space=pltpu.VMEM)] * 2 + [pl.BlockSpec(memory_space=pltpu.SMEM)],
        compiler_params=pltpu.CompilerParams(vmem_limit_bytes=VMEM_LIMIT),
    )(well_cells.reshape(1, wells), well_rate, perm_table)
    return inflow.reshape(wide, total_y, members // 2, lanes), table


def roll(value, shift):
    return pltpu.roll(value, shift, 1)


def halves_swap(low, high, left_lanes, layers):
    return (
        jnp.where(left_lanes, low, roll(high, layers)),
        jnp.where(left_lanes, roll(low, layers), high),
    )


def harmonic(left, right):
    total = left + right
    return jnp.where(total > 0.0, 2.0 * left * right / jnp.where(total > 0.0, total, 1.0), 0.0)


def face(w12, w06, p, s, p_next, s_next):
    push = w12 * (p_next - p)
    carried = push * jnp.where(push > 0.0, s_next, s)
    return push, w06 * (s_next - s) + (DT_ADVECT / DT_PRESSURE) * carried


def flux_kernel(fast, *refs):
    if fast:
        own_ref, packed, other, beside, cross = refs[:5]
        refs = refs[5:]
    else:
        slab = refs[0]
        refs = refs[1:]
    table, inflow, basis_hbm, snaps, keep, give, fin, send = refs[:8]
    press_a, sat_a, press_b, sat_b, rock, perm, w12, w06, carry, history, sums, inner_uu, basis, sems = refs[8:]
    wide, total_y = inflow.shape[:2]
    group, lanes = inflow.shape[2:]
    layers = lanes // 2
    blocks, along = rock.shape[1:3]
    rows = wide - 2 * STEPS
    parts = sems.shape[0]
    cells = rows * total_y
    copies = [
        pltpu.make_async_copy(
            basis_hbm.at[pl.ds(i * (cells // parts), cells // parts)],
            basis.at[pl.ds(i * (cells // parts), cells // parts)],
            sems.at[i],
        )
        for i in range(parts)
    ]
    for copy in copies:
        copy.start()
    lane = lax.broadcasted_iota(jnp.int32, (group, lanes), 1)
    left_lanes = lane < layers
    lane_y = lax.broadcasted_iota(jnp.int32, (along, lanes), 1)
    sec = lax.axis_index("sec")

    def put_packed(ref, count, x_at, block):
        def row(x, c):
            for y in range(along):
                value = ref[x, y].astype(jnp.float32)
                press_a[x_at + x, block * along + y] = value[:group]
                sat_a[x_at + x, block * along + y] = value[group:]
            rock[x_at + x, block] = ref[x, along].astype(jnp.float32)[:along]
            return c

        lax.fori_loop(0, count, row, 0)

    if fast:
        across = packed.shape[0]
        here, there = (1 - sec) * STEPS, sec * across

        def own(x, c):
            for y in range(along):
                press_a[here + x, sec * along + y] = own_ref[x, y, :group]
                sat_a[here + x, sec * along + y] = own_ref[x, y, group:]
            rock[here + x, sec] = packed[x, along].astype(jnp.float32)[:along]
            return c

        lax.fori_loop(0, across, own, 0)
        put_packed(other, across, here, 1 - sec)
        put_packed(beside, STEPS, there, sec)
        put_packed(cross, STEPS, there, 1 - sec)
    else:
        for block in range(blocks):
            put_packed(slab.at[:, block], wide, 0, block)
    zero = jnp.zeros((group, lanes), jnp.float32)
    for x in range(wide):
        for ref in (press_a, sat_a, press_b, sat_b):
            ref[x, total_y] = zero

    first, total_x = place(wide)

    def look_up(x, c):
        inside = ((first + x >= 0) & (first + x < total_x)).astype(jnp.float32)
        for block in range(blocks):
            kind = rock[x, block]
            values = [jnp.zeros((along, lanes), jnp.float32)] * 3
            for r in range(table.shape[1]):
                here = kind == float(r)
                values = [jnp.where(here, jnp.broadcast_to(table[d, r : r + 1, :], here.shape), values[d]) for d in range(3)]
            for d in range(3):
                perm[d, x, pl.ds(block * along, along), :] = values[d] * inside
        return c

    several(wide, look_up, 6)
    for d in range(3):
        perm[d, wide] = jnp.zeros(perm.shape[2:], jnp.float32)
    perm[1, :, total_y:, :] = jnp.zeros((wide + 1, perm.shape[2] - total_y, lanes), jnp.float32)

    def weigh(x, c):
        for block in range(blocks):
            at = block * along
            here = [perm[d, x, pl.ds(at, along), :] for d in range(3)]
            z_next = jnp.where((lane_y == layers - 1) | (lane_y == lanes - 1), 0.0, roll(here[2], lanes - 1))
            beyond = (perm[0, x + 1, pl.ds(at, along), :], perm[1, x, pl.ds(at + 1, along), :], z_next)
            for d in range(3):
                weight = harmonic(here[d], beyond[d])
                w12[d, x, block] = DT_PRESSURE * weight
                w06[d, x, block] = DT_SATURATION * weight
        return c

    several(wide, weigh, 6)

    def spread(ref, d, x, block, j):
        return jnp.broadcast_to(ref[d, x, block, j : j + 1, :], (group, lanes))

    def x_face(p_ref, s_ref, x, block, j):
        y = block * along + j
        return face(
            spread(w12, 0, x, block, j), spread(w06, 0, x, block, j),
            p_ref[x, y], s_ref[x, y], p_ref[x + 1, y], s_ref[x + 1, y],
        )

    buffers = [(press_a, sat_a), (press_b, sat_b)]
    chunk = along * next(n for n in (2, 1) if blocks % n == 0)
    chunks = total_y // chunk

    def columns(c):
        return [(c * chunk + i, c * (chunk // along) + i // along, i % along) for i in range(chunk)]

    for step in range(STEPS):
        (p_ref, s_ref), (p_new, s_new) = buffers[step % 2], buffers[(step + 1) % 2]

        def begin(c, none):
            for y, block, j in columns(c):
                carry[0, y], carry[1, y] = x_face(p_ref, s_ref, step, block, j)
            return none

        lax.fori_loop(0, chunks, begin, 0)
        span = wide - 2 - 2 * step
        deep = 2 if span % 2 == 0 else 1

        def some_rows(r, none):
            x0 = step + 1 + r * deep

            def one_chunk(c, back):
                back = list(back)
                for y, block, j in columns(c):
                    before = carry[0, y], carry[1, y]
                    for i in range(deep):
                        x = x0 + i
                        p, s = p_ref[x, y], s_ref[x, y]
                        xp, xs = x_face(p_ref, s_ref, x, block, j)
                        yp, ys = face(
                            spread(w12, 1, x, block, j), spread(w06, 1, x, block, j),
                            p, s, p_ref[x, y + 1], s_ref[x, y + 1],
                        )
                        zp, zs = face(
                            spread(w12, 2, x, block, j), spread(w06, 2, x, block, j),
                            p, s, roll(p, lanes - 1), roll(s, lanes - 1),
                        )
                        back_p, back_s = back[2 * i : 2 * i + 2]
                        p_new[x, y] = p + (xp - before[0]) + (yp - back_p) + (zp - roll(zp, 1)) + inflow[x, y]
                        s_new[x, y] = s + (xs - before[1]) + (ys - back_s) + (zs - roll(zs, 1))
                        before = xp, xs
                        back[2 * i : 2 * i + 2] = [yp, ys]
                    carry[0, y], carry[1, y] = before
                return tuple(back)

            lax.fori_loop(0, chunks, one_chunk, (zero,) * (2 * deep))
            return none

        lax.fori_loop(0, span // deep, some_rows, 0)

        def save(x, none):
            def save_chunk(c, none):
                for y, block, j in columns(c):
                    low, high = halves_swap(p_new[STEPS + x, y], s_new[STEPS + x, y], left_lanes, layers)
                    history[x * total_y + y, step * group : (step + 1) * group] = low
                    history[x * total_y + y, (STEPS + step) * group : (STEPS + step + 1) * group] = high
                    if step == STEPS - 1 and not fast:
                        fin[x, block, j] = jnp.concatenate([low, high], 0)
                return none

            return lax.fori_loop(0, chunks, save_chunk, none)

        several(rows, save, 4)

    if fast:
        last = slice((STEPS - 1) * group, STEPS * group)
        past = slice((2 * STEPS - 1) * group, 2 * STEPS * group)
        for ref, block in ((fin, sec), (send, 1 - sec)):
            for x in range(rows):
                for j in range(along):
                    at = x * total_y + block * along + j
                    ref[x, j, :group] = history[at, last]
                    ref[x, j, group:] = history[at, past]

    for copy in copies:
        copy.wait()
    count = basis.shape[2]
    snap_count = 2 * STEPS * group
    run = next(n for n in (16, 8, 4, 2, 1) if cells % n == 0)
    inner_su = jnp.zeros((snap_count, count), jnp.float32)
    inner_ss = jnp.zeros((snap_count, snap_count), jnp.float32)
    inner_uu[...] = jnp.zeros_like(inner_uu)
    for q in range(0, cells, run):
        rows_q = basis[q : q + run].reshape(run * lanes, count)
        inner_uu[...] += lax.dot_general(rows_q, rows_q, (((0,), (0,)), ((), ())), preferred_element_type=jnp.float32)
        part = [history[q + i].astype(jnp.bfloat16) for i in range(run)]
        for i in range(run):
            snaps[q + i] = part[i]
        both = jnp.concatenate(part, 1)
        inner_su += jnp.dot(both, basis[q : q + run].reshape(run * lanes, count), preferred_element_type=jnp.float32)
        inner_ss += lax.dot_general(both, both, (((1,), (1,)), ((), ())), preferred_element_type=jnp.float32)
    fold(sums, inner_uu, inner_su, inner_ss)
    half = sums.shape[0] // 2
    core = lax.rem(lax.axis_index("gx"), 2)
    keep[...] = sums[pl.ds(pl.multiple_of(core * half, 8), half), :]
    give[...] = sums[pl.ds(pl.multiple_of((1 - core) * half, 8), half), :]


def several(total, one, most):
    deep = next(n for n in range(most, 0, -1) if total % n == 0)

    def some(r, none):
        for i in range(deep):
            one(r * deep + i, 0)
        return none

    lax.fori_loop(0, total // deep, some, 0)


def folded_rows(count, snap_count):
    used = count + snap_count * (count // LANE) + snap_count // 2 + 1
    return -(-used // 16) * 16


def lower_mask(side):
    row = lax.broadcasted_iota(jnp.int32, (side, side), 0)
    column = lax.broadcasted_iota(jnp.int32, (side, side), 1)
    return row > column, row == column


def fold(sums, inner_uu, inner_su, inner_ss):
    below, on = lower_mask(LANE)
    first = inner_uu[:LANE, :LANE]
    sums[:LANE] = jnp.where(below, first, inner_uu[LANE:, LANE:])
    sums[LANE : 2 * LANE] = inner_uu[LANE:, :LANE]
    snap_count = inner_su.shape[0]
    at = 2 * LANE
    for tile in range(2):
        sums[at : at + snap_count] = inner_su[:, tile * LANE : (tile + 1) * LANE]
        at += snap_count
    half = snap_count // 2
    sums[at : at + half] = jnp.concatenate([inner_ss[:half], inner_ss[half:]], 1)
    at += half
    diagonal = jnp.sum(jnp.where(on, first, 0.0), axis=0, keepdims=True)
    left = sums.shape[0] - at
    sums[at:] = jnp.broadcast_to(diagonal, (left, LANE))


def unfold(sums, grams, snap_count, scale):
    count = 2 * LANE
    below, on = lower_mask(LANE)
    mixed = sums[:LANE] * scale
    cross = sums[LANE : 2 * LANE] * scale
    at = count + 2 * snap_count
    half = snap_count // 2
    diagonal = sums[at + half : at + half + 1] * scale
    low = jnp.where(below, mixed, 0.0)
    high = jnp.where(below, 0.0, mixed)
    grams[:LANE, :LANE] = low + low.T + jnp.where(on, jnp.broadcast_to(diagonal, on.shape), 0.0)
    grams[LANE:count, LANE:count] = high + jnp.where(on, 0.0, high).T
    grams[LANE:count, :LANE] = cross
    grams[:LANE, LANE:count] = cross.T
    for tile in range(2):
        part = sums[count + tile * snap_count : count + (tile + 1) * snap_count] * scale
        grams[count : count + snap_count, tile * LANE : (tile + 1) * LANE] = part
        wide = jnp.concatenate([part, jnp.zeros((LANE - snap_count, LANE), jnp.float32)], 0)
        grams[tile * LANE : (tile + 1) * LANE, count:] = wide.T
    folded = sums[at : at + half] * scale
    grams[count : count + half, count : count + snap_count] = folded[:, :snap_count]
    grams[count + half : count + snap_count, count : count + snap_count] = folded[:, snap_count:]


def flux(fields, table, inflow, basis_blocks, along):
    fast = len(fields) > 1
    wide, total_y, group, lanes = inflow.shape
    blocks = total_y // along
    rows = wide - 2 * STEPS
    count = basis_blocks.shape[-1]
    snaps = 2 * STEPS * group
    folded = folded_rows(count, snaps)
    f32 = jnp.float32
    fin = (rows, along, 2 * group, lanes) if fast else (rows, blocks, along, 2 * group, lanes)
    outs = [
        jax.ShapeDtypeStruct((rows * total_y, snaps, lanes), jnp.bfloat16),
        jax.ShapeDtypeStruct((folded // 2, LANE), f32),
        jax.ShapeDtypeStruct((folded // 2, LANE), f32),
        jax.ShapeDtypeStruct(fin, f32),
        jax.ShapeDtypeStruct(fin if fast else (8, lanes), f32),
    ]
    state = pltpu.VMEM((wide, total_y + 1, group, lanes), f32)
    whole = pl.BlockSpec(memory_space=pltpu.VMEM)
    return pl.pallas_call(
        lambda *refs: flux_kernel(fast, *refs),
        out_shape=outs,
        in_specs=[whole] * len(fields)
        + [whole, whole, pl.BlockSpec(memory_space=pl.ANY)],
        scratch_shapes=[
            state, state, state, state,
            pltpu.VMEM((wide, blocks, along, lanes), f32),
            pltpu.VMEM((3, wide + 1, total_y + 8, lanes), f32),
            pltpu.VMEM((3, wide, blocks, along, lanes), f32),
            pltpu.VMEM((3, wide, blocks, along, lanes), f32),
            pltpu.VMEM((2, total_y, group, lanes), f32),
            pltpu.VMEM((rows * total_y, snaps, lanes), f32),
            pltpu.VMEM((folded, LANE), f32),
            pltpu.VMEM((count, count), f32),
            pltpu.VMEM(basis_blocks.shape, jnp.bfloat16),
            pltpu.SemaphoreType.DMA((next(n for n in (4, 2, 1) if rows * total_y % n == 0),)),
        ],
        compiler_params=pltpu.CompilerParams(vmem_limit_bytes=VMEM_LIMIT),
    )(*fields, table, inflow, basis_blocks)


def unpack_kernel(parts, *refs):
    out_ref = refs[-1]
    along = refs[0].shape[1]
    members = refs[0].shape[2]
    stride = out_ref.shape[0] // members
    sec = lax.axis_index("sec")
    for part in range(parts):
        rows = refs[part].shape[0]
        start = 0 if parts == 1 else (sec if part == 0 else 1 - sec) * rows
        for x in range(rows):
            for y in range(along):
                out_ref[pl.ds((start + x) * along + y, members, stride=stride), :] = refs[part][x, y]


def unpack(parts):
    rows, along, members, lanes = parts[0].shape
    across = rows * len(parts)
    out = pl.pallas_call(
        lambda *refs: unpack_kernel(len(parts), *refs),
        out_shape=jax.ShapeDtypeStruct((members * across * along, lanes), jnp.float32),
        compiler_params=pltpu.CompilerParams(vmem_limit_bytes=VMEM_LIMIT),
    )(*parts)
    return out.reshape(members, across, along, lanes)


def all_sum(keep, give, beside=None):
    swapped = None
    counts = [lax.axis_size(axis) for axis in AXES]
    total = counts[0] * counts[1]
    pair = counts[1]
    swap = [(i, i ^ pair) for i in range(total)]
    value = keep + lax.ppermute(give, AXES, swap)
    masks = [1 << b for b in range(total.bit_length() - 1) if 1 << b != pair]
    turned = list(masks)
    for i in range(0, len(masks) - 1, 2):
        turned[i], turned[i + 1] = masks[i + 1], masks[i]
    for hop, (even, odd) in enumerate(zip(masks, turned)):
        value = value + lax.ppermute(value, AXES, [(i, i ^ (odd if i & pair else even)) for i in range(total)])
        if hop == 1 and beside is not None:
            beside, value = lax.optimization_barrier((beside, value))
            swapped = lax.ppermute(beside, "sec", [(0, 1), (1, 0)])
    return value, lax.ppermute(value, AXES, swap), swapped


def to_bf16(value):
    return value.astype(jnp.bfloat16)


def hdot(a, b, left=1, right=0):
    return lax.dot_general(a, b, (((left,), (right,)), ((), ())), precision=HIGHEST, preferred_element_type=jnp.float32)

SUB = 8
PANEL = 32
LANE = 128

def row_of(value, j):
    return jnp.broadcast_to(value[j:j + 1], (SUB, LANE))

def eliminate(panel, column):
    groups = PANEL // SUB
    tiles = panel.shape[1] // LANE
    row = lax.broadcasted_iota(jnp.int32, (SUB, LANE), 0)
    strip = [[panel[h * SUB:(h + 1) * SUB, t * LANE:(t + 1) * LANE] for t in range(tiles)] for h in range(groups)]
    spread = {}

    def expand(g, first_group):
        for h in range(first_group, groups):
            for j in range(g * SUB, (g + 1) * SUB):
                tile, lane = (column + j) // LANE, (column + j) % LANE
                spread[h, j] = jnp.broadcast_to(strip[h][tile][:, lane:lane + 1], (SUB, LANE))

    expand(0, 0)
    for g in range(groups):
        if g + 1 < groups:
            expand(g + 1, g)
        scale = jnp.zeros((SUB, LANE), jnp.float32)
        for j in range(0, SUB, 2):
            left, right = spread[g, g * SUB + j], spread[g, g * SUB + j + 1]
            a, b, c = row_of(left, j), row_of(right, j), row_of(right, j + 1)
            det = a * c - b * b
            inv_a, inv_det = 1.0 / a, 1.0 / det
            slope = b * inv_a
            second = a * inv_det
            scale = jnp.where(row == j, a, jnp.where(row == j + 1, det * inv_a, scale))
            one, two = {}, {}
            for h in range(g, groups):
                one[h] = spread[h, g * SUB + j] * inv_a
                two[h] = (spread[h, g * SUB + j + 1] - one[h] * b) * second
            one[g] = jnp.where(row > j, one[g], 0.0)
            two[g] = jnp.where(row > j + 1, two[g], 0.0)
            for k in range(g * SUB + j + 2, min(g + 2, groups) * SUB):
                first = row_of(spread[g, k], j)
                next_ = row_of(spread[g, k], j + 1) - slope * first
                for h in range(g, groups):
                    spread[h, k] = spread[h, k] - one[h] * first - two[h] * next_
            for t in range(tiles):
                first = row_of(strip[g][t], j)
                next_ = row_of(strip[g][t], j + 1) - slope * first
                for h in range(g, groups):
                    strip[h][t] = strip[h][t] - one[h] * first - two[h] * next_
        root = lax.rsqrt(scale)
        for t in range(tiles):
            strip[g][t] = strip[g][t] * root
    return jnp.concatenate([jnp.concatenate(s, 1) for s in strip], 0)

def terms(value):
    high = value.astype(jnp.bfloat16)
    rest = value - high.astype(jnp.float32)
    middle = rest.astype(jnp.bfloat16)
    return high, middle, (rest - middle.astype(jnp.float32)).astype(jnp.bfloat16)

def left_stack(t):
    return jnp.concatenate([t[0], t[0], t[1], t[1], t[0], t[2]], 0)

def right_stack(t):
    return jnp.concatenate([t[0], t[1], t[0], t[1], t[2], t[0]], 0)

def stacked_dot(left, right):
    return lax.dot_general(left, right, (((0,), (0,)), ((), ())), preferred_element_type=jnp.float32)

def tdot(a, b):
    return stacked_dot(left_stack(terms(a)), right_stack(terms(b)))

def solve(aug, count):
    for start in range(0, count, PANEL):
        first = start // LANE * LANE
        done = eliminate(aug[start:start + PANEL, first:], start - first)
        aug[start:start + PANEL, first:] = done
        rest = start + PANEL
        if rest < count:
            base = rest // LANE * LANE
            parts = terms(done[:, base - first:])
            left, right = left_stack(parts), right_stack(parts)
            change = stacked_dot(left[:, :count - base], right)
            aug[rest:, base:] = aug[rest:, base:] - change[rest - base:]

def next_squares(turned, extra, coeffs, gram, sig2):
    energy = turned * turned * sig2
    ones = jnp.ones((8, turned.shape[0]), jnp.float32)
    low = hdot(turned, coeffs, 1, 1) + hdot(extra, gram)
    return hdot(ones, energy, 1, 1)[:1] + hdot(ones[:, : low.shape[1]], low * low, 1, 1)[:1]


def small_kernel(
    scale, mine_ref, other_ref, sigma_ref, snaps_hbm, basis_hbm, fresh_hbm, sigma_out,
    aug, sums, gram_ref, weights, snaps_ref, basis, fresh, in_sems, out_sems,
):
    copies = [
        pltpu.make_async_copy(basis_hbm, basis, in_sems.at[0]),
        pltpu.make_async_copy(snaps_hbm, snaps_ref, in_sems.at[1]),
    ]
    for copy in copies:
        copy.start()
    count = sigma_ref.shape[1]
    snaps = (gram_ref.shape[0] - count) // 2
    half = sums.shape[0] // 2
    core = lax.rem(lax.axis_index("gx"), 2)
    sums[pl.ds(pl.multiple_of(core * half, 8), half), :] = mine_ref[...]
    sums[pl.ds(pl.multiple_of((1 - core) * half, 8), half), :] = other_ref[...]
    unfold(sums, gram_ref, 2 * snaps, scale)
    eye = lax.broadcasted_iota(jnp.int32, (count, count), 0) == lax.broadcasted_iota(jnp.int32, (count, count), 1)
    pad = LANE - snaps
    sig2 = sigma_ref[...] * sigma_ref[...]
    prior = None
    for group in range(2):
        rows = gram_ref[count + group * snaps: count + (group + 1) * snaps]
        if group == 0:
            coeffs = rows[:, :count]
            own = rows[:, count:count + snaps]
        else:
            reach = count + snaps
            coeffs = hdot(rows[:, :reach], prior[:, :reach], 1, 1)
            own = rows[:, reach:reach + snaps]
        rounded = coeffs.astype(jnp.bfloat16).astype(jnp.float32)
        if group == 0:
            mapped = rounded
            known = gram_ref[:count, :count]
        else:
            mapped = hdot(rounded, prior[:, :reach])
            known = gram_ref[:reach, :reach]
        spread = hdot(mapped, known)
        gram = own - hdot(rounded, coeffs, 1, 1) - hdot(coeffs, rounded, 1, 1) + hdot(spread, mapped, 1, 1)
        lead = tdot(coeffs, coeffs) + jnp.where(eye, jnp.broadcast_to(sig2, eye.shape), 0.0)
        inner = hdot(lead, lead) + tdot(coeffs, hdot(gram, coeffs))
        aug[:, :count] = inner
        aug[:, count:2 * count] = lead
        aug[:, 2 * count:] = jnp.concatenate([coeffs, jnp.zeros((pad, count), jnp.float32)], 0).T
        solve(aug, count)
        turned = aug[:, count:2 * count]
        extra = aug[:, 2 * count:2 * count + snaps]
        step = turned.astype(jnp.bfloat16).astype(jnp.float32) - hdot(extra, rounded)
        if group == 0:
            sig2 = next_squares(turned, extra, coeffs, gram, sig2)
            prior = jnp.concatenate([step, aug[:, 2 * count:]], 1)
        else:
            final = hdot(step, prior)
            high = final[:, :count].astype(jnp.bfloat16)
            weights[:count] = high.T
            both = jnp.concatenate([final[:, count:].T[:snaps], aug[:, 2 * count:].T[:snaps]], 0)
            high = both.astype(jnp.bfloat16)
            weights[count:count + 2 * snaps] = high
            weights[count + 2 * snaps:] = (both - high.astype(jnp.float32)).astype(jnp.bfloat16)
    for copy in copies:
        copy.wait()
    wait_all = renew(weights, snaps_ref, basis, fresh, fresh_hbm, out_sems)
    sigma_out[...] = jnp.sqrt(next_squares(turned, extra, coeffs, gram, sig2))
    wait_all()


def renew(weights, snaps_ref, basis, fresh, fresh_hbm, out_sems):
    parts = out_sems.shape[0]
    cells, _, lanes = snaps_ref.shape
    run = cells // parts

    def out(i):
        rows = pl.ds(i * run * lanes, run * lanes)
        return pltpu.make_async_copy(fresh.at[rows], fresh_hbm.at[rows], out_sems.at[i])

    def part(i):
        at = i * run * lanes
        flat = basis[pl.ds(at, run * lanes), :]
        turned = []
        for q in range(run):
            one = snaps_ref[i * run + q]
            turned.append(jnp.concatenate([one, one], 0).T)
        value = jnp.dot(
            jnp.concatenate([flat, jnp.concatenate(turned, 0)], 1), weights[...],
            preferred_element_type=jnp.float32,
        )
        fresh[pl.ds(at, run * lanes), :] = value.astype(jnp.bfloat16)
        out(i).start()

    for i in range(parts):
        part(i)

    def wait_all():
        for i in range(parts):
            out(i).wait()

    return wait_all


def small(mine, other, sigma, snaps, flat, rows_total):
    count = sigma.shape[0]
    cells, snap_count, lanes = snaps.shape
    rows = count + snap_count
    parts = next(n for n in (8, 4, 2, 1) if cells % n == 0)
    whole = pl.BlockSpec(memory_space=pltpu.VMEM)
    outside = pl.BlockSpec(memory_space=pl.ANY)
    fresh, sigma_out = pl.pallas_call(
        functools.partial(small_kernel, 1.0 / rows_total),
        out_shape=(
            jax.ShapeDtypeStruct(flat.shape, jnp.bfloat16),
            jax.ShapeDtypeStruct((1, count), jnp.float32),
        ),
        in_specs=[whole, whole, whole, outside, outside],
        out_specs=(outside, whole),
        scratch_shapes=[
            pltpu.VMEM((count, 2 * count + LANE), jnp.float32),
            pltpu.VMEM((2 * mine.shape[0], LANE), jnp.float32),
            pltpu.VMEM((rows, count + LANE), jnp.float32),
            pltpu.VMEM((count + 2 * snap_count, count), jnp.bfloat16),
            pltpu.VMEM(snaps.shape, jnp.bfloat16),
            pltpu.VMEM(flat.shape, jnp.bfloat16),
            pltpu.VMEM(flat.shape, jnp.bfloat16),
            pltpu.SemaphoreType.DMA((2,)),
            pltpu.SemaphoreType.DMA((parts,)),
        ],
        compiler_params=pltpu.CompilerParams(vmem_limit_bytes=VMEM_LIMIT),
        cost_estimate=pl.CostEstimate(flops=2 * 10**10, bytes_accessed=2**20, transcendentals=0),
    )(mine, other, sigma.reshape(1, count), snaps, flat)
    return fresh, sigma_out.reshape(count)


def body(state_init, rock_type, perm_table, well_cells, well_rate, basis_in, singular):
    members, across, along, lanes = state_init.shape
    gx_count = lax.axis_size("gx")
    sec_count = lax.axis_size("sec")
    rows = across // sec_count
    wide = rows + 2 * STEPS
    total_y = along * sec_count
    count = basis_in.shape[-1]
    fast = sec_count == 2 and across == 2 * STEPS
    if fast:
        own, packed = pack(state_init, rock_type)
        outward, inward = split(packed)
        straight, crossed = [], []
        for r in range(gx_count):
            if r > 0:
                straight.append((2 * (r - 1), 2 * r))
                crossed.append((2 * (r - 1) + 1, 2 * r))
            if r < gx_count - 1:
                straight.append((2 * (r + 1) + 1, 2 * r + 1))
                crossed.append((2 * (r + 1), 2 * r + 1))
        other = lax.ppermute(packed, "sec", [(0, 1), (1, 0)])
        cross = lax.ppermute(inward, AXES, crossed)
        beside = lax.ppermute(outward, AXES, straight)
        fields = (own, packed, other, beside, cross)
    else:
        _, packed = pack(state_init, rock_type)
        slab = lax.all_gather(packed, "sec", axis=1)
        low = lax.ppermute(slab[across - STEPS :], "gx", [(i, i + 1) for i in range(gx_count - 1)])
        high = lax.ppermute(slab[:STEPS], "gx", [(i + 1, i) for i in range(gx_count - 1)])
        padded = jnp.concatenate([low, slab, high], 0)
        fields = (lax.dynamic_slice_in_dim(padded, lax.axis_index("sec") * rows, wide, axis=0),)
    flat = basis_in.reshape(-1, count)
    rows_total = flat.shape[0] * gx_count * sec_count
    inflow, table = before_flux(well_cells, well_rate, perm_table, wide, total_y, lanes)
    snaps, keep, give, fin, send = flux(
        fields, table, inflow, flat.reshape(-1, lanes, count), along
    )
    mine, others, received = all_sum(keep, give, send if fast else None)
    if fast:
        state_out = unpack((fin, received))
        state_out, mine = lax.optimization_barrier((state_out, mine))
    else:
        moved = lax.all_to_all(fin, "sec", split_axis=1, concat_axis=0, tiled=True)
        state_out = unpack((moved.reshape(across, along, members, lanes),))
    fresh, sigma = small(mine, others, singular, snaps, flat, rows_total)
    return state_out, fresh.reshape(basis_in.shape), sigma


def solution(mesh):
    return jax.shard_map(
        body,
        mesh=mesh,
        in_specs=(
            P(None, "gx", "sec", None),
            P("gx", "sec"),
            P(),
            P(),
            P(),
            P(("gx", "sec"), None, None, None),
            P(),
        ),
        out_specs=(P(None, "gx", "sec", None), P(("gx", "sec"), None, None, None), P()),
        check_vma=False,
    )
```
